32 devices in a mesh: expert: 8 (over z, y), dp: 4 (over x, core).
Axes of the slice: x: 2, y: 2, z: 4, core: 2. Of those that a mesh axis runs over, the one named last changes fastest.
Arguments:
- block_input: bfloat16 [4, 12288, 1024], P('dp', 'expert'), may hold values from -6 to 6
- expert_ids: int32 [4, 8192], P('dp', 'expert'), may hold values from 0 to 7, as said below
- ln1_gain: float32 [1024], replicated, may hold values from 0.1 to 1.9
- ln1_bias: float32 [1024], replicated, may hold values from -3 to 3
- w_qkv: bfloat16 [1024, 3072], replicated, may hold values from -0.1875 to 0.1875
- w_o: bfloat16 [1024, 1024], replicated, may hold values from -2 to 2
- ln2_gain: float32 [1024], replicated, may hold values from 0.1 to 1.9
- ln2_bias: float32 [1024], replicated, may hold values from -3 to 3
- w_in: bfloat16 [8, 4096, 1024], P('expert', 'dp'), may hold values from -0.1875 to 0.1875
- b_in: bfloat16 [8, 4096], P('expert', 'dp'), may hold values from -4 to 4
- w_out: bfloat16 [8, 4096, 1024], P('expert', 'dp'), may hold values from -0.09375 to 0.09375
- b_out: bfloat16 [8, 1024], P('expert', 'dp'), may hold values from -3 to 3
- cotangent: bfloat16 [4, 12288, 1024], P('dp', 'expert'), may hold values from -6 to 6
Outputs:
- out: bfloat16 [4, 12288, 1024], P('dp', 'expert')
- grad_input: bfloat16 [4, 12288, 1024], P('dp', 'expert')
- grad_ln1_gain: float32 [1024], replicated
- grad_ln1_bias: float32 [1024], replicated
- grad_w_qkv: float32 [1024, 3072], replicated
- grad_w_o: float32 [1024, 1024], replicated
- grad_ln2_gain: float32 [1024], replicated
- grad_ln2_bias: float32 [1024], replicated
- grad_w_in: float32 [8, 4096, 1024], P('expert', 'dp')
- grad_b_in: float32 [8, 4096], P('expert', 'dp')
- grad_w_out: float32 [8, 4096, 1024], P('expert', 'dp')
- grad_b_out: float32 [8, 1024], P('expert', 'dp')
The draws below stay inside these ranges and needn't reach their ends.
Inputs may be any that keep to these rules, and one draw needn't show every extreme that they name: `expert_ids`: in each group every expert takes exactly 640 tokens of one sequence of the group and at least 1 but fewer than 640 tokens of each other sequence; one expert, drawn from the seed, takes exactly 1536 tokens of the group in all, every other expert fewer.
All inputs are finite; a program needn't handle non-finite values.
Results may differ from the reference program's by a relative error of at most 0.012.
Values may be sent and summed in bfloat16 or wider, within the bound.
A program may use at most 384 MiB of HBM per device.

```python
import jax
import jax.numpy as jnp
from jax import lax

D = 1024
HEADS = 16
HEAD_DIM = 64
FF = 4096
LEN = 1024
EXPERTS = 8
GROUPS = 4
CAP = 640
EROWS = 1536


def draw_expert_ids(key, part):
    key = jax.random.fold_in(key, 11)
    hot_base = (EROWS - CAP) // (EXPERTS - 1)
    hot_extra = EROWS - CAP - hot_base * (EXPERTS - 1)
    expert_range = jnp.arange(EXPERTS, dtype=jnp.int32)

    def one_group(group_key):
        hot_key, peak_key, seq_key = jax.random.split(group_key, 3)
        hottest = jax.random.randint(hot_key, (), 0, EXPERTS).astype(jnp.int32)
        peaks = jax.random.permutation(peak_key, EXPERTS).astype(jnp.int32)
        hot_seq = jnp.sum(jnp.where(peaks == hottest, expert_range, 0)).astype(jnp.int32)
        other_rank = expert_range - (expert_range > hot_seq).astype(jnp.int32)
        hot_counts = jnp.where(expert_range == hot_seq, CAP, hot_base + (other_rank < hot_extra).astype(jnp.int32)).astype(jnp.int32)

        def one_sequence(seq_seed, peak_one, hot_count, is_hot_seq):
            order_key, delta_key, shuffle_key = jax.random.split(seq_seed, 3)
            filler = ((expert_range != peak_one) & (expert_range != hottest)).astype(jnp.int32)
            filler_count = jnp.sum(filler)
            remaining = LEN - CAP - jnp.where(is_hot_seq, 0, hot_count)
            fill_base = remaining // filler_count
            fill_extra = remaining - fill_base * filler_count
            ordering = jax.random.permutation(order_key, EXPERTS).astype(jnp.int32)
            ranks_in_order = jnp.cumsum(filler[ordering]) - 1
            filler_rank = jnp.zeros((EXPERTS,), jnp.int32).at[ordering].set(ranks_in_order.astype(jnp.int32))
            deltas = jax.random.randint(delta_key, (EXPERTS,), 0, 1 << 20).astype(jnp.int32) % (fill_base // 2 + 1)
            pair_delta = deltas[filler_rank // 2]
            paired = filler_rank // 2 * 2 + 1 < filler_count
            signed = jnp.where(filler_rank % 2 == 0, pair_delta, -pair_delta)
            fill = fill_base + (filler_rank < fill_extra).astype(jnp.int32) + jnp.where(paired, signed, 0)
            counts = jnp.where(expert_range == peak_one, CAP, jnp.where(expert_range == hottest, hot_count, fill)).astype(jnp.int32)
            flattened = jnp.repeat(expert_range, counts, total_repeat_length=LEN)
            return jax.random.permutation(shuffle_key, flattened)
        seq_seeds = jax.random.split(seq_key, EXPERTS)
        drawn = jax.vmap(one_sequence)(seq_seeds, peaks, hot_counts, expert_range == hot_seq)
        return drawn.reshape(EXPERTS * LEN)
    group_keys = jax.random.split(key, GROUPS)
    return jax.vmap(one_group)(group_keys).astype(jnp.int32)


def block_scale(rng, shape, cuts, smallest, top_value):
    level = 1.0
    for axis_at, blocks in cuts:
        heights = jax.random.uniform(jax.random.fold_in(jax.random.fold_in(rng, 6), axis_at), (blocks,), jnp.float32, smallest / len(cuts), top_value / len(cuts))
        level = level * jnp.repeat(jnp.exp(heights), shape[axis_at] // blocks).reshape((-1,) + (1,) * (len(shape) - 1 - axis_at))
    return level


def gaussian(rng, dims, scale, most, shards=(), kind=jnp.bfloat16):
    values = scale * jax.random.normal(rng, dims, jnp.float32)
    if shards:
        values = values * block_scale(rng, dims, shards, -0.22, 0.18)
    return jnp.clip(values, -most, most).astype(kind)


def setup_inputs(seed: int = 0) -> dict:
    streams_of = jax.random.split(jax.random.key(seed), 14)
    block_input = gaussian(streams_of[0], (GROUPS, EXPERTS * EROWS, D), 1.0, 6.0, ((0, 4), (1, 8)))
    expert_ids = draw_expert_ids(jax.random.fold_in(streams_of[13], 71), 0)
    ln1_gain = jnp.clip(1.0 + 0.18 * jax.random.normal(streams_of[2], (D,), jnp.float32), 0.1, 1.9)
    ln1_bias = gaussian(streams_of[3], (D,), 0.2, 3.0, (), jnp.float32)
    w_qkv = gaussian(streams_of[4], (D, 3 * D), D ** -0.5, 0.1875)
    w_o = gaussian(streams_of[5], (D, D), (D * 8 // LEN) ** -0.5, 2.0)
    ln2_gain = jnp.clip(1.0 + 0.18 * jax.random.normal(streams_of[6], (D,), jnp.float32), 0.1, 1.9)
    ln2_bias = gaussian(streams_of[7], (D,), 0.2, 3.0, (), jnp.float32)
    w_in = gaussian(streams_of[8], (EXPERTS, FF, D), D ** -0.5, 0.1875, ((0, 8), (1, 4)))
    b_in = gaussian(streams_of[9], (EXPERTS, FF), 0.3, 4.0, ((0, 8), (1, 4)))
    w_out = gaussian(streams_of[10], (EXPERTS, FF, D), FF ** -0.5, 0.09375, ((0, 8), (1, 4)))
    b_out = gaussian(streams_of[11], (EXPERTS, D), 0.2, 3.0, ((0, 8), (1, 4)))
    cotangent = gaussian(streams_of[12], (GROUPS, EXPERTS * EROWS, D), 1.0, 6.0, ((0, 4), (1, 8)))
    return dict(block_input=block_input, expert_ids=expert_ids, ln1_gain=ln1_gain, ln1_bias=ln1_bias, w_qkv=w_qkv, w_o=w_o, ln2_gain=ln2_gain, ln2_bias=ln2_bias, w_in=w_in, b_in=b_in, w_out=w_out, b_out=b_out, cotangent=cotangent)


@jax.custom_vjp
def low(v):
    return lax.optimization_barrier(v.astype(jnp.bfloat16)).astype(jnp.float32)

@jax.custom_vjp
def low_back(v):
    return v

def low_keep(v):
    return (low(v), None)

def low_pass(kept, grad):
    return (grad,)

def back_keep(v):
    return (v, None)

def back_low(kept, grad):
    return (low(grad),)
low.defvjp(low_keep, low_pass)
low_back.defvjp(back_keep, back_low)
highest = lax.Precision.HIGHEST
epsilon = 1e-05
gelu_c = 0.7978845608028654

def normalize(values_in, gains, offsets):
    centre = lax.optimization_barrier(jnp.mean(values_in, axis=-1, keepdims=True))
    centred = values_in - centre
    spread = lax.optimization_barrier(jnp.mean(centred * centred, axis=-1, keepdims=True))
    return centred * lax.rsqrt(spread + epsilon) * gains + offsets

def smooth_gelu(pre_act):
    inner_arg = gelu_c * (pre_act + 0.044715 * pre_act * pre_act * pre_act)
    return 0.5 * pre_act * (1.0 + jnp.tanh(inner_arg))

def attend_block(block_queries, block_start, keys_all, values_all):
    scores = low_back(jnp.einsum('qhd,khd->hqk', block_queries, keys_all, precision=highest) * 0.125)
    row_pos = block_start + jnp.arange(block_queries.shape[0], dtype=jnp.int32)
    col_pos = jnp.arange(keys_all.shape[0], dtype=jnp.int32)
    allowed = col_pos[None, :] <= row_pos[:, None]
    scores = jnp.where(allowed[None], scores, -1e+30)
    probs_low = low(jax.nn.softmax(scores, axis=-1))
    return jnp.einsum('hqk,khd->qhd', probs_low, values_all, precision=highest)

def attend_sequence(queries, keys_all, values_all):
    step_rows = min(512, LEN)
    block_count = LEN // step_rows
    block_queries = queries.reshape(block_count, step_rows, HEADS, HEAD_DIM)
    block_starts = jnp.arange(block_count, dtype=jnp.int32) * step_rows

    def block_fn(pieces):
        return attend_block(pieces[0], pieces[1], keys_all, values_all)
    attended = lax.map(jax.checkpoint(block_fn), (block_queries, block_starts))
    return attended.reshape(LEN, HEADS, HEAD_DIM)

def group_forward(group_rows, group_ids, params):
    ln1_gain, ln1_bias, w_qkv, w_o, ln2_gain, ln2_bias, w_in, b_in, w_out, b_out = params
    choose = (group_ids[:, None] == jnp.arange(EXPERTS, dtype=jnp.int32)[None, :]).astype(jnp.int32)
    rank_in = lax.optimization_barrier(jnp.sum((jnp.cumsum(choose, axis=0) - 1) * choose, axis=1))
    slot_of = (group_ids * EROWS + rank_in).astype(jnp.int32)
    present = jnp.zeros((EXPERTS * EROWS,), jnp.float32).at[slot_of].set(1.0)
    tokens = group_rows[slot_of]
    normed = low(normalize(tokens, ln1_gain, ln1_bias))
    mixed_qkv = low(low_back(jnp.dot(normed, w_qkv, precision=highest)))
    queries = mixed_qkv[:, :D].reshape(EXPERTS, LEN, HEADS, HEAD_DIM)
    keys_all = mixed_qkv[:, D:2 * D].reshape(EXPERTS, LEN, HEADS, HEAD_DIM)
    values_all = mixed_qkv[:, 2 * D:].reshape(EXPERTS, LEN, HEADS, HEAD_DIM)
    attended = lax.map(lambda pieces: attend_sequence(pieces[0], pieces[1], pieces[2]), (queries, keys_all, values_all))
    context = low(low_back(attended.reshape(EXPERTS * LEN, D)))
    hidden = tokens + jnp.dot(context, w_o, precision=highest)
    sent_rows = low(low_back(hidden))
    placed = jnp.zeros((EXPERTS * EROWS, D), jnp.float32).at[slot_of].set(sent_rows)
    normed_two = low(normalize(placed, ln2_gain, ln2_bias)).reshape(EXPERTS, EROWS, D)

    def expert_rows(pieces):
        block_rows, weight_in, bias_in, weight_out, bias_out = pieces
        pre_act = low_back(jnp.einsum('rd,fd->rf', block_rows, weight_in, precision=highest) + bias_in)
        act_low = low(smooth_gelu(pre_act))
        return jnp.dot(act_low, weight_out, precision=highest) + bias_out
    expert_out = lax.map(jax.checkpoint(expert_rows), (normed_two, w_in, b_in, w_out, b_out))
    return (placed + expert_out.reshape(EXPERTS * EROWS, D)) * present[:, None]

def reference(block_input, expert_ids, ln1_gain, ln1_bias, w_qkv, w_o, ln2_gain, ln2_bias, w_in, b_in, w_out, b_out, cotangent):
    params = tuple((piece.astype(jnp.float32) for piece in (ln1_gain, ln1_bias, w_qkv, w_o, ln2_gain, ln2_bias, w_in, b_in, w_out, b_out)))

    def one_group(totals, pieces):
        group_rows, group_ids, grad_out = pieces
        result, pullback = jax.vjp(lambda inputs_f, params_f: group_forward(inputs_f, group_ids, params_f), group_rows.astype(jnp.float32), params)
        grad_rows, grad_params = pullback(grad_out.astype(jnp.float32))
        totals = jax.tree.map(jnp.add, totals, grad_params)
        return (totals, (result.astype(jnp.bfloat16), grad_rows.astype(jnp.bfloat16)))
    zero_grads = jax.tree.map(jnp.zeros_like, params)
    totals, outputs = lax.scan(one_group, zero_grads, (block_input, expert_ids, cotangent))
    return (outputs[0], outputs[1], totals[0], totals[1], totals[2], totals[3], totals[4], totals[5], totals[6], totals[7], totals[8], totals[9])
```

```python
import jax
import jax.numpy as jnp
from jax import lax
from jax.sharding import PartitionSpec as P

HEADS = 16
HEAD_DIM = 64


epsilon = 1e-05
gelu_c = 0.7978845608028654
contract_last = (((1,), (1,)), ((), ()))
contract_first = (((0,), (0,)), ((), ()))


def normalize(values_in, gains, offsets):
    centre = jnp.mean(values_in, axis=-1, keepdims=True)
    centred = values_in - centre
    spread = jnp.mean(centred * centred, axis=-1, keepdims=True)
    inverse = lax.rsqrt(spread + epsilon)
    scaled = centred * inverse
    return (scaled * gains + offsets, scaled, inverse)


def normalize_back(grad_output, scaled, inverse, gains):
    grad_scaled = grad_output * gains
    first_mean = jnp.mean(grad_scaled, axis=-1, keepdims=True)
    second_mean = jnp.mean(grad_scaled * scaled, axis=-1, keepdims=True)
    grad_values = inverse * (grad_scaled - first_mean - scaled * second_mean)
    return (grad_values, jnp.sum(grad_output * scaled, axis=0), jnp.sum(grad_output, axis=0))


def smooth_gelu(pre_act):
    inner_arg = gelu_c * (pre_act + 0.044715 * pre_act * pre_act * pre_act)
    return 0.5 * pre_act * (1.0 + jnp.tanh(inner_arg))


def gelu_slope(pre_act):
    tangent = jnp.tanh(gelu_c * (pre_act + 0.044715 * pre_act * pre_act * pre_act))
    return 0.5 * (1.0 + tangent) + 0.5 * pre_act * (1.0 - tangent * tangent) * gelu_c * (
        1.0 + 3.0 * 0.044715 * pre_act * pre_act
    )


def causal_mask(first_row, height, breadth):
    row_pos = first_row + lax.broadcasted_iota(jnp.int32, (height, breadth), 0)
    col_pos = lax.broadcasted_iota(jnp.int32, (height, breadth), 1)
    return col_pos <= row_pos


def block_scores(block_queries, keys_part, first_row):
    scores = (
        jnp.einsum("qhd,khd->hqk", block_queries, keys_part, preferred_element_type=jnp.float32)
        * 0.125
    )
    allowed = causal_mask(first_row, block_queries.shape[0], keys_part.shape[0])
    return jnp.where(allowed[None], scores, -1e30)


def attend_forward(queries, keys_all, values_all):
    length = queries.shape[0]
    step_rows = min(512, length)
    outputs = []
    log_totals = []
    for first_row in range(0, length, step_rows):
        last_row = first_row + step_rows
        scores = block_scores(queries[first_row:last_row], keys_all[:last_row], first_row)
        row_peak = jnp.max(scores, axis=-1, keepdims=True)
        exponent = jnp.exp(scores - row_peak)
        row_total = jnp.sum(exponent, axis=-1, keepdims=True)
        weights_low = (exponent / row_total).astype(jnp.bfloat16)
        outputs.append(
            jnp.einsum(
                "hqk,khd->qhd",
                weights_low,
                values_all[:last_row],
                preferred_element_type=jnp.float32,
            )
        )
        log_totals.append(row_peak + jnp.log(row_total))
    return (jnp.concatenate(outputs, axis=0), log_totals)


def attend_backward(queries, keys_all, values_all, grad_context, log_totals):
    length = queries.shape[0]
    step_rows = min(512, length)
    grad_queries = []
    grad_keys = jnp.zeros(keys_all.shape, jnp.float32)
    grad_values = jnp.zeros(values_all.shape, jnp.float32)
    for index_block, first_row in enumerate(range(0, length, step_rows)):
        last_row = first_row + step_rows
        block_queries = queries[first_row:last_row]
        block_grad = grad_context[first_row:last_row]
        scores = block_scores(block_queries, keys_all[:last_row], first_row)
        weights_f = jnp.exp(scores - log_totals[index_block])
        weights_low = weights_f.astype(jnp.bfloat16)
        grad_weights = jnp.einsum(
            "qhd,khd->hqk", block_grad, values_all[:last_row], preferred_element_type=jnp.float32
        )
        row_centre = jnp.sum(weights_f * grad_weights, axis=-1, keepdims=True)
        grad_scores = (weights_f * (grad_weights - row_centre)).astype(jnp.bfloat16)
        grad_queries.append(
            jnp.einsum(
                "hqk,khd->qhd", grad_scores, keys_all[:last_row], preferred_element_type=jnp.float32
            )
            * 0.125
        )
        grad_keys = grad_keys.at[:last_row].add(
            jnp.einsum(
                "hqk,qhd->khd", grad_scores, block_queries, preferred_element_type=jnp.float32
            )
            * 0.125
        )
        grad_values = grad_values.at[:last_row].add(
            jnp.einsum("hqk,qhd->khd", weights_low, block_grad, preferred_element_type=jnp.float32)
        )
    return (jnp.concatenate(grad_queries, axis=0), grad_keys, grad_values)


bf16 = jnp.bfloat16


def select_rows(columns, count, table):
    chosen = (columns[:, None] == jnp.arange(count, dtype=jnp.int32)[None, :]).astype(bf16)
    return jnp.dot(chosen, table, preferred_element_type=jnp.float32)


def place_rows(columns, count, table):
    chosen = (columns[None, :] == jnp.arange(count, dtype=jnp.int32)[:, None]).astype(bf16)
    return jnp.dot(chosen, table, preferred_element_type=jnp.float32).astype(bf16)


def exchange(packed, expert_count):
    return lax.all_to_all(
        packed.reshape(expert_count, -1, packed.shape[-1]),
        "expert",
        split_axis=0,
        concat_axis=0,
        tiled=True,
    ).reshape(-1, packed.shape[-1])


def move_rows(table, from_columns, to_columns, local_rows, chunk, expert_count, rounds):
    from_local, from_device, from_rank = from_columns
    to_local, to_device, to_rank = to_columns
    span = expert_count * chunk

    def remote_column(device, rank, step):
        return jnp.where(rank // chunk == step, device * chunk + rank % chunk, -1)

    def one_round(step):
        packed = place_rows(remote_column(from_device, from_rank, step), span, table)
        arrived = exchange(packed, expert_count)
        return select_rows(remote_column(to_device, to_rank, step), span, arrived)

    local = place_rows(from_local, local_rows, table)
    total = one_round(0) + select_rows(to_local, local_rows, local)

    def again(state):
        step, sums = state
        return (step + 1, sums + one_round(step))

    return lax.while_loop(lambda state: state[0] < rounds, again, (jnp.int32(1), total))[1]


def swap(values, axis, bit):
    size = lax.axis_size(axis)
    return lax.ppermute(values, axis, [(i, i ^ bit) for i in range(size)])


def bits_of(axis):
    size = lax.axis_size(axis)
    return [(axis, 1 << k) for k in range(size.bit_length() - 1)]


def sum_everywhere(values, steps):
    part = values
    for axis, bit in steps:
        upper = (lax.axis_index(axis) // bit) % 2
        halves = part.reshape(2, -1, part.shape[-1])
        kept = lax.dynamic_index_in_dim(halves, upper, 0, keepdims=False)
        given = lax.dynamic_index_in_dim(halves, 1 - upper, 0, keepdims=False)
        got = swap(given.astype(bf16), axis, bit)
        part = kept.astype(jnp.float32) + got.astype(jnp.float32)
    part = part.astype(bf16)
    for axis, bit in reversed(steps):
        upper = (lax.axis_index(axis) // bit) % 2
        got = swap(part, axis, bit)
        first = jnp.where(upper == 0, part, got)
        second = jnp.where(upper == 0, got, part)
        part = jnp.concatenate([first, second], axis=0)
    return part.astype(jnp.float32)


def sum_small(values, steps):
    for axis, bit in steps:
        values = values + swap(values, axis, bit)
    return values


def body(
    block_input,
    expert_ids,
    ln1_gain,
    ln1_bias,
    w_qkv,
    w_o,
    ln2_gain,
    ln2_bias,
    w_in,
    b_in,
    w_out,
    b_out,
    cotangent,
):
    expert_count = lax.axis_size("expert")
    own_expert = lax.axis_index("expert")
    slot_rows = block_input.shape[1]
    model_width = block_input.shape[2]
    seq_ids = expert_ids[0]
    seq_length = seq_ids.shape[0]
    capacity = 5 * seq_length // expert_count
    chunk = seq_length // expert_count
    group_ids = lax.all_to_all(
        jnp.broadcast_to(seq_ids[None], (expert_count, seq_length)),
        "expert",
        split_axis=0,
        concat_axis=0,
        tiled=True,
    )
    devices = jnp.arange(expert_count, dtype=jnp.int32)
    counts = jnp.sum(
        (group_ids[:, :, None] == devices[None, None, :]).astype(jnp.int32), axis=1
    )
    fullest = jnp.argmax(counts, axis=0).astype(jnp.int32)
    taken = jnp.sum((fullest[:, None] == devices[None, :]).astype(jnp.int32), axis=0)
    distinct = jnp.all(taken == 1)
    held_by = jnp.where(distinct, fullest, devices)
    owner = jnp.sum(
        (held_by[:, None] == devices[None, :]).astype(jnp.int32) * devices[:, None], axis=0
    )
    held = held_by[own_expert]
    most = jnp.max(jnp.where(owner[:, None] == devices[None, :], 0, counts))
    for axis, bit in bits_of("dp"):
        most = jnp.maximum(most, swap(most, axis, bit))
    rounds = (most + chunk - 1) // chunk
    from_each = counts[:, own_expert]
    ends_at = jnp.cumsum(from_each)
    starts_at = ends_at - from_each
    slot_index = jnp.arange(slot_rows, dtype=jnp.int32)
    passed = (ends_at[None, :] <= slot_index[:, None]).astype(jnp.int32)
    source = jnp.sum(passed, axis=1)
    occupied = slot_index < ends_at[-1]
    within = slot_index - jnp.sum(passed * from_each[None, :], axis=1)
    at_device = jnp.sum(
        (source[:, None] == devices[None, :]).astype(jnp.int32) * owner[None, :], axis=1
    )
    at_home = at_device == own_expert
    slot_columns = (
        jnp.where(occupied & at_home, within, -1),
        at_device,
        jnp.where(occupied & ~at_home, within, -chunk),
    )
    held_ids = lax.dynamic_index_in_dim(group_ids, held, 0, keepdims=False)
    choose = (held_ids[:, None] == devices[None, :]).astype(jnp.int32)
    rank_in = jnp.sum((jnp.cumsum(choose, axis=0) - 1) * choose, axis=1)
    is_own = held_ids == own_expert
    token_columns = (
        jnp.where(is_own, rank_in, -1),
        held_ids,
        jnp.where(is_own, -chunk, rank_in),
    )

    def to_sequence(table):
        return move_rows(
            table, slot_columns, token_columns, capacity, chunk, expert_count, rounds
        )

    def to_expert(table):
        return move_rows(
            table, token_columns, slot_columns, capacity, chunk, expert_count, rounds
        )

    tokens_in = to_sequence(block_input[0])
    normed, scaled_one, inverse_one = normalize(tokens_in, ln1_gain, ln1_bias)
    normed_low = normed.astype(jnp.bfloat16)
    mixed_qkv = jnp.dot(normed_low, w_qkv, preferred_element_type=jnp.float32).astype(jnp.bfloat16)
    heads_shape = (seq_length, HEADS, HEAD_DIM)
    queries = mixed_qkv[:, :model_width].reshape(heads_shape)
    keys_all = mixed_qkv[:, model_width : 2 * model_width].reshape(heads_shape)
    values_all = mixed_qkv[:, 2 * model_width :].reshape(heads_shape)
    context, log_totals = attend_forward(queries, keys_all, values_all)
    context_low = context.reshape(seq_length, model_width).astype(jnp.bfloat16)
    hidden = tokens_in + jnp.dot(context_low, w_o, preferred_element_type=jnp.float32)
    placed = to_expert(hidden.astype(bf16))
    normed_two, scaled_two, inverse_two = normalize(placed, ln2_gain, ln2_bias)
    inputs_low = normed_two.astype(jnp.bfloat16)
    live = occupied[:, None]
    grad_low = jnp.where(live, cotangent[0], jnp.zeros((), jnp.bfloat16))
    full_in, full_out, full_bias_in, full_bias_out = (
        lax.all_gather(w_in, "dp", axis=1, tiled=True),
        lax.all_gather(w_out, "dp", axis=1, tiled=True),
        lax.all_gather(b_in, "dp", axis=1, tiled=True),
        lax.all_gather(b_out, "dp", axis=1, tiled=True),
    )
    weight_in = full_in[0]
    weight_out = full_out[0]
    pre_act = lax.dot_general(
        inputs_low, weight_in, contract_last, preferred_element_type=jnp.float32
    ) + full_bias_in[0].astype(jnp.float32)
    act_low = smooth_gelu(pre_act).astype(jnp.bfloat16)
    expert_out = jnp.dot(act_low, weight_out, preferred_element_type=jnp.float32) + full_bias_out[
        0
    ].astype(jnp.float32)
    result = jnp.where(live, placed + expert_out, 0.0).astype(jnp.bfloat16)
    grad_act = lax.dot_general(
        grad_low, weight_out, contract_last, preferred_element_type=jnp.float32
    )
    grad_pre = (grad_act * gelu_slope(pre_act)).astype(jnp.bfloat16)
    grad_normed = jnp.dot(grad_pre, weight_in, preferred_element_type=jnp.float32)
    local_w_in = lax.dot_general(
        grad_pre, inputs_low, contract_first, preferred_element_type=jnp.float32
    )
    local_w_out = lax.dot_general(
        act_low, grad_low, contract_first, preferred_element_type=jnp.float32
    )
    local_b_in = jnp.sum(grad_pre.astype(jnp.float32), axis=0)
    local_b_out = jnp.sum(grad_low.astype(jnp.float32), axis=0)
    grad_w_in, grad_w_out, grad_b_in, grad_b_out = (
        lax.psum_scatter(
            local_w_in[None].astype(jnp.bfloat16), "dp", scatter_dimension=1, tiled=True
        ).astype(jnp.float32),
        lax.psum_scatter(
            local_w_out[None].astype(jnp.bfloat16), "dp", scatter_dimension=1, tiled=True
        ).astype(jnp.float32),
        lax.psum_scatter(
            local_b_in[None].astype(jnp.bfloat16), "dp", scatter_dimension=1, tiled=True
        ).astype(jnp.float32),
        lax.psum_scatter(
            local_b_out[None].astype(jnp.bfloat16), "dp", scatter_dimension=1, tiled=True
        ).astype(jnp.float32),
    )
    grad_placed_norm, local_ln2_gain, local_ln2_bias = normalize_back(
        grad_normed, scaled_two, inverse_two, ln2_gain
    )
    grad_placed = grad_low.astype(jnp.float32) + grad_placed_norm
    grad_hidden = to_sequence(grad_placed.astype(bf16)).astype(bf16)
    local_w_o = lax.dot_general(
        context_low, grad_hidden, contract_first, preferred_element_type=jnp.float32
    )
    grad_context = (
        lax.dot_general(grad_hidden, w_o, contract_last, preferred_element_type=jnp.float32)
        .astype(jnp.bfloat16)
        .reshape(heads_shape)
    )
    grad_queries, grad_keys, grad_values = attend_backward(
        queries, keys_all, values_all, grad_context, log_totals
    )
    grad_mixed = jnp.concatenate(
        [
            grad_queries.reshape(seq_length, model_width),
            grad_keys.reshape(seq_length, model_width),
            grad_values.reshape(seq_length, model_width),
        ],
        axis=1,
    ).astype(jnp.bfloat16)
    local_w_qkv = lax.dot_general(
        normed_low, grad_mixed, contract_first, preferred_element_type=jnp.float32
    )
    grad_normed_one = lax.dot_general(
        grad_mixed, w_qkv, contract_last, preferred_element_type=jnp.float32
    )
    grad_tokens_norm, local_ln1_gain, local_ln1_bias = normalize_back(
        grad_normed_one, scaled_one, inverse_one, ln1_gain
    )
    grad_tokens = grad_hidden.astype(jnp.float32) + grad_tokens_norm
    grad_input = to_expert(grad_tokens.astype(bf16)).astype(bf16)
    by_x = bits_of("dp") + bits_of("expert")
    dense = jnp.concatenate([local_w_qkv.astype(bf16), local_w_o.astype(bf16)], axis=1)
    summed = sum_everywhere(dense, by_x)
    grad_w_qkv = summed[:, : 3 * model_width]
    grad_w_o = summed[:, 3 * model_width :]
    norms = sum_small(
        jnp.stack([local_ln1_gain, local_ln1_bias, local_ln2_gain, local_ln2_bias]), by_x
    )
    grad_ln1_gain, grad_ln1_bias, grad_ln2_gain, grad_ln2_bias = norms
    return (
        result[None],
        grad_input[None],
        grad_ln1_gain,
        grad_ln1_bias,
        grad_w_qkv,
        grad_w_o,
        grad_ln2_gain,
        grad_ln2_bias,
        grad_w_in,
        grad_b_in,
        grad_w_out,
        grad_b_out,
    )


def solution(mesh):
    placed = (
        P("dp", "expert", None),
        P("dp", "expert"),
        P(),
        P(),
        P(),
        P(),
        P(),
        P(),
        P("expert", "dp", None),
        P("expert", "dp"),
        P("expert", "dp", None),
        P("expert", "dp"),
        P("dp", "expert", None),
    )
    return jax.shard_map(
        body,
        mesh=mesh,
        in_specs=placed,
        out_specs=(
            P("dp", "expert", None),
            P("dp", "expert", None),
            P(),
            P(),
            P(),
            P(),
            P(),
            P(),
            P("expert", "dp", None),
            P("expert", "dp"),
            P("expert", "dp", None),
            P("expert", "dp"),
        ),
        check_vma=False,
    )
```

```python
import functools

import jax
import jax.numpy as jnp
from jax import lax
from jax.experimental import pallas as pl
from jax.experimental.pallas import tpu as pltpu
from jax.sharding import PartitionSpec as P

HEADS = 16
HEAD_DIM = 64


epsilon = 1e-05
gelu_c = 0.7978845608028654
contract_last = (((1,), (1,)), ((), ()))
contract_first = (((0,), (0,)), ((), ()))


bf16 = jnp.bfloat16
PAIR = 2 * HEAD_DIM
BIG_VMEM = 48 << 20
f32 = jnp.float32


def dot(left, right):
    return jnp.dot(left, right, preferred_element_type=f32)


def dot_last(left, right):
    return lax.dot_general(left, right, contract_last, preferred_element_type=f32)


def dot_first(left, right):
    return lax.dot_general(left, right, contract_first, preferred_element_type=f32)


def head_parts(pair):
    first = lax.broadcasted_iota(jnp.int32, (1, PAIR), 1) < HEAD_DIM
    zero = jnp.zeros_like(pair)
    return [jnp.where(first, pair, zero), jnp.where(first, zero, pair)]


def attend_kernel(block, q_ref, k_ref, v_ref, context_ref, logs_ref):
    length = q_ref.shape[0]
    keys = head_parts(k_ref[...])
    values_t = v_ref[...].T
    rows = lax.broadcasted_iota(jnp.int32, (block, block), 0)
    cols = lax.broadcasted_iota(jnp.int32, (block, block), 1)
    allowed = rows <= cols
    for low in range(0, length, block):
        high = low + block
        queries = q_ref[low:high, :] * jnp.asarray(0.125, bf16)
        outputs = []
        for head in range(2):
            value_rows = values_t[head * HEAD_DIM : (head + 1) * HEAD_DIM]
            near = jnp.where(allowed, dot_last(keys[head][low:high], queries), -1e30)
            peak = jnp.max(near, axis=0, keepdims=True)
            if low:
                far = dot_last(keys[head][:low], queries)
                peak = jnp.maximum(peak, jnp.max(far, axis=0, keepdims=True))
            near = jnp.exp(near - peak)
            total = jnp.sum(near, axis=0, keepdims=True)
            result = dot(value_rows[:, low:high], near.astype(bf16))
            if low:
                far = jnp.exp(far - peak)
                total = total + jnp.sum(far, axis=0, keepdims=True)
                result = result + dot(value_rows[:, :low], far.astype(bf16))
            outputs.append(result / total)
            logs_ref[0, head : head + 1, low:high] = peak + jnp.log(total)
        context_ref[low:high, :] = jnp.concatenate(outputs, axis=0).T.astype(bf16)


def pair_columns(length, offset):
    return pl.BlockSpec((length, PAIR), lambda pair: (0, offset + pair))


def pair_logs(length):
    return pl.BlockSpec((1, 8, length), lambda pair: (pair, 0, 0))


def attend(mixed):
    length, width = mixed.shape[0], mixed.shape[1] // 3
    pairs = width // PAIR
    return pl.pallas_call(
        functools.partial(attend_kernel, min(512, length)),
        grid=(pairs,),
        in_specs=[pair_columns(length, part * pairs) for part in range(3)],
        out_specs=[pair_columns(length, 0), pair_logs(length)],
        out_shape=[
            jax.ShapeDtypeStruct((length, width), bf16),
            jax.ShapeDtypeStruct((pairs, 8, length), f32),
        ],
        compiler_params=pltpu.CompilerParams(vmem_limit_bytes=BIG_VMEM),
        cost_estimate=pl.CostEstimate(
            flops=4 * length * length * width,
            bytes_accessed=8 * length * width,
            transcendentals=length * length * width // HEAD_DIM,
        ),
    )(mixed, mixed, mixed)


def attend_back_kernel(
    block, q_ref, k_ref, v_ref, context_ref, grad_ref, logs_ref, out_ref, grad_k, grad_v
):
    length = q_ref.shape[0]
    keys, values, grads = k_ref[...], v_ref[...], grad_ref[...]
    queries = head_parts(q_ref[...] * jnp.asarray(0.125, bf16))
    key_parts = head_parts(keys)
    grad_parts = head_parts(grads)
    products = head_parts(grads.astype(f32) * context_ref[...].astype(f32))
    centres = [jnp.sum(part, axis=1, keepdims=True) for part in products]
    logs = logs_ref[0].T
    rows = lax.broadcasted_iota(jnp.int32, (block, block), 0)
    cols = lax.broadcasted_iota(jnp.int32, (block, block), 1)
    allowed = cols <= rows
    for low in reversed(range(0, length, block)):
        high = low + block
        add_q, add_k, add_v = [], [], []
        for head in range(2):
            scores = dot_last(queries[head][low:high], keys[:high])
            probs = jnp.exp(scores - logs[low:high, head : head + 1])
            near = jnp.where(allowed, probs[:, low:], 0.0)
            probs = jnp.concatenate([probs[:, :low], near], axis=1) if low else near
            grad_probs = dot_last(grad_parts[head][low:high], values[:high])
            grad_scores = (probs * (grad_probs - centres[head][low:high])).astype(bf16)
            add_q.append(dot(grad_scores, key_parts[head][:high]))
            add_k.append(dot_first(grad_scores, queries[head][low:high]))
            add_v.append(dot_first(probs.astype(bf16), grad_parts[head][low:high]))
        out_ref[0, low:high, :] = ((add_q[0] + add_q[1]) * 0.125).astype(bf16)
        if high == length:
            grad_k[...] = add_k[0] + add_k[1]
            grad_v[...] = add_v[0] + add_v[1]
        else:
            grad_k[:high, :] += add_k[0] + add_k[1]
            grad_v[:high, :] += add_v[0] + add_v[1]
    out_ref[1] = grad_k[...].astype(bf16)
    out_ref[2] = grad_v[...].astype(bf16)


def attend_back(mixed, context, grad_context, logs):
    length, width = context.shape
    pairs = width // PAIR
    return pl.pallas_call(
        functools.partial(attend_back_kernel, min(256, length)),
        grid=(pairs,),
        in_specs=[pair_columns(length, part * pairs) for part in range(3)]
        + [pair_columns(length, 0)] * 2
        + [pair_logs(length)],
        out_specs=pl.BlockSpec((3, length, PAIR), lambda pair: (0, 0, pair)),
        out_shape=jax.ShapeDtypeStruct((3, length, width), bf16),
        scratch_shapes=[pltpu.VMEM((length, PAIR), f32), pltpu.VMEM((length, PAIR), f32)],
        compiler_params=pltpu.CompilerParams(vmem_limit_bytes=BIG_VMEM),
        cost_estimate=pl.CostEstimate(
            flops=10 * length * length * width,
            bytes_accessed=16 * length * width,
            transcendentals=length * length * width // HEAD_DIM,
        ),
    )(mixed, mixed, mixed, context, grad_context, logs)


def place_rows(columns, count, table):
    chosen = (columns[None, :] == jnp.arange(count, dtype=jnp.int32)[:, None]).astype(bf16)
    return dot(chosen, table).astype(bf16)


def exchange(packed, expert_count):
    return lax.all_to_all(
        packed.reshape(expert_count, -1, packed.shape[-1]),
        "expert",
        split_axis=0,
        concat_axis=0,
        tiled=True,
    ).reshape(-1, packed.shape[-1])


def remote_column(places, chunk, step):
    device, rank = places[1:]
    return jnp.where(rank // chunk == step, device * chunk + rank % chunk, -1)


def pack(table, places, chunk, expert_count, step=0):
    return place_rows(remote_column(places, chunk, step), expert_count * chunk, table)


def more_rounds(arrived, table, source, target, chunk, expert_count, rounds):
    def again(state):
        step, kept = state
        packed = pack(table, source, chunk, expert_count, step)
        got = select_rows(remote_column(target, chunk, step), exchange(packed, expert_count))
        return (step + 1, kept + got)

    count = target[0].shape[0]
    start = (jnp.int32(1), jnp.zeros((count, table.shape[1]), bf16))
    return lax.while_loop(lambda state: state[0] < rounds, again, start)[1]


def select_rows(columns, table):
    chosen = (columns[:, None] == jnp.arange(table.shape[0], dtype=jnp.int32)[None, :]).astype(bf16)
    return dot(chosen, table).astype(bf16)


def swap(values, axis, bit):
    size = lax.axis_size(axis)
    return lax.ppermute(values, axis, [(i, i ^ bit) for i in range(size)])


def bits_of(axis, size=None):
    size = size or lax.axis_size(axis)
    return [(axis, 1 << k) for k in range(size.bit_length() - 1)]


def peer_index(axis, bit):
    own = lax.axis_index(axis)
    side = (own // bit) % 2
    return side, own + bit * (1 - 2 * side)


def greet(peers):
    barrier = pltpu.get_barrier_semaphore()
    for axis, index in peers:
        pl.semaphore_signal(
            barrier, inc=1, device_id={axis: index}, device_id_type=pl.DeviceIdType.MESH
        )
    pl.semaphore_wait(barrier, len(peers))


def ring_peers(count):
    own = lax.axis_index("expert")
    return [lax.rem(own + step, count) for step in range(1, count)]


def remote(source, target, send_sem, recv_sem, axis, index):
    return pltpu.make_async_remote_copy(
        src_ref=source,
        dst_ref=target,
        send_sem=send_sem,
        recv_sem=recv_sem,
        device_id={axis: index},
        device_id_type=pl.DeviceIdType.MESH,
    )


def rows_of(offset, size):
    return pl.ds(pl.multiple_of(offset, 16), size)


def plan_orders(dp_count, expert_count, rows, width):
    dp_bits, expert_bits = bits_of("dp", dp_count), bits_of("expert", expert_count)
    across, along = dp_bits[1:], expert_bits
    y_bits = along[: max(1, len(along) // 2)]
    z_bits = along[len(y_bits) :]
    if expert_count == 8:
        y_bits, z_bits = along[:1], along[1:]
    orders = (across + y_bits + z_bits, y_bits + across + z_bits)
    steps = len(orders[0])
    chunks = max(1, rows // (4 * 16 << steps))
    return dp_bits[0], orders, chunks


def finish_kernel(
    first, orders, chunks, count, dense_ref, norm_ref, packed_ref, sum_ref, norm_out, bias_out, arrived_ref,
    work, done, *scratch
):
    steps = len(orders[0])
    core_slots = scratch[0]
    part_slots = scratch[1 : 1 + steps]
    norm_work, norm_slots = scratch[1 + steps : 3 + steps]
    core_send, core_recv, part_send, part_recv, norm_send, norm_recv = scratch[3 + steps : 9 + steps]
    swap_send, swap_recv, local_sem = scratch[9 + steps :]
    rows = work.shape[0] // chunks
    half, quarter = rows // 2, rows // 4
    own = lax.axis_index("expert")
    others = ring_peers(count)
    links = [first] + list(orders[0])
    dp_peers = [(axis, peer_index(axis, bit)[1]) for axis, bit in links if axis == "dp"]
    greet([("expert", index) for index in others] + dp_peers)

    swaps = []
    import os
    for step, index in enumerate(others):
        copy = remote(packed_ref.at[index], arrived_ref.at[own], swap_send.at[step], swap_recv.at[step], "expert", index)
        copy.start()
        swaps.append(copy)
    home = pltpu.make_async_copy(packed_ref.at[own], arrived_ref.at[own], local_sem.at[chunks])
    home.start()

    side0, peer0 = peer_index(*first)
    started = []
    norm_work[...] = norm_ref[...]

    def add_rows(offset, size, slot, target):
        block = min(size, 64)

        @pl.loop(0, size // block)
        def _(index):
            here = rows_of(offset + index * block, block)
            there = rows_of(index * block, block)
            target[here, :] = (work[here, :].astype(f32) + slot[there, :].astype(f32)).astype(bf16)

    state = {}

    def event(chunk, number):
        base = chunk * rows
        if number == 0:
            kept = base + side0 * half
            given = base + (1 - side0) * half
            load = pltpu.make_async_copy(dense_ref.at[rows_of(kept, half)], work.at[rows_of(kept, half)], local_sem.at[chunk])
            load.start()
            copy = remote(dense_ref.at[rows_of(given, half)], core_slots.at[chunk], core_send.at[chunk, 0], core_recv.at[chunk, 0], first[0], peer0)
            copy.start()
            started.append(copy)
            state[chunk] = dict(kept=kept, load=load, copy=copy)
        elif number <= 2 * steps + 1:
            for part in range(2):
                go_on(chunk, part, number - 1)
        if number == 2 * steps + 1:
            kept = state[chunk]["kept"]
            copy = remote(done.at[rows_of(kept, half)], done.at[rows_of(kept, half)], core_send.at[chunk, 1], core_recv.at[chunk, 1], first[0], peer0)
            copy.start()
            started.append(copy)
            state[chunk]["copy"] = copy
        if number == 2 * steps + 2:
            state[chunk]["copy"].wait_recv()
            store = pltpu.make_async_copy(done.at[pl.ds(base, rows)], sum_ref.at[pl.ds(base, rows)], local_sem.at[chunk])
            store.start()
            state[chunk]["store"] = store

    def go_on(chunk, part, step):
        here = state[chunk]
        if step == 0:
            if part == 0:
                here["load"].wait()
                here["copy"].wait_recv()
                add_rows(here["kept"], half, core_slots.at[chunk], work)
            offset = here["kept"] + part * quarter
        else:
            offset, size, copy, slot = here[part]
            copy.wait_recv()
            if step <= steps:
                add_rows(offset, size, slot, work if step < steps else done)
        if step < steps:
            axis, bit = orders[part][step]
            side, peer = peer_index(axis, bit)
            size = quarter >> (step + 1)
            slot = part_slots[step].at[chunk, part]
            given = offset + (1 - side) * size
            kept = offset + side * size
            copy = remote(work.at[rows_of(given, size)], slot, part_send.at[chunk, part, step], part_recv.at[chunk, part, step], axis, peer)
            copy.start()
            started.append(copy)
            here[part] = (kept, size, copy, slot)
        elif step < 2 * steps:
            back = 2 * steps - 1 - step
            axis, bit = orders[part][back]
            side, peer = peer_index(axis, bit)
            size = quarter >> (back + 1)
            if step > steps:
                offset = offset - here["side", part] * (size // 2)
            here["side", part] = side
            copy = remote(done.at[rows_of(offset, size)], done.at[rows_of(offset, size)], part_send.at[chunk, part, step], part_recv.at[chunk, part, step], axis, peer)
            copy.start()
            started.append(copy)
            here[part] = (offset, size, copy, None)

    norm_copy = None
    for tick in range(2 * steps + 2 + chunks):
        for chunk in range(chunks):
            number = tick - chunk
            if 0 <= number <= 2 * steps + 2:
                event(chunk, number)
        if tick <= len(links):
            if norm_copy is not None:
                norm_copy.wait()
                norm_work[...] += norm_slots[tick - 1]
                if tick == sum(axis == "dp" for axis, _ in links):
                    bias_out[...] = norm_work[8:16, :]
            if tick < len(links):
                axis, bit = links[tick]
                norm_copy = remote(norm_work, norm_slots.at[tick], norm_send.at[tick], norm_recv.at[tick], axis, peer_index(axis, bit)[1])
                norm_copy.start()
            else:
                norm_out[...] = norm_work[...]
    for copy in started:
        copy.wait_send()
    for copy in swaps:
        copy.wait()
    home.wait()
    for chunk in range(chunks):
        state[chunk]["store"].wait()


def finish(dense, norms, packed, dp_count):
    count = packed.shape[0]
    rows, width = dense.shape
    first, orders, chunks = plan_orders(dp_count, count, rows, width)
    steps = len(orders[0])
    part = rows // chunks // 4
    return pl.pallas_call(
        functools.partial(finish_kernel, first, orders, chunks, count),
        in_specs=[
            pl.BlockSpec(memory_space=pl.ANY),
            pl.BlockSpec(memory_space=pltpu.VMEM),
            pl.BlockSpec(memory_space=pl.ANY),
        ],
        out_specs=[
            pl.BlockSpec(memory_space=pl.ANY),
            pl.BlockSpec(memory_space=pltpu.VMEM),
            pl.BlockSpec(memory_space=pltpu.VMEM),
            pl.BlockSpec(memory_space=pl.ANY),
        ],
        out_shape=[
            jax.ShapeDtypeStruct(dense.shape, bf16),
            jax.ShapeDtypeStruct(norms.shape, f32),
            jax.ShapeDtypeStruct((8, width), f32),
            jax.ShapeDtypeStruct(packed.shape, bf16),
        ],
        scratch_shapes=[pltpu.VMEM(dense.shape, bf16)] * 2 + [pltpu.VMEM((chunks, 2 * part, width), bf16)]
        + [pltpu.VMEM((chunks, 2, part >> (step + 1), width), bf16) for step in range(steps)]
        + [
            pltpu.VMEM(norms.shape, f32),
            pltpu.VMEM((steps + 1,) + norms.shape, f32),
            pltpu.SemaphoreType.DMA((chunks, 2)),
            pltpu.SemaphoreType.DMA((chunks, 2)),
            pltpu.SemaphoreType.DMA((chunks, 2, 2 * steps)),
            pltpu.SemaphoreType.DMA((chunks, 2, 2 * steps)),
            pltpu.SemaphoreType.DMA((steps + 1,)),
            pltpu.SemaphoreType.DMA((steps + 1,)),
            pltpu.SemaphoreType.DMA((count - 1,)),
            pltpu.SemaphoreType.DMA((count - 1,)),
            pltpu.SemaphoreType.DMA((chunks + 1,)),
        ],
        compiler_params=pltpu.CompilerParams(
            collective_id=7, has_side_effects=True, vmem_limit_bytes=BIG_VMEM
        ),
        cost_estimate=pl.CostEstimate(
            flops=2 * rows * width, bytes_accessed=8 * rows * width, transcendentals=0
        ),
    )(dense, norms, packed)


def pick(columns, numbers, table):
    return dot((columns == numbers).astype(bf16), table)


def joined_rows(near_ref, far_ref, extra_ref, numbers_ref, table_ref, arrived_ref):
    places = lax.broadcasted_iota(jnp.int32, (1, arrived_ref.shape[0]), 1)
    rows = pick(near_ref[...], numbers_ref[...], table_ref[...])
    return rows + pick(far_ref[...], places, arrived_ref[...]) + extra_ref[...].astype(f32)


def norm_parts(rows):
    centre = jnp.mean(rows, axis=-1, keepdims=True)
    centred = rows - centre
    inverse = lax.rsqrt(jnp.mean(centred * centred, axis=-1, keepdims=True) + epsilon)
    return centred * inverse, inverse


def norm_back(grad, scaled, inverse, gains):
    grad_scaled = grad * gains
    first = jnp.mean(grad_scaled, axis=-1, keepdims=True)
    second = jnp.mean(grad_scaled * scaled, axis=-1, keepdims=True)
    return inverse * (grad_scaled - first - scaled * second)


def first_kernel(near, far, extra, numbers, table, arrived, gain, bias, weight, rows_ref, normed_ref, mixed_ref):
    rows = joined_rows(near, far, extra, numbers, table, arrived)
    rows_ref[...] = rows.astype(bf16)
    normed = (norm_parts(rows)[0] * gain[...] + bias[...]).astype(bf16)
    normed_ref[...] = normed
    mixed_ref[...] = dot(normed, weight[...]).astype(bf16)


def third_kernel(near, far, extra, numbers, table, arrived, weight, rows_ref, product_ref):
    rows = joined_rows(near, far, extra, numbers, table, arrived).astype(bf16)
    rows_ref[...] = rows
    product_ref[...] = dot_last(rows, weight[...]).astype(bf16)


def last_kernel(near, far, extra, numbers, table, arrived, rows_ref):
    rows_ref[...] = joined_rows(near, far, extra, numbers, table, arrived).astype(bf16)


def block_rows(width):
    return pl.BlockSpec((256, width), lambda step: (step, 0))


def in_full(array):
    return pl.BlockSpec(array.shape, lambda step: (0,) * array.ndim, pipeline_mode=pl.Buffered(1))


def join(kernel, blocked, whole, widths):
    count = blocked[0].shape[0]
    width = whole[1].shape[1]
    inside = whole[1].shape[0] + whole[2].shape[0]
    return pl.pallas_call(
        kernel,
        grid=(count // 256,),
        in_specs=[block_rows(array.shape[1]) for array in blocked]
        + [in_full(array) for array in whole],
        out_specs=[block_rows(size) for size in widths],
        out_shape=[jax.ShapeDtypeStruct((count, size), bf16) for size in widths],
        compiler_params=pltpu.CompilerParams(vmem_limit_bytes=BIG_VMEM),
        cost_estimate=pl.CostEstimate(
            flops=2 * count * width * (inside + sum(widths) - width),
            bytes_accessed=2 * (inside * width + count * sum(widths)),
            transcendentals=0,
        ),
    )(*blocked, *whole)


def expert_kernel(
    near, far, extra, live, grad_y, grad_act, numbers, table, arrived, gain, bias,
    weight_in, bias_in, weight_out, bias_out,
    out_ref, normed_ref, act_ref, grad_pre_ref, grad_ref, sum_ref, bias_sum_ref,
):
    rows = joined_rows(near, far, extra, numbers, table, arrived).astype(bf16).astype(f32)
    scaled, inverse = norm_parts(rows)
    normed = (scaled * gain[...] + bias[...]).astype(bf16)
    normed_ref[...] = normed
    hidden = weight_in.shape[0]
    block = min(512, hidden)

    @pl.when(pl.program_id(0) == 0)
    def _():
        sum_ref[...] = jnp.zeros_like(sum_ref)
        bias_sum_ref[...] = jnp.zeros_like(bias_sum_ref)

    result = jnp.zeros(rows.shape, f32)
    grad = jnp.zeros(rows.shape, f32)
    for low in range(0, hidden, block):
        part = slice(low, low + block)
        pre = dot_last(normed, weight_in[part, :]) + bias_in[:, part]
        square = pre * pre
        tangent = jnp.tanh(gelu_c * (pre + 0.044715 * pre * square))
        half = 0.5 * pre
        act = (half + half * tangent).astype(bf16)
        slope = (0.5 + 0.5 * tangent) + half * (1.0 - tangent * tangent) * (
            gelu_c + (3.0 * 0.044715 * gelu_c) * square
        )
        grad_pre_f = grad_act[:, part].astype(f32) * slope
        grad_pre = grad_pre_f.astype(bf16)
        act_ref[:, part] = act
        grad_pre_ref[:, part] = grad_pre
        bias_sum_ref[0:1, part] += jnp.sum(grad_pre.astype(f32), axis=0, keepdims=True)
        result += dot(act, weight_out[part, :])
        grad += dot(grad_pre, weight_in[part, :])
    out = rows + result + bias_out[...]
    out_ref[...] = jnp.where(live[...] > 0, out, 0.0).astype(bf16)
    grad_in = grad_y[...].astype(f32)
    grad_ref[...] = (grad_in + norm_back(grad, scaled, inverse, gain[...])).astype(bf16)
    sum_ref[0:1, :] += jnp.sum(grad * scaled, axis=0, keepdims=True)
    sum_ref[1:2, :] += jnp.sum(grad, axis=0, keepdims=True)
    sum_ref[2:3, :] += jnp.sum(grad_in, axis=0, keepdims=True)


def run_expert(blocked, whole, hidden):
    count, width = blocked[2].shape
    widths = (width, width, hidden, hidden, width)

    def sums(size):
        return pl.BlockSpec((8, size), lambda step: (0, 0))

    return pl.pallas_call(
        expert_kernel,
        grid=(count // 256,),
        in_specs=[block_rows(array.shape[1]) for array in blocked]
        + [in_full(array) for array in whole],
        out_specs=[block_rows(size) for size in widths] + [sums(width), sums(hidden)],
        out_shape=[jax.ShapeDtypeStruct((count, size), bf16) for size in widths]
        + [jax.ShapeDtypeStruct((8, width), f32), jax.ShapeDtypeStruct((8, hidden), f32)],
        compiler_params=pltpu.CompilerParams(vmem_limit_bytes=58 << 20),
        cost_estimate=pl.CostEstimate(
            flops=6 * count * width * hidden,
            bytes_accessed=2 * count * (5 * width + 3 * hidden) + 4 * width * hidden,
            transcendentals=count * hidden,
        ),
    )(*blocked, *whole)


def back_kernel(grad_ref, weight_ref, tokens_ref, hidden_ref, gain_ref, out_ref, sum_ref):
    width = gain_ref.shape[1]
    grad = sum(
        dot_last(grad_ref[part], weight_ref[:, part * width : (part + 1) * width])
        for part in range(3)
    )
    scaled, inverse = norm_parts(tokens_ref[...].astype(f32))
    result = hidden_ref[...].astype(f32) + norm_back(grad, scaled, inverse, gain_ref[...])
    out_ref[...] = result.astype(bf16)

    @pl.when(pl.program_id(0) == 0)
    def _():
        sum_ref[...] = jnp.zeros_like(sum_ref)

    sum_ref[0:1, :] += jnp.sum(grad * scaled, axis=0, keepdims=True)
    sum_ref[1:2, :] += jnp.sum(grad, axis=0, keepdims=True)


def back(grad_mixed, weight, tokens, grad_hidden, gain):
    count, width = tokens.shape
    block = 256

    def by_rows():
        return pl.BlockSpec((block, width), lambda step: (step, 0))

    return pl.pallas_call(
        back_kernel,
        grid=(count // block,),
        in_specs=[
            pl.BlockSpec((3, block, width), lambda step: (0, step, 0)),
            pl.BlockSpec(weight.shape, lambda step: (0, 0)),
            by_rows(),
            by_rows(),
            pl.BlockSpec((1, width), lambda step: (0, 0)),
        ],
        out_specs=[by_rows(), pl.BlockSpec((8, width), lambda step: (0, 0))],
        out_shape=[
            jax.ShapeDtypeStruct((count, width), bf16),
            jax.ShapeDtypeStruct((8, width), f32),
        ],
        compiler_params=pltpu.CompilerParams(vmem_limit_bytes=BIG_VMEM),
        cost_estimate=pl.CostEstimate(
            flops=6 * count * width * width, bytes_accessed=20 * count * width, transcendentals=0
        ),
    )(grad_mixed, weight, tokens, grad_hidden, gain)


def body(
    block_input,
    expert_ids,
    ln1_gain,
    ln1_bias,
    w_qkv,
    w_o,
    ln2_gain,
    ln2_bias,
    w_in,
    b_in,
    w_out,
    b_out,
    cotangent,
):
    expert_count = lax.axis_size("expert")
    own_expert = lax.axis_index("expert")
    slot_rows = block_input.shape[1]
    model_width = block_input.shape[2]
    seq_ids = expert_ids[0]
    seq_length = seq_ids.shape[0]
    capacity = 5 * seq_length // expert_count
    chunk = seq_length // expert_count
    group_ids = lax.all_to_all(
        jnp.broadcast_to(seq_ids[None], (expert_count, seq_length)),
        "expert",
        split_axis=0,
        concat_axis=0,
        tiled=True,
    )
    devices = jnp.arange(expert_count, dtype=jnp.int32)
    counts = jnp.sum(
        (group_ids[:, :, None] == devices[None, None, :]).astype(jnp.int32), axis=1
    )
    fullest = jnp.argmax(counts, axis=0).astype(jnp.int32)
    taken = jnp.sum((fullest[:, None] == devices[None, :]).astype(jnp.int32), axis=0)
    distinct = jnp.all(taken == 1)
    held_by = jnp.where(distinct, fullest, devices)
    owner = jnp.sum(
        (held_by[:, None] == devices[None, :]).astype(jnp.int32) * devices[:, None], axis=0
    )
    held = held_by[own_expert]
    most = jnp.max(jnp.where(owner[:, None] == devices[None, :], 0, counts))
    for axis, bit in bits_of("dp"):
        most = jnp.maximum(most, swap(most, axis, bit))
    rounds = (most + chunk - 1) // chunk
    from_each = counts[:, own_expert]
    ends_at = jnp.cumsum(from_each)
    starts_at = ends_at - from_each
    slot_index = jnp.arange(slot_rows, dtype=jnp.int32)
    passed = (ends_at[None, :] <= slot_index[:, None]).astype(jnp.int32)
    source = jnp.sum(passed, axis=1)
    occupied = slot_index < ends_at[-1]
    within = slot_index - jnp.sum(passed * from_each[None, :], axis=1)
    at_device = jnp.sum(
        (source[:, None] == devices[None, :]).astype(jnp.int32) * owner[None, :], axis=1
    )
    at_home = at_device == own_expert
    slot_places = (
        jnp.where(occupied & at_home, within, -2),
        at_device,
        jnp.where(occupied & ~at_home, within, -chunk),
    )
    held_ids = lax.dynamic_index_in_dim(group_ids, held, 0, keepdims=False)
    choose = (held_ids[:, None] == devices[None, :]).astype(jnp.int32)
    rank_in = jnp.sum((jnp.cumsum(choose, axis=0) - 1) * choose, axis=1)
    is_own = held_ids == own_expert
    token_places = (
        jnp.where(is_own, rank_in, -1),
        held_ids,
        jnp.where(is_own, -chunk, rank_in),
    )

    def start(table, places):
        return exchange(pack(table, places, chunk, expert_count), expert_count)

    def sides(arrived, table, source, target):
        extra = more_rounds(arrived, table, source, target, chunk, expert_count, rounds)
        blocked = [target[0][:, None], remote_column(target, chunk, 0)[:, None], extra]
        return blocked, [source[0][None, :], table, arrived]

    def row(values):
        return values.astype(f32).reshape(1, -1)

    dp_index = lax.axis_index("dp")
    dp_count = lax.axis_size("dp")
    biases = jnp.concatenate([b_in, b_out], axis=1)
    for axis, bit in bits_of("dp"):
        got = swap(biases, axis, bit)
        upper = (dp_index // bit) % 2 == 1
        biases = jnp.where(
            upper, jnp.concatenate([got, biases]), jnp.concatenate([biases, got])
        )
    full_in = lax.all_gather(w_in[0], "dp", axis=0, tiled=True)
    full_out = lax.all_gather(w_out[0], "dp", axis=0, tiled=True)
    hidden_part = b_in.shape[1]
    full_bias_in = row(biases[:, :hidden_part])
    full_bias_out = row(biases[:, hidden_part:])

    arrived = start(block_input[0], slot_places)
    blocked, whole = sides(arrived, block_input[0], slot_places, token_places)
    tokens_in, normed_low, mixed_qkv = join(
        first_kernel,
        blocked,
        whole + [row(ln1_gain), row(ln1_bias), w_qkv],
        (model_width, model_width, 3 * model_width),
    )
    context_low, log_totals = attend(mixed_qkv)
    hidden = (tokens_in.astype(f32) + dot(context_low, w_o)).astype(bf16)
    arrived = start(hidden, token_places)
    live = occupied[:, None]
    grad_low = jnp.where(live, cotangent[0], jnp.zeros((), jnp.bfloat16))
    grad_act = dot_last(grad_low, full_out).astype(bf16)
    arrived, grad_act = lax.optimization_barrier((arrived, grad_act))
    blocked, whole = sides(arrived, hidden, token_places, slot_places)
    result, normed_two, act_low, grad_pre, grad_placed, sums_two, bias_sums = run_expert(
        blocked + [live.astype(jnp.int32), grad_low, grad_act],
        whole + [row(ln2_gain), row(ln2_bias), full_in, full_bias_in, full_out, full_bias_out],
        full_in.shape[0],
    )
    arrived = start(grad_placed, slot_places)
    local_w_in = dot_first(grad_pre, normed_two).astype(bf16)
    local_w_out = dot_first(act_low, grad_low).astype(bf16)
    arrived, local_w_in, local_w_out = lax.optimization_barrier((arrived, local_w_in, local_w_out))
    grad_w_in = lax.psum_scatter(local_w_in, "dp", scatter_dimension=0, tiled=True).astype(f32)
    grad_w_out = lax.psum_scatter(local_w_out, "dp", scatter_dimension=0, tiled=True).astype(f32)
    blocked, whole = sides(arrived, grad_placed, slot_places, token_places)
    grad_hidden, grad_context = join(
        third_kernel, blocked, whole + [w_o], (model_width, model_width)
    )
    local_w_o = lax.dot_general(
        context_low, grad_hidden, contract_first, preferred_element_type=jnp.float32
    )
    grad_mixed = attend_back(mixed_qkv, context_low, grad_context, log_totals)
    grad_tokens, sums_one = back(grad_mixed, w_qkv, tokens_in, grad_hidden, row(ln1_gain))
    packed = pack(grad_tokens, token_places, chunk, expert_count)
    dense = jnp.concatenate(
        [dot_first(normed_low, grad_mixed[part]).astype(bf16) for part in range(3)]
        + [local_w_o.astype(bf16)]
    )
    norms = jnp.concatenate(
        [
            sums_one[:2],
            sums_two[:2],
            jnp.zeros((4, model_width), f32),
            bias_sums[0].reshape(-1, model_width),
            sums_two[2:3],
            jnp.zeros((3, model_width), f32),
        ]
    )
    summed, norms, bias_sums, arrived = finish(
        dense, norms, packed.reshape(expert_count, chunk, model_width), dp_count
    )
    blocked, whole = sides(
        arrived.reshape(-1, model_width), grad_tokens, token_places, slot_places
    )
    (grad_input,) = join(last_kernel, blocked, whole, (model_width,))
    grad_w_qkv = jnp.concatenate(
        [summed[part * model_width : (part + 1) * model_width] for part in range(3)], axis=1
    ).astype(f32)
    grad_w_o = summed[3 * model_width :].astype(f32)
    grad_ln1_gain, grad_ln1_bias, grad_ln2_gain, grad_ln2_bias = norms[:4]
    full_parts = bias_sums[:4].reshape(dp_count, -1)
    grad_b_in = lax.dynamic_index_in_dim(full_parts, dp_index, 0, keepdims=False)
    grad_b_out = lax.dynamic_index_in_dim(
        bias_sums[4].reshape(dp_count, -1), dp_index, 0, keepdims=False
    )
    return (
        result[None],
        grad_input[None],
        grad_ln1_gain,
        grad_ln1_bias,
        grad_w_qkv,
        grad_w_o,
        grad_ln2_gain,
        grad_ln2_bias,
        grad_w_in[None],
        grad_b_in[None],
        grad_w_out[None],
        grad_b_out[None],
    )


def solution(mesh):
    placed = (
        P("dp", "expert", None),
        P("dp", "expert"),
        P(),
        P(),
        P(),
        P(),
        P(),
        P(),
        P("expert", "dp", None),
        P("expert", "dp"),
        P("expert", "dp", None),
        P("expert", "dp"),
        P("dp", "expert", None),
    )
    return jax.shard_map(
        body,
        mesh=mesh,
        in_specs=placed,
        out_specs=(
            P("dp", "expert", None),
            P("dp", "expert", None),
            P(),
            P(),
            P(),
            P(),
            P(),
            P(),
            P("expert", "dp", None),
            P("expert", "dp"),
            P("expert", "dp", None),
            P("expert", "dp"),
        ),
        check_vma=False,
    )
```

```python
import functools

import jax
import jax.numpy as jnp
from jax import lax
from jax.experimental import pallas as pl
from jax.experimental.pallas import tpu as pltpu
from jax.sharding import PartitionSpec as P

HEADS = 16
HEAD_DIM = 64


epsilon = 1e-05
gelu_c = 0.7978845608028654
contract_last = (((1,), (1,)), ((), ()))
contract_first = (((0,), (0,)), ((), ()))


bf16 = jnp.bfloat16
PAIR = 2 * HEAD_DIM
BIG_VMEM = 48 << 20
f32 = jnp.float32


def dot(left, right):
    return jnp.dot(left, right, preferred_element_type=f32)


def dot_last(left, right):
    return lax.dot_general(left, right, contract_last, preferred_element_type=f32)


def dot_first(left, right):
    return lax.dot_general(left, right, contract_first, preferred_element_type=f32)


def head_parts(pair):
    first = lax.broadcasted_iota(jnp.int32, (1, PAIR), 1) < HEAD_DIM
    zero = jnp.zeros_like(pair)
    return [jnp.where(first, pair, zero), jnp.where(first, zero, pair)]


def attend_kernel(block, q_ref, k_ref, v_ref, context_ref, logs_ref):
    length = q_ref.shape[0]
    keys = head_parts(k_ref[...])
    values_t = v_ref[...].T
    rows = lax.broadcasted_iota(jnp.int32, (block, block), 0)
    cols = lax.broadcasted_iota(jnp.int32, (block, block), 1)
    allowed = rows <= cols
    for low in range(0, length, block):
        high = low + block
        queries = q_ref[low:high, :] * jnp.asarray(0.125, bf16)
        outputs = []
        for head in range(2):
            value_rows = values_t[head * HEAD_DIM : (head + 1) * HEAD_DIM]
            near = jnp.where(allowed, dot_last(keys[head][low:high], queries), -1e30)
            peak = jnp.max(near, axis=0, keepdims=True)
            if low:
                far = dot_last(keys[head][:low], queries)
                peak = jnp.maximum(peak, jnp.max(far, axis=0, keepdims=True))
            near = jnp.exp(near - peak)
            total = jnp.sum(near, axis=0, keepdims=True)
            result = dot(value_rows[:, low:high], near.astype(bf16))
            if low:
                far = jnp.exp(far - peak)
                total = total + jnp.sum(far, axis=0, keepdims=True)
                result = result + dot(value_rows[:, :low], far.astype(bf16))
            outputs.append(result / total)
            logs_ref[0, head : head + 1, low:high] = peak + jnp.log(total)
        context_ref[low:high, :] = jnp.concatenate(outputs, axis=0).T.astype(bf16)


def pair_columns(length, offset):
    return pl.BlockSpec((length, PAIR), lambda pair: (0, offset + pair))


def pair_logs(length):
    return pl.BlockSpec((1, 8, length), lambda pair: (pair, 0, 0))


def attend(mixed):
    length, width = mixed.shape[0], mixed.shape[1] // 3
    pairs = width // PAIR
    return pl.pallas_call(
        functools.partial(attend_kernel, min(512, length)),
        grid=(pairs,),
        in_specs=[pair_columns(length, part * pairs) for part in range(3)],
        out_specs=[pair_columns(length, 0), pair_logs(length)],
        out_shape=[
            jax.ShapeDtypeStruct((length, width), bf16),
            jax.ShapeDtypeStruct((pairs, 8, length), f32),
        ],
        compiler_params=pltpu.CompilerParams(vmem_limit_bytes=BIG_VMEM),
        cost_estimate=pl.CostEstimate(
            flops=4 * length * length * width,
            bytes_accessed=8 * length * width,
            transcendentals=length * length * width // HEAD_DIM,
        ),
    )(mixed, mixed, mixed)


def attend_back_pair(
    block, q_ref, k_ref, v_ref, context_ref, grad_ref, logs_ref, out_ref, grad_k, grad_v
):
    length = q_ref.shape[0]
    keys, values, grads = k_ref[...], v_ref[...], grad_ref[...]
    queries = head_parts(q_ref[...] * jnp.asarray(0.125, bf16))
    key_parts = head_parts(keys)
    grad_parts = head_parts(grads)
    products = head_parts(grads.astype(f32) * context_ref[...].astype(f32))
    centres = [jnp.sum(part, axis=1, keepdims=True) for part in products]
    logs = logs_ref[0].T
    rows = lax.broadcasted_iota(jnp.int32, (block, block), 0)
    cols = lax.broadcasted_iota(jnp.int32, (block, block), 1)
    allowed = cols <= rows
    for low in reversed(range(0, length, block)):
        high = low + block
        add_q, add_k, add_v = [], [], []
        for head in range(2):
            scores = dot_last(queries[head][low:high], keys[:high])
            probs = jnp.exp(scores - logs[low:high, head : head + 1])
            near = jnp.where(allowed, probs[:, low:], 0.0)
            probs = jnp.concatenate([probs[:, :low], near], axis=1) if low else near
            grad_probs = dot_last(grad_parts[head][low:high], values[:high])
            grad_scores = (probs * (grad_probs - centres[head][low:high])).astype(bf16)
            add_q.append(dot(grad_scores, key_parts[head][:high]))
            add_k.append(dot_first(grad_scores, queries[head][low:high]))
            add_v.append(dot_first(probs.astype(bf16), grad_parts[head][low:high]))
        out_ref[low:high, :PAIR] = ((add_q[0] + add_q[1]) * 0.125).astype(bf16)
        if high == length:
            grad_k[...] = add_k[0] + add_k[1]
            grad_v[...] = add_v[0] + add_v[1]
        else:
            grad_k[:high, :] += add_k[0] + add_k[1]
            grad_v[:high, :] += add_v[0] + add_v[1]
    out_ref[:, PAIR : 2 * PAIR] = grad_k[...].astype(bf16)
    out_ref[:, 2 * PAIR :] = grad_v[...].astype(bf16)


def attend_back_kernel(block, *refs):
    out_ref, pair_grad, grad_k, grad_v = refs[6:]
    attend_back_pair(block, *refs[:6], pair_grad, grad_k, grad_v)
    for part in range(3):
        out_ref[part] = pair_grad[:, part * PAIR : (part + 1) * PAIR]


def attend_back(mixed, context, grad_context, logs):
    length, width = context.shape
    pairs = width // PAIR
    return pl.pallas_call(
        functools.partial(attend_back_kernel, min(256, length)),
        grid=(pairs,),
        in_specs=[pair_columns(length, part * pairs) for part in range(3)]
        + [pair_columns(length, 0)] * 2
        + [pair_logs(length)],
        out_specs=pl.BlockSpec((3, length, PAIR), lambda pair: (0, 0, pair)),
        out_shape=jax.ShapeDtypeStruct((3, length, width), bf16),
        scratch_shapes=[pltpu.VMEM((length, 3 * PAIR), bf16)]
        + [pltpu.VMEM((length, PAIR), f32)] * 2,
        compiler_params=pltpu.CompilerParams(vmem_limit_bytes=BIG_VMEM),
        cost_estimate=pl.CostEstimate(
            flops=10 * length * length * width,
            bytes_accessed=16 * length * width,
            transcendentals=length * length * width // HEAD_DIM,
        ),
    )(mixed, mixed, mixed, context, grad_context, logs)


def place_rows(columns, count, table):
    chosen = (columns[None, :] == jnp.arange(count, dtype=jnp.int32)[:, None]).astype(bf16)
    return dot(chosen, table).astype(bf16)


def exchange(packed, expert_count):
    return lax.all_to_all(
        packed.reshape(expert_count, -1, packed.shape[-1]),
        "expert",
        split_axis=0,
        concat_axis=0,
        tiled=True,
    ).reshape(-1, packed.shape[-1])


def remote_column(places, chunk, step):
    device, rank = places[1:]
    return jnp.where(rank // chunk == step, device * chunk + rank % chunk, -1)


def pack(table, places, chunk, expert_count, step=0):
    return place_rows(remote_column(places, chunk, step), expert_count * chunk, table)


def more_rounds(kept, table, source, target, chunk, expert_count, rounds):
    def again(state):
        step, sums = state
        packed = pack(table, source, chunk, expert_count, step)
        got = select_rows(remote_column(target, chunk, step), exchange(packed, expert_count))
        return (step + 1, sums + got)

    return lax.while_loop(lambda state: state[0] < rounds, again, (jnp.int32(1), kept))[1]


def select_rows(columns, table):
    chosen = (columns[:, None] == jnp.arange(table.shape[0], dtype=jnp.int32)[None, :]).astype(bf16)
    return dot(chosen, table).astype(bf16)


def swap(values, axis, bit):
    size = lax.axis_size(axis)
    return lax.ppermute(values, axis, [(i, i ^ bit) for i in range(size)])


def bits_of(axis, size=None):
    size = size or lax.axis_size(axis)
    return [(axis, 1 << k) for k in range(size.bit_length() - 1)]


def peer_index(axis, bit):
    own = lax.axis_index(axis)
    side = (own // bit) % 2
    return side, own + bit * (1 - 2 * side)


def greet(peers):
    barrier = pltpu.get_barrier_semaphore()
    for axis, index in peers:
        pl.semaphore_signal(
            barrier, inc=1, device_id={axis: index}, device_id_type=pl.DeviceIdType.MESH
        )
    pl.semaphore_wait(barrier, len(peers))


def ring_peers(count):
    own = lax.axis_index("expert")
    return [lax.rem(own + step, count) for step in range(1, count)]


def remote(source, target, send_sem, recv_sem, axis, index):
    return pltpu.make_async_remote_copy(
        src_ref=source,
        dst_ref=target,
        send_sem=send_sem,
        recv_sem=recv_sem,
        device_id={axis: index},
        device_id_type=pl.DeviceIdType.MESH,
    )


def rows_of(offset, size):
    return pl.ds(pl.multiple_of(offset, 16), size)


def plan_orders(dp_count, expert_count, rows, width):
    dp_bits, expert_bits = bits_of("dp", dp_count), bits_of("expert", expert_count)
    across, along = dp_bits[1:], expert_bits
    y_bits = along[: max(1, len(along) // 2)]
    z_bits = along[len(y_bits) :]
    if expert_count == 8:
        y_bits, z_bits = along[:1], along[1:]
    orders = (across + y_bits + z_bits, y_bits + across + z_bits)
    steps = len(orders[0])
    short = tuple(order[: steps - len(z_bits)] for order in orders)
    chunks = max(1, rows // (4 * 16 << steps))
    return dp_bits[0], orders, chunks, short, [bit for _, bit in z_bits]


def finish_kernel(
    first, orders, chunks, count, dense_ref, norm_ref, packed_ref, sum_ref, norm_out, bias_out, arrived_ref,
    work, done, *scratch
):
    steps = len(orders[0])
    core_slots = scratch[0]
    part_slots = scratch[1 : 1 + steps]
    norm_work, norm_slots = scratch[1 + steps : 3 + steps]
    core_send, core_recv, part_send, part_recv, norm_send, norm_recv = scratch[3 + steps : 9 + steps]
    swap_send, swap_recv, local_sem = scratch[9 + steps :]
    rows = work.shape[0] // chunks
    half, quarter = rows // 2, rows // 4
    own = lax.axis_index("expert")
    others = ring_peers(count)
    links = [first] + list(orders[0])
    dp_peers = [(axis, peer_index(axis, bit)[1]) for axis, bit in links if axis == "dp"]
    greet([("expert", index) for index in others] + dp_peers)

    swaps = []
    import os
    for step, index in enumerate(others):
        copy = remote(packed_ref.at[index], arrived_ref.at[own], swap_send.at[step], swap_recv.at[step], "expert", index)
        copy.start()
        swaps.append(copy)
    home = pltpu.make_async_copy(packed_ref.at[own], arrived_ref.at[own], local_sem.at[chunks])
    home.start()

    side0, peer0 = peer_index(*first)
    started = []
    norm_work[...] = norm_ref[...]

    def add_rows(offset, size, slot, target):
        block = min(size, 64)

        @pl.loop(0, size // block)
        def _(index):
            here = rows_of(offset + index * block, block)
            there = rows_of(index * block, block)
            target[here, :] = (work[here, :].astype(f32) + slot[there, :].astype(f32)).astype(bf16)

    state = {}

    def event(chunk, number):
        base = chunk * rows
        if number == 0:
            kept = base + side0 * half
            given = base + (1 - side0) * half
            load = pltpu.make_async_copy(dense_ref.at[rows_of(kept, half)], work.at[rows_of(kept, half)], local_sem.at[chunk])
            load.start()
            copy = remote(dense_ref.at[rows_of(given, half)], core_slots.at[chunk], core_send.at[chunk, 0], core_recv.at[chunk, 0], first[0], peer0)
            copy.start()
            started.append(copy)
            state[chunk] = dict(kept=kept, load=load, copy=copy)
        elif number <= 2 * steps + 1:
            for part in range(2):
                go_on(chunk, part, number - 1)
        if number == 2 * steps + 1:
            kept = state[chunk]["kept"]
            copy = remote(done.at[rows_of(kept, half)], done.at[rows_of(kept, half)], core_send.at[chunk, 1], core_recv.at[chunk, 1], first[0], peer0)
            copy.start()
            started.append(copy)
            state[chunk]["copy"] = copy
        if number == 2 * steps + 2:
            state[chunk]["copy"].wait_recv()
            store = pltpu.make_async_copy(done.at[pl.ds(base, rows)], sum_ref.at[pl.ds(base, rows)], local_sem.at[chunk])
            store.start()
            state[chunk]["store"] = store

    def go_on(chunk, part, step):
        here = state[chunk]
        if step == 0:
            if part == 0:
                here["load"].wait()
                here["copy"].wait_recv()
                add_rows(here["kept"], half, core_slots.at[chunk], work)
            offset = here["kept"] + part * quarter
        else:
            offset, size, copy, slot = here[part]
            copy.wait_recv()
            if step <= steps:
                add_rows(offset, size, slot, work if step < steps else done)
        if step < steps:
            axis, bit = orders[part][step]
            side, peer = peer_index(axis, bit)
            size = quarter >> (step + 1)
            slot = part_slots[step].at[chunk, part]
            given = offset + (1 - side) * size
            kept = offset + side * size
            copy = remote(work.at[rows_of(given, size)], slot, part_send.at[chunk, part, step], part_recv.at[chunk, part, step], axis, peer)
            copy.start()
            started.append(copy)
            here[part] = (kept, size, copy, slot)
        elif step < 2 * steps:
            back = 2 * steps - 1 - step
            axis, bit = orders[part][back]
            side, peer = peer_index(axis, bit)
            size = quarter >> (back + 1)
            if step > steps:
                offset = offset - here["side", part] * (size // 2)
            here["side", part] = side
            copy = remote(done.at[rows_of(offset, size)], done.at[rows_of(offset, size)], part_send.at[chunk, part, step], part_recv.at[chunk, part, step], axis, peer)
            copy.start()
            started.append(copy)
            here[part] = (offset, size, copy, None)

    norm_copy = None
    for tick in range(2 * steps + 2 + chunks):
        for chunk in range(chunks):
            number = tick - chunk
            if 0 <= number <= 2 * steps + 2:
                event(chunk, number)
        if tick <= len(links):
            if norm_copy is not None:
                norm_copy.wait()
                norm_work[...] += norm_slots[tick - 1]
                if tick == sum(axis == "dp" for axis, _ in links):
                    bias_out[...] = norm_work[8:16, :]
            if tick < len(links):
                axis, bit = links[tick]
                norm_copy = remote(norm_work, norm_slots.at[tick], norm_send.at[tick], norm_recv.at[tick], axis, peer_index(axis, bit)[1])
                norm_copy.start()
            else:
                norm_out[...] = norm_work[...]
    for copy in started:
        copy.wait_send()
    for copy in swaps:
        copy.wait()
    home.wait()
    for chunk in range(chunks):
        state[chunk]["store"].wait()


def finish(dense, norms, packed, dp_count):
    count = packed.shape[0]
    rows, width = dense.shape
    first, orders, chunks, _, _ = plan_orders(dp_count, count, rows, width)
    steps = len(orders[0])
    part = rows // chunks // 4
    return pl.pallas_call(
        functools.partial(finish_kernel, first, orders, chunks, count),
        in_specs=[
            pl.BlockSpec(memory_space=pl.ANY),
            pl.BlockSpec(memory_space=pltpu.VMEM),
            pl.BlockSpec(memory_space=pl.ANY),
        ],
        out_specs=[
            pl.BlockSpec(memory_space=pl.ANY),
            pl.BlockSpec(memory_space=pltpu.VMEM),
            pl.BlockSpec(memory_space=pltpu.VMEM),
            pl.BlockSpec(memory_space=pl.ANY),
        ],
        out_shape=[
            jax.ShapeDtypeStruct(dense.shape, bf16),
            jax.ShapeDtypeStruct(norms.shape, f32),
            jax.ShapeDtypeStruct((8, width), f32),
            jax.ShapeDtypeStruct(packed.shape, bf16),
        ],
        scratch_shapes=[pltpu.VMEM(dense.shape, bf16)] * 2 + [pltpu.VMEM((chunks, 2 * part, width), bf16)]
        + [pltpu.VMEM((chunks, 2, part >> (step + 1), width), bf16) for step in range(steps)]
        + [
            pltpu.VMEM(norms.shape, f32),
            pltpu.VMEM((steps + 1,) + norms.shape, f32),
            pltpu.SemaphoreType.DMA((chunks, 2)),
            pltpu.SemaphoreType.DMA((chunks, 2)),
            pltpu.SemaphoreType.DMA((chunks, 2, 2 * steps)),
            pltpu.SemaphoreType.DMA((chunks, 2, 2 * steps)),
            pltpu.SemaphoreType.DMA((steps + 1,)),
            pltpu.SemaphoreType.DMA((steps + 1,)),
            pltpu.SemaphoreType.DMA((count - 1,)),
            pltpu.SemaphoreType.DMA((count - 1,)),
            pltpu.SemaphoreType.DMA((chunks + 1,)),
        ],
        compiler_params=pltpu.CompilerParams(
            collective_id=7, has_side_effects=True, vmem_limit_bytes=BIG_VMEM
        ),
        cost_estimate=pl.CostEstimate(
            flops=2 * rows * width, bytes_accessed=8 * rows * width, transcendentals=0
        ),
    )(dense, norms, packed)


def pick(columns, numbers, table):
    return dot((columns == numbers).astype(bf16), table)


def joined_rows(far, kept, arrived):
    places = lax.broadcasted_iota(jnp.int32, (1, arrived.shape[0]), 1)
    return pick(far[...], places, arrived[...]) + kept[...].astype(f32)


def near_kernel(near, numbers, table, rows_ref):
    rows_ref[...] = pick(near[...], numbers[...], table[...]).astype(bf16)


def norm_parts(rows):
    centre = jnp.mean(rows, axis=-1, keepdims=True)
    centred = rows - centre
    inverse = lax.rsqrt(jnp.mean(centred * centred, axis=-1, keepdims=True) + epsilon)
    return centred * inverse, inverse


def norm_back(grad, scaled, inverse, gains):
    grad_scaled = grad * gains
    first = jnp.mean(grad_scaled, axis=-1, keepdims=True)
    second = jnp.mean(grad_scaled * scaled, axis=-1, keepdims=True)
    return inverse * (grad_scaled - first - scaled * second)


def first_kernel(far, kept, arrived, gain, bias, weight, rows_ref, normed_ref, mixed_ref, turned_ref):
    rows = joined_rows(far, kept, arrived)
    rows_ref[...] = rows.astype(bf16)
    normed = (norm_parts(rows)[0] * gain[...] + bias[...]).astype(bf16)
    normed_ref[...] = normed
    turned_ref[...] = normed.T
    mixed_ref[...] = dot(normed, weight[...]).astype(bf16)


def third_kernel(far, kept, arrived, weight, rows_ref, product_ref):
    rows = joined_rows(far, kept, arrived).astype(bf16)
    rows_ref[...] = rows
    product_ref[...] = dot_last(rows, weight[...]).astype(bf16)


def last_kernel(far, kept, arrived, rows_ref):
    rows_ref[...] = joined_rows(far, kept, arrived).astype(bf16)


def block_rows(width):
    return pl.BlockSpec((256, width), lambda step: (step, 0))


def in_full(array):
    return pl.BlockSpec(array.shape, lambda step: (0,) * array.ndim, pipeline_mode=pl.Buffered(1))


def join(kernel, blocked, whole, widths, turned=()):
    count = blocked[0].shape[0]
    table = next(array for array in whole if array.dtype == bf16)
    inside, width = table.shape
    return pl.pallas_call(
        kernel,
        grid=(count // 256,),
        in_specs=[block_rows(array.shape[1]) for array in blocked]
        + [in_full(array) for array in whole],
        out_specs=[block_rows(size) for size in widths]
        + [pl.BlockSpec((size, 256), lambda step: (0, step)) for size in turned],
        out_shape=[jax.ShapeDtypeStruct((count, size), bf16) for size in widths]
        + [jax.ShapeDtypeStruct((size, count), bf16) for size in turned],
        compiler_params=pltpu.CompilerParams(vmem_limit_bytes=BIG_VMEM),
        cost_estimate=pl.CostEstimate(
            flops=2 * count * width * (inside + sum(widths) - width),
            bytes_accessed=2 * (inside * width + count * sum(widths)),
            transcendentals=0,
        ),
    )(*blocked, *whole)


def expert_kernel(
    far, kept, live, grad_y, grad_act, arrived, gain, bias,
    weight_in, bias_in, weight_out, bias_out,
    out_ref, normed_ref, act_ref, grad_pre_ref, grad_ref, sum_ref, bias_sum_ref,
):
    rows = joined_rows(far, kept, arrived)
    scaled, inverse = norm_parts(rows)
    normed = (scaled * gain[...] + bias[...]).astype(bf16)
    normed_ref[...] = normed
    hidden = weight_in.shape[0]
    block = min(1024, hidden)

    @pl.when(pl.program_id(0) == 0)
    def _():
        sum_ref[...] = jnp.zeros_like(sum_ref)
        bias_sum_ref[...] = jnp.zeros_like(bias_sum_ref)

    result = jnp.zeros(rows.shape, f32)
    grad = jnp.zeros(rows.shape, f32)
    for low in range(0, hidden, block):
        part = slice(low, low + block)
        pre = dot_last(normed, weight_in[part, :]) + bias_in[:, part]
        square = pre * pre
        tangent = jnp.tanh(gelu_c * (pre + 0.044715 * pre * square))
        half = 0.5 * pre
        act = (half + half * tangent).astype(bf16)
        slope = (0.5 + 0.5 * tangent) + half * (1.0 - tangent * tangent) * (
            gelu_c + (3.0 * 0.044715 * gelu_c) * square
        )
        grad_pre_f = grad_act[:, part].astype(f32) * slope
        grad_pre = grad_pre_f.astype(bf16)
        act_ref[:, part] = act
        grad_pre_ref[:, part] = grad_pre
        bias_sum_ref[0:1, part] += jnp.sum(grad_pre.astype(f32), axis=0, keepdims=True)
        result += dot(act, weight_out[part, :])
        grad += dot(grad_pre, weight_in[part, :])
    out = rows + result + bias_out[...]
    out_ref[...] = jnp.where(live[...] > 0, out, 0.0).astype(bf16)
    grad_in = grad_y[...].astype(f32)
    grad_ref[...] = (grad_in + norm_back(grad, scaled, inverse, gain[...])).astype(bf16)
    sum_ref[0:1, :] += jnp.sum(grad * scaled, axis=0, keepdims=True)
    sum_ref[1:2, :] += jnp.sum(grad, axis=0, keepdims=True)
    sum_ref[2:3, :] += jnp.sum(grad_in, axis=0, keepdims=True)


def run_expert(blocked, whole, hidden):
    count, width = blocked[1].shape
    widths = (width, width, hidden, hidden, width)

    def sums(size):
        return pl.BlockSpec((8, size), lambda step: (0, 0))

    return pl.pallas_call(
        expert_kernel,
        grid=(count // 256,),
        in_specs=[block_rows(array.shape[1]) for array in blocked]
        + [in_full(array) for array in whole],
        out_specs=[block_rows(size) for size in widths] + [sums(width), sums(hidden)],
        out_shape=[jax.ShapeDtypeStruct((count, size), bf16) for size in widths]
        + [jax.ShapeDtypeStruct((8, width), f32), jax.ShapeDtypeStruct((8, hidden), f32)],
        compiler_params=pltpu.CompilerParams(vmem_limit_bytes=58 << 20),
        cost_estimate=pl.CostEstimate(
            flops=6 * count * width * hidden,
            bytes_accessed=2 * count * (5 * width + 3 * hidden) + 4 * width * hidden,
            transcendentals=count * hidden,
        ),
    )(*blocked, *whole)


def backward_kernel(
    first, orders, along, count, pairs,
    q_ref, k_ref, v_ref, context_ref, grad_ref, logs_ref, wq_ref, wk_ref, wv_ref, dense_ref,
    normed_t, tokens_ref, hidden_ref, gain_ref, norm_ref, send_numbers, near_column, near_numbers,
    mixed_sum, dense_sum, norm_out, bias_out, arrived_ref, near_ref, tokens_grad,
    work, done, core_slots, *scratch
):
    steps = len(orders[0])
    part_slots = scratch[:steps]
    (
        along_slots, pair_grad, grad_k, grad_v, total, packed, norm_work, norm_slots,
        core_send, core_recv, part_send, part_recv, along_send, along_recv,
        norm_send, norm_recv, swap_send, swap_recv, local_sem,
    ) = scratch[steps:]
    tick = pl.program_id(0)
    rows, width = work.shape[1], pairs * PAIR
    half, quarter = rows // 2, rows // 4
    own = lax.axis_index("expert")
    others = ring_peers(count)
    links = [first] + list(orders[0]) + [("expert", bit) for bit in along]
    link_peers = [(axis, peer_index(axis, bit)[1]) for axis, bit in links]
    events = 2 * steps + 4
    last = pairs + events // 2 - 1

    @pl.when(tick == 0)
    def _():
        greet([("expert", index) for index in others] + [peer for peer in link_peers if peer[0] == "dp"])

    side0, peer0 = peer_index(*first)
    offsets, sides, peers = [], [], []
    for part in range(2):
        offset = side0 * half + part * quarter
        at, side_list, peer_list = [offset], [], []
        for step, (axis, bit) in enumerate(orders[part]):
            side, peer = peer_index(axis, bit)
            offset = offset + side * (quarter >> (step + 1))
            at.append(offset)
            side_list.append(side)
            peer_list.append((axis, peer))
        offsets.append(at)
        sides.append(side_list)
        peers.append(peer_list)
    spread = 1 << len(along)
    place = (own // along[0]) % spread
    piece = quarter >> steps >> len(along)

    def core_give(chunk):
        given = rows_of((1 - side0) * half, half)
        return remote(work.at[chunk, given], core_slots.at[chunk], core_send.at[chunk, 0], core_recv.at[chunk, 0], first[0], peer0)

    def core_return(chunk):
        kept = rows_of(side0 * half, half)
        return remote(done.at[chunk, kept], done.at[chunk, kept], core_send.at[chunk, 1], core_recv.at[chunk, 1], first[0], peer0)

    def part_give(chunk, part, step):
        size = quarter >> (step + 1)
        given = rows_of(offsets[part][step] + (1 - sides[part][step]) * size, size)
        return remote(
            work.at[chunk, given], part_slots[step].at[chunk, part],
            part_send.at[chunk, part, step], part_recv.at[chunk, part, step], *peers[part][step]
        )

    def part_return(chunk, part, step):
        kept = rows_of(offsets[part][step + 1], quarter >> (step + 1))
        return remote(
            done.at[chunk, kept], done.at[chunk, kept],
            part_send.at[chunk, part, steps + step], part_recv.at[chunk, part, steps + step], *peers[part][step]
        )

    def along_copies(chunk, part, back):
        copies = []
        for turn in range(1, spread):
            there = lax.rem(place + turn, spread)
            index = turn - 1 + back * (spread - 1)
            if back:
                source = target = done.at[chunk, rows_of(offsets[part][steps] + place * piece, piece)]
            else:
                source = work.at[chunk, rows_of(offsets[part][steps] + there * piece, piece)]
                target = along_slots.at[chunk, part, turn - 1]
            copies.append(
                remote(
                    source, target, along_send.at[chunk, part, index], along_recv.at[chunk, part, index],
                    "expert", own + (there - place) * along[0]
                )
            )
        return copies

    def store(chunk):
        for part in range(4):
            source = done.at[chunk, :, part * PAIR : (part + 1) * PAIR]
            column = pl.ds(pl.multiple_of(chunk * PAIR + (part % 3) * width, PAIR), PAIR)
            target = mixed_sum if part < 3 else dense_sum
            yield pltpu.make_async_copy(source, target.at[:, column], local_sem.at[chunk, part])

    def add_rows(chunk, offset, size, slots, target):
        block = min(size, 64)

        @pl.loop(0, size // block)
        def _(index):
            here = rows_of(offset + index * block, block)
            there = rows_of(index * block, block)
            sums = work[chunk, here, :].astype(f32)
            for slot in slots:
                sums = sums + slot[there, :].astype(f32)
            target[chunk, here, :] = sums.astype(bf16)

    def event(chunk, number):
        if number == 1:
            core_give(chunk).wait_recv()
            add_rows(chunk, side0 * half, half, [core_slots.at[chunk]], work)
        for part in range(2):
            if 2 <= number <= steps + 1:
                step = number - 2
                part_give(chunk, part, step).wait_recv()
                add_rows(
                    chunk, offsets[part][step + 1], quarter >> (step + 1), [part_slots[step].at[chunk, part]], work
                )
            if number <= steps:
                part_give(chunk, part, number - 1).start()
            elif number == steps + 1:
                for copy in along_copies(chunk, part, 0):
                    copy.start()
            elif number == steps + 2:
                for copy in along_copies(chunk, part, 0):
                    copy.wait_recv()
                slots = [along_slots.at[chunk, part, turn] for turn in range(spread - 1)]
                add_rows(chunk, offsets[part][steps] + place * piece, piece, slots, done)
                for copy in along_copies(chunk, part, 1):
                    copy.start()
            elif number <= 2 * steps + 3:
                back = 2 * steps + 2 - number
                if back == steps - 1:
                    for copy in along_copies(chunk, part, 1):
                        copy.wait_recv()
                else:
                    part_return(chunk, part, back + 1).wait_recv()
                if back >= 0:
                    part_return(chunk, part, back).start()
        if number == 2 * steps + 3:
            core_return(chunk).start()
        if number == 2 * steps + 4:
            core_return(chunk).wait_recv()
            for copy in store(chunk):
                copy.start()

    def norm_step(step):
        return remote(norm_work.at[step], norm_slots.at[step], norm_send.at[step], norm_recv.at[step], *link_peers[step])

    def norm_event(step):
        norm_step(step).wait_recv()
        summed = norm_work[step] + norm_slots[step]
        if step + 1 < len(links):
            norm_work[step + 1] = summed
            norm_step(step + 1).start()
        else:
            norm_out[...] = summed
        if step + 1 == sum(axis == "dp" for axis, _ in links):
            bias_out[...] = summed[8:16]

    def run_events(side):
        for number in range(events, 0, -1):
            if (number + 1) % 2 == side:
                chunk = tick - (1 + number) // 2

                @pl.when((chunk >= 0) & (chunk < pairs))
                def _(number=number, chunk=chunk):
                    event(chunk, number)

        for step in range(len(links)):
            if step % 2 == side:

                @pl.when(tick == pairs + 1 + step // 2)
                def _(step=step):
                    norm_event(step)

    run_events(0)

    @pl.when(tick < pairs)
    def _():
        attend_back_pair(
            min(256, rows), q_ref, k_ref, v_ref, context_ref, grad_ref, logs_ref,
            pair_grad, grad_k, grad_v,
        )
        run_events(1)
        work[tick, :, : 3 * PAIR] = dot(normed_t[...], pair_grad[...]).astype(bf16)
        work[tick, :, 3 * PAIR :] = dense_ref[...]
        core_give(tick).start()
        weights = jnp.concatenate([wq_ref[...], wk_ref[...], wv_ref[...]], axis=1)

        @pl.when(tick == 0)
        def _():
            total[...] = dot_last(pair_grad[...], weights)

        @pl.when(tick > 0)
        def _():
            total[...] += dot_last(pair_grad[...], weights)

    quarter_rows = packed.shape[1] // 4

    def swap_rows(step, piece):
        index = others[step]
        here = pl.ds(piece * quarter_rows, quarter_rows)
        return remote(
            packed.at[index, here], arrived_ref.at[own, here],
            swap_send.at[step, piece], swap_recv.at[step, piece], "expert", index
        )

    def start_swaps(pieces):
        for piece in pieces:
            for step in range(count - 1):
                swap_rows(step, piece).start()

    def home_rows():
        return pltpu.make_async_copy(packed.at[own], arrived_ref.at[own], local_sem.at[pairs, 0])

    @pl.when(tick == pairs)
    def _():
        sums = [jnp.zeros((1, width), f32)] * 2
        for low in range(0, rows, 256):
            part = slice(low, low + 256)
            grad = total[part, :]
            scaled, inverse = norm_parts(tokens_ref[part, :].astype(f32))
            result = hidden_ref[part, :].astype(f32) + norm_back(grad, scaled, inverse, gain_ref[...])
            tokens_grad[part, :] = result.astype(bf16)
            sums[0] = sums[0] + jnp.sum(grad * scaled, axis=0, keepdims=True)
            sums[1] = sums[1] + jnp.sum(grad, axis=0, keepdims=True)
        norm_work[0] = norm_ref[...]
        norm_work[0, 0:1, :] = sums[0]
        norm_work[0, 1:2, :] = sums[1]
        norm_step(0).start()
        chunk = packed.shape[1]
        for index in range(count):
            numbers = index * chunk + lax.broadcasted_iota(jnp.int32, (chunk, 1), 0)
            packed[index] = dot((send_numbers[...] == numbers).astype(bf16), tokens_grad[...]).astype(bf16)
        start_swaps([0])
        home_rows().start()

    @pl.when(tick == pairs + 2)
    def _():
        start_swaps([2, 3])

    @pl.when(tick >= pairs)
    def _():
        run_events(1)

    @pl.when(tick == pairs + 1)
    def _():
        start_swaps([1])

    @pl.when(tick == pairs + 2)
    def _():
        for low in range(0, near_ref.shape[0], 256):
            part = slice(low, low + 256)
            near_ref[part, :] = pick(near_column[part, :], near_numbers[...], tokens_grad[...]).astype(bf16)

    @pl.when(tick == last)
    def _():
        @pl.loop(0, pairs)
        def _(chunk):
            core_give(chunk).wait_send()
            core_return(chunk).wait_send()
            for part in range(2):
                for step in range(steps):
                    part_give(chunk, part, step).wait_send()
                    part_return(chunk, part, step).wait_send()
                for back in range(2):
                    for copy in along_copies(chunk, part, back):
                        copy.wait_send()
            for copy in store(chunk):
                copy.wait()

        for step in range(len(links)):
            norm_step(step).wait_send()
        for piece in range(4):
            for step in range(count - 1):
                swap_rows(step, piece).wait()
        home_rows().wait()


def backward(mixed, context, grad_context, logs, weight, dense, normed_t, tokens, grad_hidden, gain, norms,
             send_numbers, near_column, near_numbers, first, orders, along, count, chunk):
    length, width = context.shape
    pairs = width // PAIR
    steps = len(orders[0])
    links = 1 + steps + len(along)
    part = length // 4
    slots = near_column.shape[0]
    spread = 1 << len(along)

    def columns(offset):
        return pl.BlockSpec((length, PAIR), lambda tick: (0, offset + jnp.minimum(tick, pairs - 1)))

    def whole(array):
        return pl.BlockSpec(array.shape, lambda tick: (0,) * array.ndim, pipeline_mode=pl.Buffered(1))

    def result(shape):
        return pl.BlockSpec(shape, lambda tick: (0,) * len(shape))

    anywhere = pl.BlockSpec(memory_space=pl.ANY)
    fixed = (normed_t, tokens, grad_hidden, gain, norms, send_numbers, near_column, near_numbers)
    dma = pltpu.SemaphoreType.DMA
    return pl.pallas_call(
        functools.partial(backward_kernel, first, orders, along, count, pairs),
        grid=(pairs + steps + 2,),
        in_specs=[columns(0), columns(pairs), columns(2 * pairs), columns(0), columns(0)]
        + [pl.BlockSpec((1, 8, length), lambda tick: (jnp.minimum(tick, pairs - 1), 0, 0))]
        + [columns(0), columns(pairs), columns(2 * pairs), columns(0)]
        + [whole(array) for array in fixed],
        out_specs=[
            anywhere, anywhere, result(norms.shape), result((8, width)), anywhere,
            result((slots, width)), result((length, width)),
        ],
        out_shape=[
            jax.ShapeDtypeStruct((length, 3 * width), bf16),
            jax.ShapeDtypeStruct((length, width), bf16),
            jax.ShapeDtypeStruct(norms.shape, f32),
            jax.ShapeDtypeStruct((8, width), f32),
            jax.ShapeDtypeStruct((count, chunk, width), bf16),
            jax.ShapeDtypeStruct((slots, width), bf16),
            jax.ShapeDtypeStruct((length, width), bf16),
        ],
        scratch_shapes=[pltpu.VMEM((pairs, length, 4 * PAIR), bf16)] * 2
        + [pltpu.VMEM((pairs, length // 2, 4 * PAIR), bf16)]
        + [pltpu.VMEM((pairs, 2, part >> (step + 1), 4 * PAIR), bf16) for step in range(steps)]
        + [
            pltpu.VMEM((pairs, 2, spread - 1, part >> steps >> len(along), 4 * PAIR), bf16),
            pltpu.VMEM((length, 3 * PAIR), bf16),
            pltpu.VMEM((length, PAIR), f32),
            pltpu.VMEM((length, PAIR), f32),
            pltpu.VMEM((length, width), f32),
            pltpu.VMEM((count, chunk, width), bf16),
            pltpu.VMEM((links,) + norms.shape, f32),
            pltpu.VMEM((links,) + norms.shape, f32),
            dma((pairs, 2)),
            dma((pairs, 2)),
            dma((pairs, 2, 2 * steps)),
            dma((pairs, 2, 2 * steps)),
            dma((pairs, 2, 2 * (spread - 1))),
            dma((pairs, 2, 2 * (spread - 1))),
            dma((links,)),
            dma((links,)),
            dma((count - 1, 4)),
            dma((count - 1, 4)),
            dma((pairs + 1, 4)),
        ],
        compiler_params=pltpu.CompilerParams(
            collective_id=7, has_side_effects=True, vmem_limit_bytes=61 << 20
        ),
        cost_estimate=pl.CostEstimate(
            flops=10 * length * length * width, bytes_accessed=32 * length * width,
            transcendentals=length * length * width // HEAD_DIM,
        ),
    )(mixed, mixed, mixed, context, grad_context, logs, weight, weight, weight, dense, *fixed)


def back_kernel(grad_ref, weight_ref, tokens_ref, hidden_ref, gain_ref, out_ref, sum_ref):
    width = gain_ref.shape[1]
    grad = sum(
        dot_last(grad_ref[part], weight_ref[:, part * width : (part + 1) * width])
        for part in range(3)
    )
    scaled, inverse = norm_parts(tokens_ref[...].astype(f32))
    result = hidden_ref[...].astype(f32) + norm_back(grad, scaled, inverse, gain_ref[...])
    out_ref[...] = result.astype(bf16)

    @pl.when(pl.program_id(0) == 0)
    def _():
        sum_ref[...] = jnp.zeros_like(sum_ref)

    sum_ref[0:1, :] += jnp.sum(grad * scaled, axis=0, keepdims=True)
    sum_ref[1:2, :] += jnp.sum(grad, axis=0, keepdims=True)


def back(grad_mixed, weight, tokens, grad_hidden, gain):
    count, width = tokens.shape
    block = 256

    def by_rows():
        return pl.BlockSpec((block, width), lambda step: (step, 0))

    return pl.pallas_call(
        back_kernel,
        grid=(count // block,),
        in_specs=[
            pl.BlockSpec((3, block, width), lambda step: (0, step, 0)),
            pl.BlockSpec(weight.shape, lambda step: (0, 0)),
            by_rows(),
            by_rows(),
            pl.BlockSpec((1, width), lambda step: (0, 0)),
        ],
        out_specs=[by_rows(), pl.BlockSpec((8, width), lambda step: (0, 0))],
        out_shape=[
            jax.ShapeDtypeStruct((count, width), bf16),
            jax.ShapeDtypeStruct((8, width), f32),
        ],
        compiler_params=pltpu.CompilerParams(vmem_limit_bytes=BIG_VMEM),
        cost_estimate=pl.CostEstimate(
            flops=6 * count * width * width, bytes_accessed=20 * count * width, transcendentals=0
        ),
    )(grad_mixed, weight, tokens, grad_hidden, gain)


def body(
    block_input,
    expert_ids,
    ln1_gain,
    ln1_bias,
    w_qkv,
    w_o,
    ln2_gain,
    ln2_bias,
    w_in,
    b_in,
    w_out,
    b_out,
    cotangent,
):
    expert_count = lax.axis_size("expert")
    own_expert = lax.axis_index("expert")
    slot_rows = block_input.shape[1]
    model_width = block_input.shape[2]
    seq_ids = expert_ids[0]
    seq_length = seq_ids.shape[0]
    capacity = 5 * seq_length // expert_count
    chunk = seq_length // expert_count
    group_ids = lax.all_to_all(
        jnp.broadcast_to(seq_ids[None], (expert_count, seq_length)),
        "expert",
        split_axis=0,
        concat_axis=0,
        tiled=True,
    )
    devices = jnp.arange(expert_count, dtype=jnp.int32)
    counts = jnp.sum(
        (group_ids[:, :, None] == devices[None, None, :]).astype(jnp.int32), axis=1
    )
    fullest = jnp.argmax(counts, axis=0).astype(jnp.int32)
    taken = jnp.sum((fullest[:, None] == devices[None, :]).astype(jnp.int32), axis=0)
    distinct = jnp.all(taken == 1)
    held_by = jnp.where(distinct, fullest, devices)
    owner = jnp.sum(
        (held_by[:, None] == devices[None, :]).astype(jnp.int32) * devices[:, None], axis=0
    )
    held = held_by[own_expert]
    most = jnp.max(jnp.where(owner[:, None] == devices[None, :], 0, counts))
    for axis, bit in bits_of("dp"):
        most = jnp.maximum(most, swap(most, axis, bit))
    rounds = (most + chunk - 1) // chunk
    from_each = counts[:, own_expert]
    ends_at = jnp.cumsum(from_each)
    starts_at = ends_at - from_each
    slot_index = jnp.arange(slot_rows, dtype=jnp.int32)
    passed = (ends_at[None, :] <= slot_index[:, None]).astype(jnp.int32)
    source = jnp.sum(passed, axis=1)
    occupied = slot_index < ends_at[-1]
    within = slot_index - jnp.sum(passed * from_each[None, :], axis=1)
    at_device = jnp.sum(
        (source[:, None] == devices[None, :]).astype(jnp.int32) * owner[None, :], axis=1
    )
    at_home = at_device == own_expert
    slot_places = (
        jnp.where(occupied & at_home, within, -2),
        at_device,
        jnp.where(occupied & ~at_home, within, -chunk),
    )
    held_ids = lax.dynamic_index_in_dim(group_ids, held, 0, keepdims=False)
    choose = (held_ids[:, None] == devices[None, :]).astype(jnp.int32)
    rank_in = jnp.sum((jnp.cumsum(choose, axis=0) - 1) * choose, axis=1)
    is_own = held_ids == own_expert
    token_places = (
        jnp.where(is_own, rank_in, -1),
        held_ids,
        jnp.where(is_own, -chunk, rank_in),
    )

    def start(table, places):
        return exchange(pack(table, places, chunk, expert_count), expert_count)

    def near_rows(table, source, target):
        (rows,) = join(
            near_kernel, [target[0][:, None]], [source[0][None, :], table], (model_width,)
        )
        return rows

    def sides(arrived, kept, table, source, target):
        kept = more_rounds(kept, table, source, target, chunk, expert_count, rounds)
        return [remote_column(target, chunk, 0)[:, None], kept]

    def row(values):
        return values.astype(f32).reshape(1, -1)

    dp_index = lax.axis_index("dp")
    dp_count = lax.axis_size("dp")
    biases = jnp.concatenate([b_in, b_out], axis=1)
    for axis, bit in bits_of("dp"):
        got = swap(biases, axis, bit)
        upper = (dp_index // bit) % 2 == 1
        biases = jnp.where(
            upper, jnp.concatenate([got, biases]), jnp.concatenate([biases, got])
        )
    full_in = lax.all_gather(w_in[0], "dp", axis=0, tiled=True)
    full_out = lax.all_gather(w_out[0], "dp", axis=0, tiled=True)
    hidden_part = b_in.shape[1]
    full_bias_in = row(biases[:, :hidden_part])
    full_bias_out = row(biases[:, hidden_part:])

    arrived = start(block_input[0], slot_places)
    near = near_rows(block_input[0], slot_places, token_places)
    arrived, near = lax.optimization_barrier((arrived, near))
    tokens_in, normed_low, mixed_qkv, normed_t = join(
        first_kernel,
        sides(arrived, near, block_input[0], slot_places, token_places),
        [arrived, row(ln1_gain), row(ln1_bias), w_qkv],
        (model_width, model_width, 3 * model_width),
        (model_width,),
    )
    context_low, log_totals = attend(mixed_qkv)
    hidden = (tokens_in.astype(f32) + dot(context_low, w_o)).astype(bf16)
    arrived = start(hidden, token_places)
    live = occupied[:, None]
    grad_low = jnp.where(live, cotangent[0], jnp.zeros((), jnp.bfloat16))
    grad_act = dot_last(grad_low, full_out).astype(bf16)
    near = near_rows(hidden, token_places, slot_places)
    arrived, grad_act, near = lax.optimization_barrier((arrived, grad_act, near))
    result, normed_two, act_low, grad_pre, grad_placed, sums_two, bias_sums = run_expert(
        sides(arrived, near, hidden, token_places, slot_places)
        + [live.astype(jnp.int32), grad_low, grad_act],
        [arrived, row(ln2_gain), row(ln2_bias), full_in, full_bias_in, full_out, full_bias_out],
        full_in.shape[0],
    )
    arrived = start(grad_placed, slot_places)
    local_w_in = dot_first(grad_pre, normed_two).astype(bf16)
    local_w_out = dot_first(act_low, grad_low).astype(bf16)
    near = near_rows(grad_placed, slot_places, token_places)
    arrived, near, local_w_in, local_w_out = lax.optimization_barrier(
        (arrived, near, local_w_in, local_w_out)
    )
    grad_w_in = lax.psum_scatter(local_w_in, "dp", scatter_dimension=0, tiled=True).astype(f32)
    grad_w_out = lax.psum_scatter(local_w_out, "dp", scatter_dimension=0, tiled=True).astype(f32)
    grad_hidden, grad_context = join(
        third_kernel,
        sides(arrived, near, grad_placed, slot_places, token_places),
        [arrived, w_o],
        (model_width, model_width),
    )
    local_w_o = dot_first(context_low, grad_hidden).astype(bf16)
    sums_one = jnp.zeros((2, model_width), f32)
    other_sums = [
        sums_two[:2],
        jnp.zeros((4, model_width), f32),
        bias_sums[0].reshape(-1, model_width),
        sums_two[2:3],
        jnp.zeros((3, model_width), f32),
    ]
    first, orders, _, short, along = plan_orders(
        dp_count, expert_count, 4 * model_width, model_width
    )
    if (seq_length // 4) >> len(orders[0]) >= 16:
        norms = jnp.concatenate([sums_one, *other_sums])
        mixed_sum, dense_sum, norms, bias_sums, arrived, near, grad_tokens = backward(
            mixed_qkv, context_low, grad_context, log_totals, w_qkv, local_w_o, normed_t,
            tokens_in, grad_hidden, row(ln1_gain), norms,
            remote_column(token_places, chunk, 0)[None, :],
            slot_places[0][:, None],
            token_places[0][None, :],
            first, short, along, expert_count, chunk,
        )
        grad_w_qkv = mixed_sum.astype(f32)
        grad_w_o = dense_sum.astype(f32)
    else:
        grad_mixed = attend_back(mixed_qkv, context_low, grad_context, log_totals)
        grad_tokens, sums_one = back(grad_mixed, w_qkv, tokens_in, grad_hidden, row(ln1_gain))
        packed = pack(grad_tokens, token_places, chunk, expert_count)
        dense = jnp.concatenate(
            [dot_first(normed_low, grad_mixed[part]).astype(bf16) for part in range(3)]
            + [local_w_o]
        )
        norms = jnp.concatenate([sums_one[:2], *other_sums])
        summed, norms, bias_sums, arrived = finish(
            dense, norms, packed.reshape(expert_count, chunk, model_width), dp_count
        )
        near = near_rows(grad_tokens, token_places, slot_places)
        grad_w_qkv = jnp.concatenate(
            [summed[part * model_width : (part + 1) * model_width] for part in range(3)], axis=1
        ).astype(f32)
        grad_w_o = summed[3 * model_width :].astype(f32)
    arrived = arrived.reshape(-1, model_width)
    (grad_input,) = join(
        last_kernel,
        sides(arrived, near, grad_tokens, token_places, slot_places),
        [arrived],
        (model_width,),
    )
    grad_ln1_gain, grad_ln1_bias, grad_ln2_gain, grad_ln2_bias = norms[:4]
    full_parts = bias_sums[:4].reshape(dp_count, -1)
    grad_b_in = lax.dynamic_index_in_dim(full_parts, dp_index, 0, keepdims=False)
    grad_b_out = lax.dynamic_index_in_dim(
        bias_sums[4].reshape(dp_count, -1), dp_index, 0, keepdims=False
    )
    return (
        result[None],
        grad_input[None],
        grad_ln1_gain,
        grad_ln1_bias,
        grad_w_qkv,
        grad_w_o,
        grad_ln2_gain,
        grad_ln2_bias,
        grad_w_in[None],
        grad_b_in[None],
        grad_w_out[None],
        grad_b_out[None],
    )


def solution(mesh):
    placed = (
        P("dp", "expert", None),
        P("dp", "expert"),
        P(),
        P(),
        P(),
        P(),
        P(),
        P(),
        P("expert", "dp", None),
        P("expert", "dp"),
        P("expert", "dp", None),
        P("expert", "dp"),
        P("dp", "expert", None),
    )
    return jax.shard_map(
        body,
        mesh=mesh,
        in_specs=placed,
        out_specs=(
            P("dp", "expert", None),
            P("dp", "expert", None),
            P(),
            P(),
            P(),
            P(),
            P(),
            P(),
            P("expert", "dp", None),
            P("expert", "dp"),
            P("expert", "dp", None),
            P("expert", "dp"),
        ),
        check_vma=False,
    )
```

```python
import functools

import jax
import jax.numpy as jnp
from jax import lax
from jax.experimental import pallas as pl
from jax.experimental.pallas import tpu as pltpu
from jax.sharding import PartitionSpec as P

HEADS = 16
HEAD_DIM = 64


epsilon = 1e-05
gelu_c = 0.7978845608028654
contract_last = (((1,), (1,)), ((), ()))
contract_first = (((0,), (0,)), ((), ()))


bf16 = jnp.bfloat16
PAIR = 2 * HEAD_DIM
BIG_VMEM = 48 << 20
f32 = jnp.float32


def dot(left, right):
    return jnp.dot(left, right, preferred_element_type=f32)


def dot_last(left, right):
    return lax.dot_general(left, right, contract_last, preferred_element_type=f32)


def dot_first(left, right):
    return lax.dot_general(left, right, contract_first, preferred_element_type=f32)


def head_parts(pair):
    first = lax.broadcasted_iota(jnp.int32, (1, PAIR), 1) < HEAD_DIM
    zero = jnp.zeros_like(pair)
    return [jnp.where(first, pair, zero), jnp.where(first, zero, pair)]


def attend_kernel(block, q_ref, k_ref, v_ref, context_ref, logs_ref):
    length = q_ref.shape[0]
    keys = head_parts(k_ref[...])
    values_t = v_ref[...].T
    rows = lax.broadcasted_iota(jnp.int32, (block, block), 0)
    cols = lax.broadcasted_iota(jnp.int32, (block, block), 1)
    allowed = rows <= cols
    for low in range(0, length, block):
        high = low + block
        queries = q_ref[low:high, :] * jnp.asarray(0.125, bf16)
        outputs = []
        for head in range(2):
            value_rows = values_t[head * HEAD_DIM : (head + 1) * HEAD_DIM]
            near = jnp.where(allowed, dot_last(keys[head][low:high], queries), -1e30)
            peak = jnp.max(near, axis=0, keepdims=True)
            if low:
                far = dot_last(keys[head][:low], queries)
                peak = jnp.maximum(peak, jnp.max(far, axis=0, keepdims=True))
            near = jnp.exp(near - peak)
            total = jnp.sum(near, axis=0, keepdims=True)
            result = dot(value_rows[:, low:high], near.astype(bf16))
            if low:
                far = jnp.exp(far - peak)
                total = total + jnp.sum(far, axis=0, keepdims=True)
                result = result + dot(value_rows[:, :low], far.astype(bf16))
            outputs.append(result / total)
            logs_ref[0, head : head + 1, low:high] = peak + jnp.log(total)
        context_ref[low:high, :] = jnp.concatenate(outputs, axis=0).T.astype(bf16)


def pair_columns(length, offset):
    return pl.BlockSpec((length, PAIR), lambda pair: (0, offset + pair))


def pair_logs(length):
    return pl.BlockSpec((1, 8, length), lambda pair: (pair, 0, 0))


def attend(mixed):
    length, width = mixed.shape[0], mixed.shape[1] // 3
    pairs = width // PAIR
    return pl.pallas_call(
        functools.partial(attend_kernel, min(512, length)),
        grid=(pairs,),
        in_specs=[pair_columns(length, part * pairs) for part in range(3)],
        out_specs=[pair_columns(length, 0), pair_logs(length)],
        out_shape=[
            jax.ShapeDtypeStruct((length, width), bf16),
            jax.ShapeDtypeStruct((pairs, 8, length), f32),
        ],
        compiler_params=pltpu.CompilerParams(vmem_limit_bytes=BIG_VMEM),
        cost_estimate=pl.CostEstimate(
            flops=4 * length * length * width,
            bytes_accessed=8 * length * width,
            transcendentals=length * length * width // HEAD_DIM,
        ),
    )(mixed, mixed, mixed)


def attend_back_pair(
    block, q_ref, k_ref, v_ref, context_ref, grad_ref, logs_ref, out_ref, grad_k, grad_v
):
    length = q_ref.shape[0]
    keys, values, grads = k_ref[...], v_ref[...], grad_ref[...]
    queries = head_parts(q_ref[...] * jnp.asarray(0.125, bf16))
    key_parts = head_parts(keys)
    grad_parts = head_parts(grads)
    products = head_parts(grads.astype(f32) * context_ref[...].astype(f32))
    centres = [jnp.sum(part, axis=1, keepdims=True) for part in products]
    logs = logs_ref[0].T
    rows = lax.broadcasted_iota(jnp.int32, (block, block), 0)
    cols = lax.broadcasted_iota(jnp.int32, (block, block), 1)
    allowed = cols <= rows
    for low in reversed(range(0, length, block)):
        high = low + block
        add_q, add_k, add_v = [], [], []
        for head in range(2):
            scores = dot_last(queries[head][low:high], keys[:high])
            probs = jnp.exp(scores - logs[low:high, head : head + 1])
            near = jnp.where(allowed, probs[:, low:], 0.0)
            probs = jnp.concatenate([probs[:, :low], near], axis=1) if low else near
            grad_probs = dot_last(grad_parts[head][low:high], values[:high])
            grad_scores = (probs * (grad_probs - centres[head][low:high])).astype(bf16)
            add_q.append(dot(grad_scores, key_parts[head][:high]))
            add_k.append(dot_first(grad_scores, queries[head][low:high]))
            add_v.append(dot_first(probs.astype(bf16), grad_parts[head][low:high]))
        out_ref[low:high, :PAIR] = ((add_q[0] + add_q[1]) * 0.125).astype(bf16)
        if high == length:
            grad_k[...] = add_k[0] + add_k[1]
            grad_v[...] = add_v[0] + add_v[1]
        else:
            grad_k[:high, :] += add_k[0] + add_k[1]
            grad_v[:high, :] += add_v[0] + add_v[1]
    out_ref[:, PAIR : 2 * PAIR] = grad_k[...].astype(bf16)
    out_ref[:, 2 * PAIR :] = grad_v[...].astype(bf16)


def attend_back_kernel(block, *refs):
    out_ref, pair_grad, grad_k, grad_v = refs[6:]
    attend_back_pair(block, *refs[:6], pair_grad, grad_k, grad_v)
    for part in range(3):
        out_ref[part] = pair_grad[:, part * PAIR : (part + 1) * PAIR]


def attend_back(mixed, context, grad_context, logs):
    length, width = context.shape
    pairs = width // PAIR
    return pl.pallas_call(
        functools.partial(attend_back_kernel, min(256, length)),
        grid=(pairs,),
        in_specs=[pair_columns(length, part * pairs) for part in range(3)]
        + [pair_columns(length, 0)] * 2
        + [pair_logs(length)],
        out_specs=pl.BlockSpec((3, length, PAIR), lambda pair: (0, 0, pair)),
        out_shape=jax.ShapeDtypeStruct((3, length, width), bf16),
        scratch_shapes=[pltpu.VMEM((length, 3 * PAIR), bf16)]
        + [pltpu.VMEM((length, PAIR), f32)] * 2,
        compiler_params=pltpu.CompilerParams(vmem_limit_bytes=BIG_VMEM),
        cost_estimate=pl.CostEstimate(
            flops=10 * length * length * width,
            bytes_accessed=16 * length * width,
            transcendentals=length * length * width // HEAD_DIM,
        ),
    )(mixed, mixed, mixed, context, grad_context, logs)


def place_rows(columns, count, table):
    chosen = (columns[None, :] == jnp.arange(count, dtype=jnp.int32)[:, None]).astype(bf16)
    return dot(chosen, table).astype(bf16)


def exchange(packed, expert_count):
    return lax.all_to_all(
        packed.reshape(expert_count, -1, packed.shape[-1]),
        "expert",
        split_axis=0,
        concat_axis=0,
        tiled=True,
    ).reshape(-1, packed.shape[-1])


def remote_column(places, chunk, step):
    device, rank = places[1:]
    return jnp.where(rank // chunk == step, device * chunk + rank % chunk, -1)


def pack(table, places, chunk, expert_count, step=0):
    return place_rows(remote_column(places, chunk, step), expert_count * chunk, table)


def pack_slots_kernel(starts, limits, table_ref, out_ref):
    index = pl.program_id(0)
    rows, window = out_ref.shape[0], min(256, table_ref.shape[0])
    start = starts[index]
    base = jnp.minimum(start // 16 * 16, table_ref.shape[0] - window)
    rank = lax.broadcasted_iota(jnp.int32, (rows, window), 0)
    place = lax.broadcasted_iota(jnp.int32, (rows, window), 1)
    chosen = (place == rank + (start - base)) & (rank < limits[index])
    near = table_ref[pl.ds(pl.multiple_of(base, 16), window), :]
    out_ref[...] = dot(chosen.astype(bf16), near).astype(bf16)


def pack_slots(table, starts, limits, chunk):
    count, width = starts.shape[0], table.shape[1]
    return pl.pallas_call(
        pack_slots_kernel,
        grid_spec=pltpu.PrefetchScalarGridSpec(
            num_scalar_prefetch=2,
            grid=(count,),
            in_specs=[
                pl.BlockSpec(
                    table.shape, lambda index, *_: (0, 0), pipeline_mode=pl.Buffered(1)
                )
            ],
            out_specs=pl.BlockSpec((chunk, width), lambda index, *_: (index, 0)),
        ),
        out_shape=jax.ShapeDtypeStruct((count * chunk, width), bf16),
        compiler_params=pltpu.CompilerParams(vmem_limit_bytes=BIG_VMEM),
        cost_estimate=pl.CostEstimate(
            flops=512 * count * chunk * width, bytes_accessed=2 * table.size, transcendentals=0
        ),
    )(starts, limits, table)


def swap(values, axis, bit):
    size = lax.axis_size(axis)
    return lax.ppermute(values, axis, [(i, i ^ bit) for i in range(size)])


def bits_of(axis, size=None):
    size = size or lax.axis_size(axis)
    return [(axis, 1 << k) for k in range(size.bit_length() - 1)]


def peer_index(axis, bit):
    own = lax.axis_index(axis)
    side = (own // bit) % 2
    return side, own + bit * (1 - 2 * side)


def greet(peers):
    barrier = pltpu.get_barrier_semaphore()
    for axis, index in peers:
        pl.semaphore_signal(
            barrier, inc=1, device_id={axis: index}, device_id_type=pl.DeviceIdType.MESH
        )
    pl.semaphore_wait(barrier, len(peers))


def ring_peers(count):
    own = lax.axis_index("expert")
    return [lax.rem(own + step, count) for step in range(1, count)]


def remote(source, target, send_sem, recv_sem, axis, index):
    return pltpu.make_async_remote_copy(
        src_ref=source,
        dst_ref=target,
        send_sem=send_sem,
        recv_sem=recv_sem,
        device_id={axis: index},
        device_id_type=pl.DeviceIdType.MESH,
    )


def rows_of(offset, size):
    return pl.ds(pl.multiple_of(offset, 16), size)


def plan_orders(dp_count, expert_count, rows, width):
    dp_bits, expert_bits = bits_of("dp", dp_count), bits_of("expert", expert_count)
    across, along = dp_bits[1:], expert_bits
    y_bits = along[: max(1, len(along) // 2)]
    z_bits = along[len(y_bits) :]
    if expert_count == 8:
        y_bits, z_bits = along[:1], along[1:]
    orders = (across + y_bits + z_bits, y_bits + across + z_bits)
    steps = len(orders[0])
    short = tuple(order[: steps - len(z_bits)] for order in orders)
    chunks = max(1, rows // (4 * 16 << steps))
    return dp_bits[0], orders, chunks, short, [bit for _, bit in z_bits]


def finish_kernel(
    first, orders, chunks, count, dense_ref, norm_ref, packed_ref, sum_ref, norm_out, bias_out, arrived_ref,
    work, done, *scratch
):
    steps = len(orders[0])
    core_slots = scratch[0]
    part_slots = scratch[1 : 1 + steps]
    norm_work, norm_slots = scratch[1 + steps : 3 + steps]
    core_send, core_recv, part_send, part_recv, norm_send, norm_recv = scratch[3 + steps : 9 + steps]
    swap_send, swap_recv, local_sem = scratch[9 + steps :]
    rows = work.shape[0] // chunks
    half, quarter = rows // 2, rows // 4
    own = lax.axis_index("expert")
    others = ring_peers(count)
    links = [first] + list(orders[0])
    dp_peers = [(axis, peer_index(axis, bit)[1]) for axis, bit in links if axis == "dp"]
    greet([("expert", index) for index in others] + dp_peers)

    swaps = []
    import os
    for step, index in enumerate(others):
        copy = remote(packed_ref.at[index], arrived_ref.at[own], swap_send.at[step], swap_recv.at[step], "expert", index)
        copy.start()
        swaps.append(copy)
    home = pltpu.make_async_copy(packed_ref.at[own], arrived_ref.at[own], local_sem.at[chunks])
    home.start()

    side0, peer0 = peer_index(*first)
    started = []
    norm_work[...] = norm_ref[...]

    def add_rows(offset, size, slot, target):
        block = min(size, 64)

        @pl.loop(0, size // block)
        def _(index):
            here = rows_of(offset + index * block, block)
            there = rows_of(index * block, block)
            target[here, :] = (work[here, :].astype(f32) + slot[there, :].astype(f32)).astype(bf16)

    state = {}

    def event(chunk, number):
        base = chunk * rows
        if number == 0:
            kept = base + side0 * half
            given = base + (1 - side0) * half
            load = pltpu.make_async_copy(dense_ref.at[rows_of(kept, half)], work.at[rows_of(kept, half)], local_sem.at[chunk])
            load.start()
            copy = remote(dense_ref.at[rows_of(given, half)], core_slots.at[chunk], core_send.at[chunk, 0], core_recv.at[chunk, 0], first[0], peer0)
            copy.start()
            started.append(copy)
            state[chunk] = dict(kept=kept, load=load, copy=copy)
        elif number <= 2 * steps + 1:
            for part in range(2):
                go_on(chunk, part, number - 1)
        if number == 2 * steps + 1:
            kept = state[chunk]["kept"]
            copy = remote(done.at[rows_of(kept, half)], done.at[rows_of(kept, half)], core_send.at[chunk, 1], core_recv.at[chunk, 1], first[0], peer0)
            copy.start()
            started.append(copy)
            state[chunk]["copy"] = copy
        if number == 2 * steps + 2:
            state[chunk]["copy"].wait_recv()
            store = pltpu.make_async_copy(done.at[pl.ds(base, rows)], sum_ref.at[pl.ds(base, rows)], local_sem.at[chunk])
            store.start()
            state[chunk]["store"] = store

    def go_on(chunk, part, step):
        here = state[chunk]
        if step == 0:
            if part == 0:
                here["load"].wait()
                here["copy"].wait_recv()
                add_rows(here["kept"], half, core_slots.at[chunk], work)
            offset = here["kept"] + part * quarter
        else:
            offset, size, copy, slot = here[part]
            copy.wait_recv()
            if step <= steps:
                add_rows(offset, size, slot, work if step < steps else done)
        if step < steps:
            axis, bit = orders[part][step]
            side, peer = peer_index(axis, bit)
            size = quarter >> (step + 1)
            slot = part_slots[step].at[chunk, part]
            given = offset + (1 - side) * size
            kept = offset + side * size
            copy = remote(work.at[rows_of(given, size)], slot, part_send.at[chunk, part, step], part_recv.at[chunk, part, step], axis, peer)
            copy.start()
            started.append(copy)
            here[part] = (kept, size, copy, slot)
        elif step < 2 * steps:
            back = 2 * steps - 1 - step
            axis, bit = orders[part][back]
            side, peer = peer_index(axis, bit)
            size = quarter >> (back + 1)
            if step > steps:
                offset = offset - here["side", part] * (size // 2)
            here["side", part] = side
            copy = remote(done.at[rows_of(offset, size)], done.at[rows_of(offset, size)], part_send.at[chunk, part, step], part_recv.at[chunk, part, step], axis, peer)
            copy.start()
            started.append(copy)
            here[part] = (offset, size, copy, None)

    norm_copy = None
    for tick in range(2 * steps + 2 + chunks):
        for chunk in range(chunks):
            number = tick - chunk
            if 0 <= number <= 2 * steps + 2:
                event(chunk, number)
        if tick <= len(links):
            if norm_copy is not None:
                norm_copy.wait()
                norm_work[...] += norm_slots[tick - 1]
                if tick == sum(axis == "dp" for axis, _ in links):
                    bias_out[...] = norm_work[8:16, :]
            if tick < len(links):
                axis, bit = links[tick]
                norm_copy = remote(norm_work, norm_slots.at[tick], norm_send.at[tick], norm_recv.at[tick], axis, peer_index(axis, bit)[1])
                norm_copy.start()
            else:
                norm_out[...] = norm_work[...]
    for copy in started:
        copy.wait_send()
    for copy in swaps:
        copy.wait()
    home.wait()
    for chunk in range(chunks):
        state[chunk]["store"].wait()


def finish(dense, norms, packed, dp_count):
    count = packed.shape[0]
    rows, width = dense.shape
    first, orders, chunks, _, _ = plan_orders(dp_count, count, rows, width)
    steps = len(orders[0])
    part = rows // chunks // 4
    return pl.pallas_call(
        functools.partial(finish_kernel, first, orders, chunks, count),
        in_specs=[
            pl.BlockSpec(memory_space=pl.ANY),
            pl.BlockSpec(memory_space=pltpu.VMEM),
            pl.BlockSpec(memory_space=pl.ANY),
        ],
        out_specs=[
            pl.BlockSpec(memory_space=pl.ANY),
            pl.BlockSpec(memory_space=pltpu.VMEM),
            pl.BlockSpec(memory_space=pltpu.VMEM),
            pl.BlockSpec(memory_space=pl.ANY),
        ],
        out_shape=[
            jax.ShapeDtypeStruct(dense.shape, bf16),
            jax.ShapeDtypeStruct(norms.shape, f32),
            jax.ShapeDtypeStruct((8, width), f32),
            jax.ShapeDtypeStruct(packed.shape, bf16),
        ],
        scratch_shapes=[pltpu.VMEM(dense.shape, bf16)] * 2 + [pltpu.VMEM((chunks, 2 * part, width), bf16)]
        + [pltpu.VMEM((chunks, 2, part >> (step + 1), width), bf16) for step in range(steps)]
        + [
            pltpu.VMEM(norms.shape, f32),
            pltpu.VMEM((steps + 1,) + norms.shape, f32),
            pltpu.SemaphoreType.DMA((chunks, 2)),
            pltpu.SemaphoreType.DMA((chunks, 2)),
            pltpu.SemaphoreType.DMA((chunks, 2, 2 * steps)),
            pltpu.SemaphoreType.DMA((chunks, 2, 2 * steps)),
            pltpu.SemaphoreType.DMA((steps + 1,)),
            pltpu.SemaphoreType.DMA((steps + 1,)),
            pltpu.SemaphoreType.DMA((count - 1,)),
            pltpu.SemaphoreType.DMA((count - 1,)),
            pltpu.SemaphoreType.DMA((chunks + 1,)),
        ],
        compiler_params=pltpu.CompilerParams(
            collective_id=7, has_side_effects=True, vmem_limit_bytes=BIG_VMEM
        ),
        cost_estimate=pl.CostEstimate(
            flops=2 * rows * width, bytes_accessed=8 * rows * width, transcendentals=0
        ),
    )(dense, norms, packed)


def pick(columns, numbers, table):
    return dot((columns == numbers).astype(bf16), table)


def joined_rows(columns, kept, arrived):
    places = lax.broadcasted_iota(jnp.int32, (1, arrived.shape[0]), 1)
    return pick(columns[:, 1:2], places, arrived[...]) + kept[...].astype(f32)


def near_numbers_of(rows):
    return jnp.where(rows < 0, -2, rows)


def near_kernel(columns, numbers, table, rows_ref):
    chosen = near_numbers_of(numbers[0:1, :])
    rows_ref[...] = pick(columns[:, 0:1], chosen, table[...]).astype(bf16)


def norm_parts(rows):
    centre = jnp.mean(rows, axis=-1, keepdims=True)
    centred = rows - centre
    inverse = lax.rsqrt(jnp.mean(centred * centred, axis=-1, keepdims=True) + epsilon)
    return centred * inverse, inverse


def norm_back(grad, scaled, inverse, gains):
    grad_scaled = grad * gains
    first = jnp.mean(grad_scaled, axis=-1, keepdims=True)
    second = jnp.mean(grad_scaled * scaled, axis=-1, keepdims=True)
    return inverse * (grad_scaled - first - scaled * second)


def third_kernel(far, kept, arrived, weight, rows_ref, product_ref):
    rows = joined_rows(far, kept, arrived).astype(bf16)
    rows_ref[...] = rows
    product_ref[...] = dot_last(rows, weight[...]).astype(bf16)


def last_kernel(far, kept, arrived, *rest):
    rows_ref = rest[len(rest) // 2]
    rows_ref[...] = joined_rows(far, kept, arrived).astype(bf16)
    for source, target in zip(rest[: len(rest) // 2], rest[len(rest) // 2 + 1 :]):
        target[...] = source[...].astype(f32)


def again_kernel(columns, kept, arrived, rows_ref):
    places = lax.broadcasted_iota(jnp.int32, (1, arrived.shape[0]), 1)
    rows = pick(columns[...], places, arrived[...]) + kept[...].astype(f32)
    rows_ref[...] = rows.astype(bf16)


def first_again_kernel(columns, kept, arrived, gain, bias, weight, rows_ref, normed_ref, mixed_ref, turned_ref):
    again_kernel(columns, kept, arrived, rows_ref)
    normed = (norm_parts(rows_ref[...].astype(f32))[0] * gain[...] + bias[...]).astype(bf16)
    normed_ref[...] = normed
    mixed_ref[...] = dot(normed, weight[...]).astype(bf16)
    turned_ref[...] = normed.T


def later_rows(step, table, source, target, chunk, expert_count):
    packed = pack(table, source, chunk, expert_count, step)
    return remote_column(target, chunk, step)[:, None], exchange(packed, expert_count)


def more_rounds(kept, table, source, target, chunk, expert_count, rounds):
    def again(state):
        step, sums = state
        columns, arrived = later_rows(step, table, source, target, chunk, expert_count)
        (sums,) = join(again_kernel, [columns, sums], [arrived], (table.shape[1],))
        return (step + 1, sums)

    return lax.while_loop(lambda state: state[0] < rounds, again, (jnp.int32(1), kept))[1]


def more_first_rounds(kept, table, source, target, chunk, expert_count, rounds, gain, bias, weight):
    width = table.shape[1]

    def again(state):
        step, rows, *_ = state
        columns, arrived = later_rows(step, table, source, target, chunk, expert_count)
        rows, normed, mixed, turned = join(
            first_again_kernel, [columns, rows], [arrived, gain, bias, weight],
            (width, width, 3 * width), (width,),
        )
        return (step + 1, rows, normed, turned, mixed)

    return lax.while_loop(lambda state: state[0] < rounds, again, (jnp.int32(1), *kept))[1:]


def finish_rows(far, kept, arrived, sums):
    steps = 8

    def blocks(array):
        return pl.BlockSpec((array.shape[0] // steps, array.shape[1]), lambda step: (step, 0))

    count, width = kept.shape
    return pl.pallas_call(
        last_kernel,
        grid=(steps,),
        in_specs=[blocks(far), blocks(kept), in_full(arrived)] + [blocks(array) for array in sums],
        out_specs=[blocks(kept)] + [blocks(array) for array in sums],
        out_shape=[jax.ShapeDtypeStruct(kept.shape, bf16)]
        + [jax.ShapeDtypeStruct(array.shape, f32) for array in sums],
        compiler_params=pltpu.CompilerParams(vmem_limit_bytes=BIG_VMEM),
        cost_estimate=pl.CostEstimate(
            flops=2 * count * width * arrived.shape[0],
            bytes_accessed=4 * count * width + 6 * sum(array.size for array in sums),
            transcendentals=0,
        ),
    )(far, kept, arrived, *sums)


def block_rows(width):
    return pl.BlockSpec((256, width), lambda step: (step, 0))


def in_full(array):
    return pl.BlockSpec(array.shape, lambda step: (0,) * array.ndim, pipeline_mode=pl.Buffered(1))


def join(kernel, blocked, whole, widths, turned=()):
    count = blocked[0].shape[0]
    table = next(array for array in whole if array.dtype == bf16)
    inside, width = table.shape
    return pl.pallas_call(
        kernel,
        grid=(count // 256,),
        in_specs=[block_rows(array.shape[1]) for array in blocked]
        + [in_full(array) for array in whole],
        out_specs=[block_rows(size) for size in widths]
        + [pl.BlockSpec((size, 256), lambda step: (0, step)) for size in turned],
        out_shape=[jax.ShapeDtypeStruct((count, size), bf16) for size in widths]
        + [jax.ShapeDtypeStruct((size, count), bf16) for size in turned],
        compiler_params=pltpu.CompilerParams(vmem_limit_bytes=BIG_VMEM),
        cost_estimate=pl.CostEstimate(
            flops=2 * count * width * (inside + sum(widths) - width),
            bytes_accessed=2 * (inside * width + count * sum(widths)),
            transcendentals=0,
        ),
    )(*blocked, *whole)


def expert_kernel(
    columns, kept, grad_y, grad_act, arrived, gain, bias, bias_in, bias_out, weight_in_hbm, weight_out_hbm,
    out_ref, normed_ref, act_ref, grad_pre_ref, grad_ref, sum_ref, weight_in, weight_out, load_sem,
):
    hidden, width = weight_in.shape
    block = width
    loads = []
    for index, low in enumerate(range(0, hidden, block)):
        part = pl.ds(low, block)
        loads.append(
            [
                pltpu.make_async_copy(source.at[part], target.at[part], load_sem.at[index, side])
                for side, (source, target) in enumerate(
                    ((weight_in_hbm, weight_in), (weight_out_hbm, weight_out))
                )
            ]
        )

    def work(first):
        if first:
            for pair in loads:
                for copy in pair:
                    copy.start()
            sum_ref[...] = jnp.zeros_like(sum_ref)
        rows = joined_rows(columns, kept, arrived)
        scaled, inverse = norm_parts(rows)
        normed = (scaled * gain[...] + bias[...]).astype(bf16)
        normed_ref[...] = normed
        result = jnp.zeros(rows.shape, f32)
        grad = jnp.zeros(rows.shape, f32)
        for number, low in enumerate(range(0, hidden, block)):
            if first:
                for copy in loads[number]:
                    copy.wait()
            part = slice(low, low + block)
            pre = dot_last(normed, weight_in[part, :]) + bias_in[:, part]
            square = pre * pre
            tangent = jnp.tanh(gelu_c * (pre + 0.044715 * pre * square))
            half = 0.5 * pre
            act = (half + half * tangent).astype(bf16)
            slope = (0.5 + 0.5 * tangent) + half * (1.0 - tangent * tangent) * (
                gelu_c + (3.0 * 0.044715 * gelu_c) * square
            )
            grad_pre = (grad_act[:, part].astype(f32) * slope).astype(bf16)
            act_ref[:, part] = act
            grad_pre_ref[:, part] = grad_pre
            index = 8 + number
            sum_ref[index : index + 1, :] += jnp.sum(grad_pre.astype(f32), axis=0, keepdims=True)
            result += dot(act, weight_out[part, :])
            grad += dot(grad_pre, weight_in[part, :])
        out = rows + result + bias_out[...]
        out_ref[...] = jnp.where(columns[:, 4:5] > 0, out, 0.0).astype(bf16)
        grad_in = grad_y[...].astype(f32)
        grad_ref[...] = (grad_in + norm_back(grad, scaled, inverse, gain[...])).astype(bf16)
        sum_ref[2:3, :] += jnp.sum(grad * scaled, axis=0, keepdims=True)
        sum_ref[3:4, :] += jnp.sum(grad, axis=0, keepdims=True)
        sum_ref[12:13, :] += jnp.sum(grad_in, axis=0, keepdims=True)

    @pl.when(pl.program_id(0) == 0)
    def _():
        work(True)

    @pl.when(pl.program_id(0) > 0)
    def _():
        work(False)


def run_expert(blocked, whole, weights):
    count, width = blocked[1].shape
    hidden = weights[0].shape[0]
    widths = (width, width, hidden, hidden, width)
    return pl.pallas_call(
        expert_kernel,
        grid=(count // 256,),
        in_specs=[block_rows(array.shape[1]) for array in blocked]
        + [in_full(array) for array in whole]
        + [pl.BlockSpec(memory_space=pl.ANY)] * 2,
        out_specs=[block_rows(size) for size in widths]
        + [pl.BlockSpec((16, width), lambda step: (0, 0))],
        out_shape=[jax.ShapeDtypeStruct((count, size), bf16) for size in widths]
        + [jax.ShapeDtypeStruct((16, width), f32)],
        scratch_shapes=[pltpu.VMEM((hidden, width), bf16)] * 2
        + [pltpu.SemaphoreType.DMA((hidden // width, 2))],
        compiler_params=pltpu.CompilerParams(vmem_limit_bytes=58 << 20),
        cost_estimate=pl.CostEstimate(
            flops=6 * count * width * hidden,
            bytes_accessed=2 * count * (5 * width + 3 * hidden) + 4 * width * hidden,
            transcendentals=count * hidden,
        ),
    )(*blocked, *whole, *weights)


def backward_kernel(
    first, orders, along, count, pairs,
    q_ref, k_ref, v_ref, context_ref, grad_ref, logs_ref, wq_ref, wk_ref, wv_ref, dense_ref,
    normed_t, tokens_ref, hidden_ref, gain_ref, norm_ref, token_rows, slot_columns,
    mixed_sum, dense_sum, norm_out, bias_out, arrived_ref, near_ref, tokens_grad,
    work, done, core_slots, *scratch
):
    steps = len(orders[0])
    part_slots = scratch[:steps]
    (
        along_slots, pair_grad, grad_k, grad_v, total, packed, norm_work, norm_slots,
        core_send, core_recv, part_send, part_recv, along_send, along_recv,
        norm_send, norm_recv, swap_send, swap_recv, local_sem,
    ) = scratch[steps:]
    tick = pl.program_id(0)
    rows, width = work.shape[1], pairs * PAIR
    half, quarter = rows // 2, rows // 4
    own = lax.axis_index("expert")
    others = ring_peers(count)
    links = [first] + list(orders[0]) + [("expert", bit) for bit in along]
    link_peers = [(axis, peer_index(axis, bit)[1]) for axis, bit in links]
    events = 2 * steps + 4
    last = pairs + events // 2 - 1

    @pl.when(tick == 0)
    def _():
        greet([("expert", index) for index in others] + [peer for peer in link_peers if peer[0] == "dp"])

    side0, peer0 = peer_index(*first)
    offsets, sides, peers = [], [], []
    for part in range(2):
        offset = side0 * half + part * quarter
        at, side_list, peer_list = [offset], [], []
        for step, (axis, bit) in enumerate(orders[part]):
            side, peer = peer_index(axis, bit)
            offset = offset + side * (quarter >> (step + 1))
            at.append(offset)
            side_list.append(side)
            peer_list.append((axis, peer))
        offsets.append(at)
        sides.append(side_list)
        peers.append(peer_list)
    spread = 1 << len(along)
    place = (own // along[0]) % spread
    piece = quarter >> steps >> len(along)

    def core_give(chunk):
        given = rows_of((1 - side0) * half, half)
        return remote(work.at[chunk, given], core_slots.at[chunk], core_send.at[chunk, 0], core_recv.at[chunk, 0], first[0], peer0)

    def core_return(chunk):
        kept = rows_of(side0 * half, half)
        return remote(done.at[chunk, kept], done.at[chunk, kept], core_send.at[chunk, 1], core_recv.at[chunk, 1], first[0], peer0)

    def part_give(chunk, part, step):
        size = quarter >> (step + 1)
        given = rows_of(offsets[part][step] + (1 - sides[part][step]) * size, size)
        return remote(
            work.at[chunk, given], part_slots[step].at[chunk, part],
            part_send.at[chunk, part, step], part_recv.at[chunk, part, step], *peers[part][step]
        )

    def part_return(chunk, part, step):
        kept = rows_of(offsets[part][step + 1], quarter >> (step + 1))
        return remote(
            done.at[chunk, kept], done.at[chunk, kept],
            part_send.at[chunk, part, steps + step], part_recv.at[chunk, part, steps + step], *peers[part][step]
        )

    def along_copies(chunk, part, back):
        copies = []
        for turn in range(1, spread):
            there = lax.rem(place + turn, spread)
            index = turn - 1 + back * (spread - 1)
            if back:
                source = target = done.at[chunk, rows_of(offsets[part][steps] + place * piece, piece)]
            else:
                source = work.at[chunk, rows_of(offsets[part][steps] + there * piece, piece)]
                target = along_slots.at[chunk, part, turn - 1]
            copies.append(
                remote(
                    source, target, along_send.at[chunk, part, index], along_recv.at[chunk, part, index],
                    "expert", own + (there - place) * along[0]
                )
            )
        return copies

    def store(chunk):
        for part in range(4):
            source = done.at[chunk, :, part * PAIR : (part + 1) * PAIR]
            column = pl.ds(pl.multiple_of(chunk * PAIR + (part % 3) * width, PAIR), PAIR)
            target = mixed_sum if part < 3 else dense_sum
            yield pltpu.make_async_copy(source, target.at[:, column], local_sem.at[chunk, part])

    def add_rows(chunk, offset, size, slots, target):
        block = min(size, 64)

        @pl.loop(0, size // block)
        def _(index):
            here = rows_of(offset + index * block, block)
            there = rows_of(index * block, block)
            sums = work[chunk, here, :].astype(f32)
            for slot in slots:
                sums = sums + slot[there, :].astype(f32)
            target[chunk, here, :] = sums.astype(bf16)

    def event(chunk, number):
        if number == 1:
            core_give(chunk).wait_recv()
            add_rows(chunk, side0 * half, half, [core_slots.at[chunk]], work)
        for part in range(2):
            if 2 <= number <= steps + 1:
                step = number - 2
                part_give(chunk, part, step).wait_recv()
                add_rows(
                    chunk, offsets[part][step + 1], quarter >> (step + 1), [part_slots[step].at[chunk, part]], work
                )
            if number <= steps:
                part_give(chunk, part, number - 1).start()
            elif number == steps + 1:
                for copy in along_copies(chunk, part, 0):
                    copy.start()
            elif number == steps + 2:
                for copy in along_copies(chunk, part, 0):
                    copy.wait_recv()
                slots = [along_slots.at[chunk, part, turn] for turn in range(spread - 1)]
                add_rows(chunk, offsets[part][steps] + place * piece, piece, slots, done)
                for copy in along_copies(chunk, part, 1):
                    copy.start()
            elif number <= 2 * steps + 3:
                back = 2 * steps + 2 - number
                if back == steps - 1:
                    for copy in along_copies(chunk, part, 1):
                        copy.wait_recv()
                else:
                    part_return(chunk, part, back + 1).wait_recv()
                if back >= 0:
                    part_return(chunk, part, back).start()
        if number == 2 * steps + 3:
            core_return(chunk).start()
        if number == 2 * steps + 4:
            core_return(chunk).wait_recv()
            for copy in store(chunk):
                copy.start()

    def norm_step(step):
        return remote(norm_work.at[step], norm_slots.at[step], norm_send.at[step], norm_recv.at[step], *link_peers[step])

    def norm_event(step):
        norm_step(step).wait_recv()
        summed = norm_work[step] + norm_slots[step]
        if step + 1 < len(links):
            norm_work[step + 1] = summed
            norm_step(step + 1).start()
        else:
            norm_out[...] = summed
        if step + 1 == sum(axis == "dp" for axis, _ in links):
            bias_out[...] = summed[8:16]

    def run_events(side):
        for number in range(events, 0, -1):
            if (number + 1) % 2 == side:
                chunk = tick - (1 + number) // 2

                @pl.when((chunk >= 0) & (chunk < pairs))
                def _(number=number, chunk=chunk):
                    event(chunk, number)

        for step in range(len(links)):
            if step % 2 == side:

                @pl.when(tick == pairs + 1 + step // 2)
                def _(step=step):
                    norm_event(step)

    run_events(0)

    @pl.when(tick < pairs)
    def _():
        attend_back_pair(
            min(256, rows), q_ref, k_ref, v_ref, context_ref, grad_ref, logs_ref,
            pair_grad, grad_k, grad_v,
        )
        run_events(1)
        work[tick, :, : 3 * PAIR] = dot(normed_t[...], pair_grad[...]).astype(bf16)
        work[tick, :, 3 * PAIR :] = dense_ref[...]
        core_give(tick).start()
        weights = jnp.concatenate([wq_ref[...], wk_ref[...], wv_ref[...]], axis=1)

        @pl.when(tick == 0)
        def _():
            total[...] = dot_last(pair_grad[...], weights)

        @pl.when(tick > 0)
        def _():
            total[...] += dot_last(pair_grad[...], weights)

    pieces = swap_send.shape[1]
    piece_rows = packed.shape[1] // pieces

    def swap_rows(step, piece):
        index = others[step]
        here = pl.ds(piece * piece_rows, piece_rows)
        return remote(
            packed.at[index, here], arrived_ref.at[own, here],
            swap_send.at[step, piece], swap_recv.at[step, piece], "expert", index
        )

    def start_swaps(pieces):
        for piece in pieces:
            for step in range(count - 1):
                swap_rows(step, piece).start()

    def home_rows():
        return pltpu.make_async_copy(packed.at[own], arrived_ref.at[own], local_sem.at[pairs, 0])

    @pl.when(tick == pairs)
    def _():
        sums = [jnp.zeros((1, width), f32)] * 2
        for low in range(0, rows, 256):
            part = slice(low, low + 256)
            grad = total[part, :]
            scaled, inverse = norm_parts(tokens_ref[part, :].astype(f32))
            result = hidden_ref[part, :].astype(f32) + norm_back(grad, scaled, inverse, gain_ref[...])
            tokens_grad[part, :] = result.astype(bf16)
            sums[0] = sums[0] + jnp.sum(grad * scaled, axis=0, keepdims=True)
            sums[1] = sums[1] + jnp.sum(grad, axis=0, keepdims=True)
        norm_work[0] = norm_ref[...]
        norm_work[0, 0:1, :] = sums[0]
        norm_work[0, 1:2, :] = sums[1]
        norm_step(0).start()
        chunk = packed.shape[1]
        for index in range(count):
            numbers = index * chunk + lax.broadcasted_iota(jnp.int32, (chunk, 1), 0)
            packed[index] = dot((token_rows[1:2, :] == numbers).astype(bf16), tokens_grad[...]).astype(bf16)
        start_swaps([0])
        home_rows().start()

    @pl.when(tick == pairs + 2)
    def _():
        start_swaps([2])

    @pl.when(tick >= pairs)
    def _():
        run_events(1)

    @pl.when(tick == pairs + 1)
    def _():
        start_swaps([1])

    @pl.when(tick == pairs + 2)
    def _():
        start_swaps([3])

    @pl.when(tick == pairs + 2)
    def _():
        for low in range(0, near_ref.shape[0], 256):
            part = slice(low, low + 256)
            near_ref[part, :] = pick(slot_columns[part, 0:1], near_numbers_of(token_rows[0:1, :]), tokens_grad[...]).astype(bf16)

    @pl.when(tick == last)
    def _():
        @pl.loop(0, pairs)
        def _(chunk):
            core_give(chunk).wait_send()
            core_return(chunk).wait_send()
            for part in range(2):
                for step in range(steps):
                    part_give(chunk, part, step).wait_send()
                    part_return(chunk, part, step).wait_send()
                for back in range(2):
                    for copy in along_copies(chunk, part, back):
                        copy.wait_send()
            for copy in store(chunk):
                copy.wait()

        for step in range(len(links)):
            norm_step(step).wait_send()
        for piece in range(pieces):
            for step in range(count - 1):
                swap_rows(step, piece).wait()
        home_rows().wait()


def backward(mixed, context, grad_context, logs, weight, dense, normed_t, tokens, grad_hidden, gain, norms,
             token_rows, slot_columns, first, orders, along, count, chunk):
    length, width = context.shape
    pairs = width // PAIR
    steps = len(orders[0])
    links = 1 + steps + len(along)
    part = length // 4
    slots = slot_columns.shape[0]
    spread = 1 << len(along)

    def columns(offset):
        return pl.BlockSpec((length, PAIR), lambda tick: (0, offset + jnp.minimum(tick, pairs - 1)))

    def whole(array):
        return pl.BlockSpec(array.shape, lambda tick: (0,) * array.ndim, pipeline_mode=pl.Buffered(1))

    def result(shape):
        return pl.BlockSpec(shape, lambda tick: (0,) * len(shape))

    anywhere = pl.BlockSpec(memory_space=pl.ANY)
    fixed = (normed_t, tokens, grad_hidden, gain, norms, token_rows, slot_columns)
    dma = pltpu.SemaphoreType.DMA
    return pl.pallas_call(
        functools.partial(backward_kernel, first, orders, along, count, pairs),
        grid=(pairs + steps + 2,),
        in_specs=[columns(0), columns(pairs), columns(2 * pairs), columns(0), columns(0)]
        + [pl.BlockSpec((1, 8, length), lambda tick: (jnp.minimum(tick, pairs - 1), 0, 0))]
        + [columns(0), columns(pairs), columns(2 * pairs), columns(0)]
        + [whole(array) for array in fixed],
        out_specs=[
            anywhere, anywhere, result(norms.shape), result((8, width)), anywhere,
            result((slots, width)), result((length, width)),
        ],
        out_shape=[
            jax.ShapeDtypeStruct((length, 3 * width), bf16),
            jax.ShapeDtypeStruct((length, width), bf16),
            jax.ShapeDtypeStruct(norms.shape, f32),
            jax.ShapeDtypeStruct((8, width), f32),
            jax.ShapeDtypeStruct((count, chunk, width), bf16),
            jax.ShapeDtypeStruct((slots, width), bf16),
            jax.ShapeDtypeStruct((length, width), bf16),
        ],
        scratch_shapes=[pltpu.VMEM((pairs, length, 4 * PAIR), bf16)] * 2
        + [pltpu.VMEM((pairs, length // 2, 4 * PAIR), bf16)]
        + [pltpu.VMEM((pairs, 2, part >> (step + 1), 4 * PAIR), bf16) for step in range(steps)]
        + [
            pltpu.VMEM((pairs, 2, spread - 1, part >> steps >> len(along), 4 * PAIR), bf16),
            pltpu.VMEM((length, 3 * PAIR), bf16),
            pltpu.VMEM((length, PAIR), f32),
            pltpu.VMEM((length, PAIR), f32),
            pltpu.VMEM((length, width), f32),
            pltpu.VMEM((count, chunk, width), bf16),
            pltpu.VMEM((links,) + norms.shape, f32),
            pltpu.VMEM((links,) + norms.shape, f32),
            dma((pairs, 2)),
            dma((pairs, 2)),
            dma((pairs, 2, 2 * steps)),
            dma((pairs, 2, 2 * steps)),
            dma((pairs, 2, 2 * (spread - 1))),
            dma((pairs, 2, 2 * (spread - 1))),
            dma((links,)),
            dma((links,)),
            dma((count - 1, 4)),
            dma((count - 1, 4)),
            dma((pairs + 1, 4)),
        ],
        compiler_params=pltpu.CompilerParams(
            collective_id=7, has_side_effects=True, vmem_limit_bytes=61 << 20
        ),
        cost_estimate=pl.CostEstimate(
            flops=10 * length * length * width, bytes_accessed=32 * length * width,
            transcendentals=length * length * width // HEAD_DIM,
        ),
    )(mixed, mixed, mixed, context, grad_context, logs, weight, weight, weight, dense, *fixed)


def begin_kernel(
    count, chunk, dp_count, ids_ref, table_hbm, gain_ref, bias_ref, weight_hbm,
    token_columns, slot_columns, token_rows, slot_rows, info_ref, rows_out, normed_out, turned_out, mixed_out,
    ids_all, table, weight, packed, arrived, near, rows_work, normed_work, turned_work, mixed_work, most_work, most_slots,
    ids_send, ids_recv, swap_send, swap_recv, most_send, most_recv, local_sem, out_sem,
):
    own = lax.axis_index("expert")
    others = ring_peers(count)
    load = pltpu.make_async_copy(table_hbm, table, local_sem.at[0])
    load.start()
    load_weight = pltpu.make_async_copy(weight_hbm, weight, local_sem.at[1])
    load_weight.start()
    dp_own = lax.axis_index("dp")
    dp_others = [lax.rem(dp_own + step, dp_count) for step in range(1, dp_count)]
    greet([("expert", index) for index in others] + [("dp", index) for index in dp_others])
    sends = [
        remote(ids_ref, ids_all.at[own], ids_send.at[step], ids_recv.at[step], "expert", index)
        for step, index in enumerate(others)
    ]
    for copy in sends:
        copy.start()
    ids_all[own] = ids_ref[...]
    length, slots = ids_ref.shape[1], table.shape[0]
    earlier = lax.broadcasted_iota(jnp.int32, (length, length), 0) < lax.broadcasted_iota(
        jnp.int32, (length, length), 1
    )
    earlier = earlier.astype(bf16)
    for copy in sends:
        copy.wait()

    own_f = own.astype(f32)
    rows = [ids_all[index] for index in range(count)]
    ids = jnp.concatenate(rows, axis=0).astype(f32)
    lane = lax.broadcasted_iota(jnp.int32, (count, 128), 1).astype(f32)
    sequence = lax.broadcasted_iota(jnp.int32, (count, 1), 0).astype(f32)
    counts = jnp.zeros((count, 128), f32)
    for expert in range(count):
        taken = jnp.sum((ids == float(expert)).astype(f32), axis=1, keepdims=True)
        counts = jnp.where(lane == float(expert), taken, counts)
    fullest = (counts == jnp.max(counts, axis=0, keepdims=True)) & (lane < float(count))
    fullest = fullest.astype(f32)
    peaks = jnp.sum(fullest, axis=1, keepdims=True)
    single = (jnp.max(peaks, axis=0, keepdims=True) == 1.0) & (jnp.min(peaks, axis=0, keepdims=True) == 1.0)
    owner = jnp.where(single, jnp.sum(fullest * lane, axis=1, keepdims=True), sequence)
    from_each = jnp.sum(jnp.where(lane == own_f, counts, 0.0), axis=1, keepdims=True)
    as_row = jnp.sum(jnp.where(lane == sequence, from_each, 0.0), axis=0, keepdims=True)
    starts = jnp.sum(jnp.where(lane < sequence, as_row, 0.0), axis=1, keepdims=True)
    away = jnp.max(jnp.where(lane == owner, 0.0, counts), axis=1, keepdims=True)
    most = jnp.max(away, axis=0, keepdims=True)
    at_device = lane == owner
    device_starts = jnp.sum(jnp.where(at_device, starts, 0.0), axis=0, keepdims=True)
    limits = jnp.where(owner == own_f, 0.0, from_each)
    device_limits = jnp.sum(jnp.where(at_device, limits, 0.0), axis=0, keepdims=True)
    most_work[...] = jnp.broadcast_to(most, (8, 128))
    mosts = [
        remote(most_work, most_slots.at[step], most_send.at[step], most_recv.at[step], "dp", index)
        for step, index in enumerate(dp_others)
    ]
    for copy in mosts:
        copy.start()

    def places(inside, home, device, rank):
        near = jnp.where(inside & home, rank, -1.0)
        there = inside & ~home
        far = jnp.where(there & (rank < float(chunk)), device * float(chunk) + rank, -1.0)
        rank = jnp.where(there, rank, -float(chunk))
        empty = jnp.zeros((3, rank.shape[1]), f32)
        return jnp.concatenate([near, far, device, rank, inside.astype(f32), empty], axis=0)

    slot = lax.broadcasted_iota(jnp.int32, (1, slots), 1).astype(f32)
    used = jnp.zeros((1, slots), f32)
    slot_rank = jnp.zeros((1, slots), f32)
    slot_device = jnp.zeros((1, slots), f32)
    for index in range(count):
        start = starts[index : index + 1]
        inside = (slot >= start) & (slot < start + from_each[index : index + 1])
        used = jnp.where(inside, 1.0, used)
        slot_rank = jnp.where(inside, slot - start, slot_rank)
        slot_device = jnp.where(inside, owner[index : index + 1], slot_device)
    slot_places = places(used > 0.0, slot_device == own_f, slot_device, slot_rank)
    far_slots = slot_places[1:2]

    load.wait()
    swaps = []
    for step, index in enumerate(others):
        numbers = index * chunk + lax.broadcasted_iota(jnp.int32, (chunk, 1), 0)
        chosen = (far_slots == numbers.astype(f32)).astype(bf16)
        packed[step] = dot(chosen, table[...]).astype(bf16)
        copy = remote(packed.at[step], arrived.at[own], swap_send.at[step], swap_recv.at[step], "expert", index)
        copy.start()
        swaps.append(copy)
    arrived[own] = jnp.zeros(packed.shape[1:], bf16)

    held = jnp.zeros((1, length), f32)
    for index in range(count):
        held = jnp.where(owner[index : index + 1] == own_f, rows[index].astype(f32), held)
    expert = lax.broadcasted_iota(jnp.int32, (16, 1), 0).astype(f32)
    choose = (held == expert).astype(f32)
    before = dot(choose.astype(bf16), earlier)
    token_rank = jnp.sum(choose * before, axis=0, keepdims=True)
    token_places = places(held >= 0.0, held == own_f, held, token_rank)
    slot_rows[...] = slot_places.astype(jnp.int32)
    token_rows[...] = token_places.astype(jnp.int32)
    slot_turned = slot_places.T
    token_turned = token_places.T
    slot_columns[...] = slot_turned.astype(jnp.int32)
    token_columns[...] = token_turned.astype(jnp.int32)
    near_slots = jnp.where(slot_places[0:1] < 0.0, -2.0, slot_places[0:1])
    for low in range(0, length, 256):
        part = slice(low, low + 256)
        near[part, :] = pick(token_turned[part, 0:1], near_slots, table[...]).astype(bf16)
    for copy in mosts:
        copy.wait()
    overall = most_work[0:1, :]
    for step in range(dp_count - 1):
        overall = jnp.maximum(overall, most_slots[step, 0:1, :])
    blank = jnp.zeros((5, 128), f32)
    info = jnp.concatenate([overall, device_starts, device_limits, blank], axis=0)
    info_ref[...] = info.astype(jnp.int32)
    load_weight.wait()
    for copy in swaps:
        copy.wait()
    far_places = lax.broadcasted_iota(jnp.int32, (1, count * chunk), 1).astype(f32)
    stores = []
    for index, low in enumerate(range(0, length, 256)):
        part = slice(low, low + 256)
        there = (token_turned[part, 1:2] == far_places).astype(bf16)
        got = near[part, :].astype(f32)
        for source in range(count):
            got = got + dot(there[:, source * chunk : (source + 1) * chunk], arrived[source])
        normed = (norm_parts(got)[0] * gain_ref[...] + bias_ref[...]).astype(bf16)
        rows_work[part, :] = got.astype(bf16)
        normed_work[part, :] = normed
        turned_work[:, part] = normed.T
        mixed_work[part, :] = dot(normed, weight[...]).astype(bf16)
        here = pl.ds(low, 256)
        for number, (source, target) in enumerate(
            ((rows_work, rows_out), (normed_work, normed_out), (mixed_work, mixed_out))
        ):
            stores.append(pltpu.make_async_copy(source.at[here], target.at[here], out_sem.at[index, number]))
            stores[-1].start()
        stores.append(pltpu.make_async_copy(turned_work.at[:, here], turned_out.at[:, here], out_sem.at[index, 3]))
        stores[-1].start()
    for copy in stores:
        copy.wait()


def begin(ids, table, gain, bias, weight, count, chunk, dp_count):
    length = ids.shape[0]
    slots, width = table.shape
    vmem = pl.BlockSpec(memory_space=pltpu.VMEM)
    anywhere = pl.BlockSpec(memory_space=pl.ANY)
    whole = jax.ShapeDtypeStruct
    dma = pltpu.SemaphoreType.DMA
    return pl.pallas_call(
        functools.partial(begin_kernel, count, chunk, dp_count),
        in_specs=[vmem, anywhere, vmem, vmem, anywhere],
        out_specs=[vmem] * 5 + [anywhere] * 4,
        out_shape=[
            whole((length, 8), jnp.int32),
            whole((slots, 8), jnp.int32),
            whole((8, length), jnp.int32),
            whole((8, slots), jnp.int32),
            whole((8, 128), jnp.int32),
            whole((length, width), bf16),
            whole((length, width), bf16),
            whole((width, length), bf16),
            whole((length, 3 * width), bf16),
        ],
        scratch_shapes=[
            pltpu.VMEM((count, 1, length), jnp.int32),
            pltpu.VMEM((slots, width), bf16),
            pltpu.VMEM(weight.shape, bf16),
            pltpu.VMEM((count - 1, chunk, width), bf16),
            pltpu.VMEM((count, chunk, width), bf16),
            pltpu.VMEM((length, width), bf16),
            pltpu.VMEM((length, width), bf16),
            pltpu.VMEM((length, width), bf16),
            pltpu.VMEM((width, length), bf16),
            pltpu.VMEM((length, 3 * width), bf16),
            pltpu.VMEM((8, 128), f32),
            pltpu.VMEM((dp_count - 1, 8, 128), f32),
            dma((count - 1,)),
            dma((count - 1,)),
            dma((count - 1,)),
            dma((count - 1,)),
            dma((dp_count - 1,)),
            dma((dp_count - 1,)),
            dma((2,)),
            dma((length // 256, 4)),
        ],
        compiler_params=pltpu.CompilerParams(
            collective_id=5, has_side_effects=True, vmem_limit_bytes=BIG_VMEM
        ),
        cost_estimate=pl.CostEstimate(
            flops=12 * length * slots * width, bytes_accessed=8 * slots * width, transcendentals=0
        ),
    )(ids[None, :], table, gain, bias, weight)


def back_kernel(grad_ref, weight_ref, tokens_ref, hidden_ref, gain_ref, out_ref, sum_ref):
    width = gain_ref.shape[1]
    grad = sum(
        dot_last(grad_ref[part], weight_ref[:, part * width : (part + 1) * width])
        for part in range(3)
    )
    scaled, inverse = norm_parts(tokens_ref[...].astype(f32))
    result = hidden_ref[...].astype(f32) + norm_back(grad, scaled, inverse, gain_ref[...])
    out_ref[...] = result.astype(bf16)

    @pl.when(pl.program_id(0) == 0)
    def _():
        sum_ref[...] = jnp.zeros_like(sum_ref)

    sum_ref[0:1, :] += jnp.sum(grad * scaled, axis=0, keepdims=True)
    sum_ref[1:2, :] += jnp.sum(grad, axis=0, keepdims=True)


def back(grad_mixed, weight, tokens, grad_hidden, gain):
    count, width = tokens.shape
    block = 256

    def by_rows():
        return pl.BlockSpec((block, width), lambda step: (step, 0))

    return pl.pallas_call(
        back_kernel,
        grid=(count // block,),
        in_specs=[
            pl.BlockSpec((3, block, width), lambda step: (0, step, 0)),
            pl.BlockSpec(weight.shape, lambda step: (0, 0)),
            by_rows(),
            by_rows(),
            pl.BlockSpec((1, width), lambda step: (0, 0)),
        ],
        out_specs=[by_rows(), pl.BlockSpec((8, width), lambda step: (0, 0))],
        out_shape=[
            jax.ShapeDtypeStruct((count, width), bf16),
            jax.ShapeDtypeStruct((8, width), f32),
        ],
        compiler_params=pltpu.CompilerParams(vmem_limit_bytes=BIG_VMEM),
        cost_estimate=pl.CostEstimate(
            flops=6 * count * width * width, bytes_accessed=20 * count * width, transcendentals=0
        ),
    )(grad_mixed, weight, tokens, grad_hidden, gain)


def body(
    block_input,
    expert_ids,
    ln1_gain,
    ln1_bias,
    w_qkv,
    w_o,
    ln2_gain,
    ln2_bias,
    w_in,
    b_in,
    w_out,
    b_out,
    cotangent,
):
    expert_count = lax.axis_size("expert")
    model_width = block_input.shape[2]
    seq_ids = expert_ids[0]
    seq_length = seq_ids.shape[0]
    chunk = seq_length // expert_count
    dp_index = lax.axis_index("dp")
    dp_count = lax.axis_size("dp")

    def row(values):
        return values.astype(f32).reshape(1, -1)

    token_columns, slot_columns, token_rows, slot_rows, info, *first_rows = begin(
        seq_ids, block_input[0], row(ln1_gain), row(ln1_bias), w_qkv, expert_count, chunk, dp_count
    )
    rounds = (info[0, 0] + chunk - 1) // chunk
    token_places = tuple(token_rows[part] for part in (0, 2, 3))
    slot_places = tuple(slot_rows[part] for part in (0, 2, 3))
    token_side = (token_places, token_rows, token_columns)
    slot_side = (slot_places, slot_rows, slot_columns)
    device_starts, device_limits = info[1, :expert_count], info[2, :expert_count]

    def start(table):
        return exchange(pack(table, token_places, chunk, expert_count), expert_count)

    def start_slots(table):
        packed = pack_slots(table, device_starts, device_limits, chunk)
        return exchange(packed, expert_count)

    def near_rows(table, source, target):
        (rows,) = join(near_kernel, [target[2]], [source[1], table], (model_width,))
        return rows

    def sides(kept, table, source, target):
        kept = more_rounds(kept, table, source[0], target[0], chunk, expert_count, rounds)
        return [target[2], kept]

    full_in = lax.all_gather(w_in[0], "dp", axis=0, tiled=True)
    full_out = lax.all_gather(w_out[0], "dp", axis=0, tiled=True)

    tokens_in, normed_low, normed_t, mixed_qkv = more_first_rounds(
        first_rows, block_input[0], slot_places, token_places, chunk, expert_count, rounds,
        row(ln1_gain), row(ln1_bias), w_qkv,
    )
    context_low, log_totals = attend(mixed_qkv)
    hidden = (tokens_in.astype(f32) + dot(context_low, w_o)).astype(bf16)
    late, b_in, b_out, hidden = lax.optimization_barrier((cotangent[0], b_in, b_out, hidden))
    arrived = start(hidden)
    grad_low = jnp.where(slot_columns[:, 4:5] > 0, late, jnp.zeros((), jnp.bfloat16))
    grad_act = dot_last(grad_low, full_out).astype(bf16)
    biases = jnp.concatenate([b_in, b_out], axis=1)
    for axis, bit in bits_of("dp"):
        got = swap(biases, axis, bit)
        upper = (dp_index // bit) % 2 == 1
        biases = jnp.where(
            upper, jnp.concatenate([got, biases]), jnp.concatenate([biases, got])
        )
    hidden_part = b_in.shape[1]
    full_bias_in = row(biases[:, :hidden_part])
    full_bias_out = row(biases[:, hidden_part:])
    near = near_rows(hidden, token_side, slot_side)
    arrived, grad_act, near = lax.optimization_barrier((arrived, grad_act, near))
    result, normed_two, act_low, grad_pre, grad_placed, norms = run_expert(
        sides(near, hidden, token_side, slot_side) + [grad_low, grad_act],
        [arrived, row(ln2_gain), row(ln2_bias), full_bias_in, full_bias_out],
        [full_in, full_out],
    )
    arrived = start_slots(grad_placed)
    local_w_in = dot_first(grad_pre, normed_two).astype(bf16)
    local_w_out = dot_first(act_low, grad_low).astype(bf16)
    near = near_rows(grad_placed, slot_side, token_side)
    arrived, near, local_w_in, local_w_out = lax.optimization_barrier(
        (arrived, near, local_w_in, local_w_out)
    )
    sum_in = lax.psum_scatter(local_w_in, "dp", scatter_dimension=0, tiled=True)
    sum_out = lax.psum_scatter(local_w_out, "dp", scatter_dimension=0, tiled=True)
    grad_hidden, grad_context = join(
        third_kernel,
        sides(near, grad_placed, slot_side, token_side),
        [arrived, w_o],
        (model_width, model_width),
    )
    local_w_o = dot_first(context_low, grad_hidden).astype(bf16)
    first, orders, _, short, along = plan_orders(
        dp_count, expert_count, 4 * model_width, model_width
    )
    if (seq_length // 4) >> len(orders[0]) >= 16:
        mixed_sum, dense_sum, norms, bias_sums, arrived, near, grad_tokens = backward(
            mixed_qkv, context_low, grad_context, log_totals, w_qkv, local_w_o, normed_t,
            tokens_in, grad_hidden, row(ln1_gain), norms,
            token_rows, slot_columns,
            first, short, along, expert_count, chunk,
        )
    else:
        grad_mixed = attend_back(mixed_qkv, context_low, grad_context, log_totals)
        grad_tokens, sums_one = back(grad_mixed, w_qkv, tokens_in, grad_hidden, row(ln1_gain))
        packed = pack(grad_tokens, token_places, chunk, expert_count)
        dense = jnp.concatenate(
            [dot_first(normed_low, grad_mixed[part]).astype(bf16) for part in range(3)]
            + [local_w_o]
        )
        norms = norms.at[:2].set(sums_one[:2])
        summed, norms, bias_sums, arrived = finish(
            dense, norms, packed.reshape(expert_count, chunk, model_width), dp_count
        )
        near = near_rows(grad_tokens, token_side, slot_side)
        mixed_sum = jnp.concatenate(
            [summed[part * model_width : (part + 1) * model_width] for part in range(3)], axis=1
        )
        dense_sum = summed[3 * model_width :]
    arrived = arrived.reshape(-1, model_width)
    columns, kept = sides(near, grad_tokens, token_side, slot_side)
    grad_input, grad_w_qkv, grad_w_o, grad_w_in, grad_w_out = finish_rows(
        columns, kept, arrived, [mixed_sum, dense_sum, sum_in, sum_out]
    )
    grad_ln1_gain, grad_ln1_bias, grad_ln2_gain, grad_ln2_bias = norms[:4]
    full_parts = bias_sums[:4].reshape(dp_count, -1)
    grad_b_in = lax.dynamic_index_in_dim(full_parts, dp_index, 0, keepdims=False)
    grad_b_out = lax.dynamic_index_in_dim(
        bias_sums[4].reshape(dp_count, -1), dp_index, 0, keepdims=False
    )
    return (
        result[None],
        grad_input[None],
        grad_ln1_gain,
        grad_ln1_bias,
        grad_w_qkv,
        grad_w_o,
        grad_ln2_gain,
        grad_ln2_bias,
        grad_w_in[None],
        grad_b_in[None],
        grad_w_out[None],
        grad_b_out[None],
    )


def solution(mesh):
    placed = (
        P("dp", "expert", None),
        P("dp", "expert"),
        P(),
        P(),
        P(),
        P(),
        P(),
        P(),
        P("expert", "dp", None),
        P("expert", "dp"),
        P("expert", "dp", None),
        P("expert", "dp"),
        P("dp", "expert", None),
    )
    return jax.shard_map(
        body,
        mesh=mesh,
        in_specs=placed,
        out_specs=(
            P("dp", "expert", None),
            P("dp", "expert", None),
            P(),
            P(),
            P(),
            P(),
            P(),
            P(),
            P("expert", "dp", None),
            P("expert", "dp"),
            P("expert", "dp", None),
            P("expert", "dp"),
        ),
        check_vma=False,
    )
```

```python
import functools

import jax
import jax.numpy as jnp
from jax import lax
from jax.experimental import pallas as pl
from jax.experimental.pallas import tpu as pltpu
from jax.sharding import PartitionSpec as P

HEADS = 16
HEAD_DIM = 64


epsilon = 1e-05
gelu_c = 0.7978845608028654
contract_last = (((1,), (1,)), ((), ()))
contract_first = (((0,), (0,)), ((), ()))


bf16 = jnp.bfloat16
PAIR = 2 * HEAD_DIM
BIG_VMEM = 48 << 20
f32 = jnp.float32


def dot(left, right):
    return jnp.dot(left, right, preferred_element_type=f32)


def dot_last(left, right):
    return lax.dot_general(left, right, contract_last, preferred_element_type=f32)


def dot_first(left, right):
    return lax.dot_general(left, right, contract_first, preferred_element_type=f32)


def head_parts(pair):
    first = lax.broadcasted_iota(jnp.int32, (1, PAIR), 1) < HEAD_DIM
    zero = jnp.zeros_like(pair)
    return [jnp.where(first, pair, zero), jnp.where(first, zero, pair)]


def attend_kernel(block, q_ref, k_ref, v_ref, context_ref, logs_ref):
    length = q_ref.shape[0]
    keys = head_parts(k_ref[...])
    values_t = v_ref[...].T
    rows = lax.broadcasted_iota(jnp.int32, (block, block), 0)
    cols = lax.broadcasted_iota(jnp.int32, (block, block), 1)
    allowed = rows <= cols
    for low in range(0, length, block):
        high = low + block
        queries = q_ref[low:high, :] * jnp.asarray(0.125, bf16)
        outputs = []
        for head in range(2):
            value_rows = values_t[head * HEAD_DIM : (head + 1) * HEAD_DIM]
            near = jnp.where(allowed, dot_last(keys[head][low:high], queries), -1e30)
            peak = jnp.max(near, axis=0, keepdims=True)
            if low:
                far = dot_last(keys[head][:low], queries)
                peak = jnp.maximum(peak, jnp.max(far, axis=0, keepdims=True))
            near = jnp.exp(near - peak)
            total = jnp.sum(near, axis=0, keepdims=True)
            result = dot(value_rows[:, low:high], near.astype(bf16))
            if low:
                far = jnp.exp(far - peak)
                total = total + jnp.sum(far, axis=0, keepdims=True)
                result = result + dot(value_rows[:, :low], far.astype(bf16))
            outputs.append(result / total)
            logs_ref[0, head : head + 1, low:high] = peak + jnp.log(total)
        context_ref[low:high, :] = jnp.concatenate(outputs, axis=0).T.astype(bf16)


def pair_columns(length, offset):
    return pl.BlockSpec((length, PAIR), lambda pair: (0, offset + pair))


def pair_logs(length):
    return pl.BlockSpec((1, 8, length), lambda pair: (pair, 0, 0))


def attend(mixed):
    length, width = mixed.shape[0], mixed.shape[1] // 3
    pairs = width // PAIR
    return pl.pallas_call(
        functools.partial(attend_kernel, min(1024, length)),
        grid=(pairs,),
        in_specs=[pair_columns(length, part * pairs) for part in range(3)],
        out_specs=[pair_columns(length, 0), pair_logs(length)],
        out_shape=[
            jax.ShapeDtypeStruct((length, width), bf16),
            jax.ShapeDtypeStruct((pairs, 8, length), f32),
        ],
        compiler_params=pltpu.CompilerParams(vmem_limit_bytes=BIG_VMEM),
        cost_estimate=pl.CostEstimate(
            flops=4 * length * length * width,
            bytes_accessed=8 * length * width,
            transcendentals=length * length * width // HEAD_DIM,
        ),
    )(mixed, mixed, mixed)


def attend_back_pair(
    block, q_ref, k_ref, v_ref, context_ref, grad_ref, logs_ref, out_ref, grad_k, grad_v
):
    length = q_ref.shape[0]
    keys, values, grads = k_ref[...], v_ref[...], grad_ref[...]
    queries = head_parts(q_ref[...] * jnp.asarray(0.125, bf16))
    key_parts = head_parts(keys)
    grad_parts = head_parts(grads)
    products = head_parts(grads.astype(f32) * context_ref[...].astype(f32))
    centres = [jnp.sum(part, axis=1, keepdims=True) for part in products]
    logs = logs_ref[0].T
    rows = lax.broadcasted_iota(jnp.int32, (block, block), 0)
    cols = lax.broadcasted_iota(jnp.int32, (block, block), 1)
    allowed = cols <= rows
    for low in reversed(range(0, length, block)):
        high = low + block
        add_q, add_k, add_v = [], [], []
        for head in range(2):
            scores = dot_last(queries[head][low:high], keys[:high])
            probs = jnp.exp(scores - logs[low:high, head : head + 1])
            near = jnp.where(allowed, probs[:, low:], 0.0)
            probs = jnp.concatenate([probs[:, :low], near], axis=1) if low else near
            grad_probs = dot_last(grad_parts[head][low:high], values[:high])
            grad_scores = (probs * (grad_probs - centres[head][low:high])).astype(bf16)
            add_q.append(dot(grad_scores, key_parts[head][:high]))
            add_k.append(dot_first(grad_scores, queries[head][low:high]))
            add_v.append(dot_first(probs.astype(bf16), grad_parts[head][low:high]))
        out_ref[low:high, :PAIR] = ((add_q[0] + add_q[1]) * 0.125).astype(bf16)
        if high == length:
            grad_k[...] = add_k[0] + add_k[1]
            grad_v[...] = add_v[0] + add_v[1]
        else:
            grad_k[:high, :] += add_k[0] + add_k[1]
            grad_v[:high, :] += add_v[0] + add_v[1]
    out_ref[:, PAIR : 2 * PAIR] = grad_k[...].astype(bf16)
    out_ref[:, 2 * PAIR :] = grad_v[...].astype(bf16)


def attend_back_kernel(block, *refs):
    out_ref, pair_grad, grad_k, grad_v = refs[6:]
    attend_back_pair(block, *refs[:6], pair_grad, grad_k, grad_v)
    for part in range(3):
        out_ref[part] = pair_grad[:, part * PAIR : (part + 1) * PAIR]


def attend_back(mixed, context, grad_context, logs):
    length, width = context.shape
    pairs = width // PAIR
    return pl.pallas_call(
        functools.partial(attend_back_kernel, min(256, length)),
        grid=(pairs,),
        in_specs=[pair_columns(length, part * pairs) for part in range(3)]
        + [pair_columns(length, 0)] * 2
        + [pair_logs(length)],
        out_specs=pl.BlockSpec((3, length, PAIR), lambda pair: (0, 0, pair)),
        out_shape=jax.ShapeDtypeStruct((3, length, width), bf16),
        scratch_shapes=[pltpu.VMEM((length, 3 * PAIR), bf16)]
        + [pltpu.VMEM((length, PAIR), f32)] * 2,
        compiler_params=pltpu.CompilerParams(vmem_limit_bytes=BIG_VMEM),
        cost_estimate=pl.CostEstimate(
            flops=10 * length * length * width,
            bytes_accessed=16 * length * width,
            transcendentals=length * length * width // HEAD_DIM,
        ),
    )(mixed, mixed, mixed, context, grad_context, logs)


def place_rows(columns, count, table):
    chosen = (columns[None, :] == jnp.arange(count, dtype=jnp.int32)[:, None]).astype(bf16)
    return dot(chosen, table).astype(bf16)


def exchange(packed, expert_count):
    return lax.all_to_all(
        packed.reshape(expert_count, -1, packed.shape[-1]),
        "expert",
        split_axis=0,
        concat_axis=0,
        tiled=True,
    ).reshape(-1, packed.shape[-1])


def remote_column(places, chunk, step):
    device, rank = places[1:]
    return jnp.where(rank // chunk == step, device * chunk + rank % chunk, -1)


def pack(table, places, chunk, expert_count, step=0):
    return place_rows(remote_column(places, chunk, step), expert_count * chunk, table)


def pack_slots_kernel(starts, limits, table_ref, out_ref):
    index = pl.program_id(0)
    rows, window = out_ref.shape[0], min(256, table_ref.shape[0])
    start = starts[index]
    base = jnp.minimum(start // 16 * 16, table_ref.shape[0] - window)
    rank = lax.broadcasted_iota(jnp.int32, (rows, window), 0)
    place = lax.broadcasted_iota(jnp.int32, (rows, window), 1)
    chosen = (place == rank + (start - base)) & (rank < limits[index])
    near = table_ref[pl.ds(pl.multiple_of(base, 16), window), :]
    out_ref[...] = dot(chosen.astype(bf16), near).astype(bf16)


def pack_slots(table, starts, limits, chunk):
    count, width = starts.shape[0], table.shape[1]
    return pl.pallas_call(
        pack_slots_kernel,
        grid_spec=pltpu.PrefetchScalarGridSpec(
            num_scalar_prefetch=2,
            grid=(count,),
            in_specs=[
                pl.BlockSpec(
                    table.shape, lambda index, *_: (0, 0), pipeline_mode=pl.Buffered(1)
                )
            ],
            out_specs=pl.BlockSpec((chunk, width), lambda index, *_: (index, 0)),
        ),
        out_shape=jax.ShapeDtypeStruct((count * chunk, width), bf16),
        compiler_params=pltpu.CompilerParams(vmem_limit_bytes=BIG_VMEM),
        cost_estimate=pl.CostEstimate(
            flops=512 * count * chunk * width, bytes_accessed=2 * table.size, transcendentals=0
        ),
    )(starts, limits, table)


def swap(values, axis, bit):
    size = lax.axis_size(axis)
    return lax.ppermute(values, axis, [(i, i ^ bit) for i in range(size)])


def bits_of(axis, size=None):
    size = size or lax.axis_size(axis)
    return [(axis, 1 << k) for k in range(size.bit_length() - 1)]


def peer_index(axis, bit):
    own = lax.axis_index(axis)
    side = (own // bit) % 2
    return side, own + bit * (1 - 2 * side)


def greet(peers):
    barrier = pltpu.get_barrier_semaphore()
    for axis, index in peers:
        pl.semaphore_signal(
            barrier, inc=1, device_id={axis: index}, device_id_type=pl.DeviceIdType.MESH
        )
    pl.semaphore_wait(barrier, len(peers))


def ring_peers(count):
    own = lax.axis_index("expert")
    return [lax.rem(own + step, count) for step in range(1, count)]


def remote(source, target, send_sem, recv_sem, axis, index):
    return pltpu.make_async_remote_copy(
        src_ref=source,
        dst_ref=target,
        send_sem=send_sem,
        recv_sem=recv_sem,
        device_id={axis: index},
        device_id_type=pl.DeviceIdType.MESH,
    )


def rows_of(offset, size):
    return pl.ds(pl.multiple_of(offset, 16), size)


def plan_orders(dp_count, expert_count, rows, width):
    dp_bits, expert_bits = bits_of("dp", dp_count), bits_of("expert", expert_count)
    across, along = dp_bits[1:], expert_bits
    y_bits = along[: max(1, len(along) // 2)]
    z_bits = along[len(y_bits) :]
    if expert_count == 8:
        y_bits, z_bits = along[:1], along[1:]
    orders = (across + y_bits + z_bits, y_bits + across + z_bits)
    steps = len(orders[0])
    short = tuple(order[: steps - len(z_bits)] for order in orders)
    chunks = max(1, rows // (4 * 16 << steps))
    return dp_bits[0], orders, chunks, short, [bit for _, bit in z_bits]


def finish_kernel(
    first, orders, chunks, count, dense_ref, norm_ref, packed_ref, sum_ref, norm_out, bias_out, arrived_ref,
    work, done, *scratch
):
    steps = len(orders[0])
    core_slots = scratch[0]
    part_slots = scratch[1 : 1 + steps]
    norm_work, norm_slots = scratch[1 + steps : 3 + steps]
    core_send, core_recv, part_send, part_recv, norm_send, norm_recv = scratch[3 + steps : 9 + steps]
    swap_send, swap_recv, local_sem = scratch[9 + steps :]
    rows = work.shape[0] // chunks
    half, quarter = rows // 2, rows // 4
    own = lax.axis_index("expert")
    others = ring_peers(count)
    links = [first] + list(orders[0])
    dp_peers = [(axis, peer_index(axis, bit)[1]) for axis, bit in links if axis == "dp"]
    greet([("expert", index) for index in others] + dp_peers)

    swaps = []
    import os
    for step, index in enumerate(others):
        copy = remote(packed_ref.at[index], arrived_ref.at[own], swap_send.at[step], swap_recv.at[step], "expert", index)
        copy.start()
        swaps.append(copy)
    home = pltpu.make_async_copy(packed_ref.at[own], arrived_ref.at[own], local_sem.at[chunks])
    home.start()

    side0, peer0 = peer_index(*first)
    started = []
    norm_work[...] = norm_ref[...]

    def add_rows(offset, size, slot, target):
        block = min(size, 64)

        @pl.loop(0, size // block)
        def _(index):
            here = rows_of(offset + index * block, block)
            there = rows_of(index * block, block)
            target[here, :] = (work[here, :].astype(f32) + slot[there, :].astype(f32)).astype(bf16)

    state = {}

    def event(chunk, number):
        base = chunk * rows
        if number == 0:
            kept = base + side0 * half
            given = base + (1 - side0) * half
            load = pltpu.make_async_copy(dense_ref.at[rows_of(kept, half)], work.at[rows_of(kept, half)], local_sem.at[chunk])
            load.start()
            copy = remote(dense_ref.at[rows_of(given, half)], core_slots.at[chunk], core_send.at[chunk, 0], core_recv.at[chunk, 0], first[0], peer0)
            copy.start()
            started.append(copy)
            state[chunk] = dict(kept=kept, load=load, copy=copy)
        elif number <= 2 * steps + 1:
            for part in range(2):
                go_on(chunk, part, number - 1)
        if number == 2 * steps + 1:
            kept = state[chunk]["kept"]
            copy = remote(done.at[rows_of(kept, half)], done.at[rows_of(kept, half)], core_send.at[chunk, 1], core_recv.at[chunk, 1], first[0], peer0)
            copy.start()
            started.append(copy)
            state[chunk]["copy"] = copy
        if number == 2 * steps + 2:
            state[chunk]["copy"].wait_recv()
            store = pltpu.make_async_copy(done.at[pl.ds(base, rows)], sum_ref.at[pl.ds(base, rows)], local_sem.at[chunk])
            store.start()
            state[chunk]["store"] = store

    def go_on(chunk, part, step):
        here = state[chunk]
        if step == 0:
            if part == 0:
                here["load"].wait()
                here["copy"].wait_recv()
                add_rows(here["kept"], half, core_slots.at[chunk], work)
            offset = here["kept"] + part * quarter
        else:
            offset, size, copy, slot = here[part]
            copy.wait_recv()
            if step <= steps:
                add_rows(offset, size, slot, work if step < steps else done)
        if step < steps:
            axis, bit = orders[part][step]
            side, peer = peer_index(axis, bit)
            size = quarter >> (step + 1)
            slot = part_slots[step].at[chunk, part]
            given = offset + (1 - side) * size
            kept = offset + side * size
            copy = remote(work.at[rows_of(given, size)], slot, part_send.at[chunk, part, step], part_recv.at[chunk, part, step], axis, peer)
            copy.start()
            started.append(copy)
            here[part] = (kept, size, copy, slot)
        elif step < 2 * steps:
            back = 2 * steps - 1 - step
            axis, bit = orders[part][back]
            side, peer = peer_index(axis, bit)
            size = quarter >> (back + 1)
            if step > steps:
                offset = offset - here["side", part] * (size // 2)
            here["side", part] = side
            copy = remote(done.at[rows_of(offset, size)], done.at[rows_of(offset, size)], part_send.at[chunk, part, step], part_recv.at[chunk, part, step], axis, peer)
            copy.start()
            started.append(copy)
            here[part] = (offset, size, copy, None)

    norm_copy = None
    for tick in range(2 * steps + 2 + chunks):
        for chunk in range(chunks):
            number = tick - chunk
            if 0 <= number <= 2 * steps + 2:
                event(chunk, number)
        if tick <= len(links):
            if norm_copy is not None:
                norm_copy.wait()
                norm_work[...] += norm_slots[tick - 1]
                if tick == sum(axis == "dp" for axis, _ in links):
                    bias_out[...] = norm_work[8:16, :]
            if tick < len(links):
                axis, bit = links[tick]
                norm_copy = remote(norm_work, norm_slots.at[tick], norm_send.at[tick], norm_recv.at[tick], axis, peer_index(axis, bit)[1])
                norm_copy.start()
            else:
                norm_out[...] = norm_work[...]
    for copy in started:
        copy.wait_send()
    for copy in swaps:
        copy.wait()
    home.wait()
    for chunk in range(chunks):
        state[chunk]["store"].wait()


def finish(dense, norms, packed, dp_count):
    count = packed.shape[0]
    rows, width = dense.shape
    first, orders, chunks, _, _ = plan_orders(dp_count, count, rows, width)
    steps = len(orders[0])
    part = rows // chunks // 4
    return pl.pallas_call(
        functools.partial(finish_kernel, first, orders, chunks, count),
        in_specs=[
            pl.BlockSpec(memory_space=pl.ANY),
            pl.BlockSpec(memory_space=pltpu.VMEM),
            pl.BlockSpec(memory_space=pl.ANY),
        ],
        out_specs=[
            pl.BlockSpec(memory_space=pl.ANY),
            pl.BlockSpec(memory_space=pltpu.VMEM),
            pl.BlockSpec(memory_space=pltpu.VMEM),
            pl.BlockSpec(memory_space=pl.ANY),
        ],
        out_shape=[
            jax.ShapeDtypeStruct(dense.shape, bf16),
            jax.ShapeDtypeStruct(norms.shape, f32),
            jax.ShapeDtypeStruct((8, width), f32),
            jax.ShapeDtypeStruct(packed.shape, bf16),
        ],
        scratch_shapes=[pltpu.VMEM(dense.shape, bf16)] * 2 + [pltpu.VMEM((chunks, 2 * part, width), bf16)]
        + [pltpu.VMEM((chunks, 2, part >> (step + 1), width), bf16) for step in range(steps)]
        + [
            pltpu.VMEM(norms.shape, f32),
            pltpu.VMEM((steps + 1,) + norms.shape, f32),
            pltpu.SemaphoreType.DMA((chunks, 2)),
            pltpu.SemaphoreType.DMA((chunks, 2)),
            pltpu.SemaphoreType.DMA((chunks, 2, 2 * steps)),
            pltpu.SemaphoreType.DMA((chunks, 2, 2 * steps)),
            pltpu.SemaphoreType.DMA((steps + 1,)),
            pltpu.SemaphoreType.DMA((steps + 1,)),
            pltpu.SemaphoreType.DMA((count - 1,)),
            pltpu.SemaphoreType.DMA((count - 1,)),
            pltpu.SemaphoreType.DMA((chunks + 1,)),
        ],
        compiler_params=pltpu.CompilerParams(
            collective_id=7, has_side_effects=True, vmem_limit_bytes=BIG_VMEM
        ),
        cost_estimate=pl.CostEstimate(
            flops=2 * rows * width, bytes_accessed=8 * rows * width, transcendentals=0
        ),
    )(dense, norms, packed)


def pick(columns, numbers, table):
    return dot((columns == numbers).astype(bf16), table)


def joined_rows(columns, kept, arrived):
    places = lax.broadcasted_iota(jnp.int32, (1, arrived.shape[0]), 1)
    return pick(columns[:, 1:2], places, arrived[...]) + kept[...].astype(f32)


def near_numbers_of(rows):
    return jnp.where(rows < 0, -2, rows)


def near_kernel(columns, numbers, table, rows_ref):
    chosen = near_numbers_of(numbers[0:1, :])
    rows_ref[...] = pick(columns[:, 0:1], chosen, table[...]).astype(bf16)


def norm_parts(rows):
    centre = jnp.mean(rows, axis=-1, keepdims=True)
    centred = rows - centre
    inverse = lax.rsqrt(jnp.mean(centred * centred, axis=-1, keepdims=True) + epsilon)
    return centred * inverse, inverse


def norm_back(grad, scaled, inverse, gains):
    grad_scaled = grad * gains
    first = jnp.mean(grad_scaled, axis=-1, keepdims=True)
    second = jnp.mean(grad_scaled * scaled, axis=-1, keepdims=True)
    return inverse * (grad_scaled - first - scaled * second)


def third_kernel(far, kept, arrived, weight, rows_ref, product_ref):
    rows = joined_rows(far, kept, arrived).astype(bf16)
    rows_ref[...] = rows
    product_ref[...] = dot_last(rows, weight[...]).astype(bf16)


def last_kernel(far, kept, arrived, *rest):
    rows_ref = rest[len(rest) // 2]
    rows_ref[...] = joined_rows(far, kept, arrived).astype(bf16)
    for source, target in zip(rest[: len(rest) // 2], rest[len(rest) // 2 + 1 :]):
        target[...] = source[...].astype(f32)


def again_kernel(columns, kept, arrived, rows_ref):
    places = lax.broadcasted_iota(jnp.int32, (1, arrived.shape[0]), 1)
    rows = pick(columns[...], places, arrived[...]) + kept[...].astype(f32)
    rows_ref[...] = rows.astype(bf16)


def first_again_kernel(columns, kept, arrived, gain, bias, weight, rows_ref, normed_ref, mixed_ref, turned_ref):
    again_kernel(columns, kept, arrived, rows_ref)
    normed = (norm_parts(rows_ref[...].astype(f32))[0] * gain[...] + bias[...]).astype(bf16)
    normed_ref[...] = normed
    mixed_ref[...] = dot(normed, weight[...]).astype(bf16)
    turned_ref[...] = normed.T


def later_rows(step, table, source, target, chunk, expert_count):
    step, source, target = lax.optimization_barrier((step, source, target))
    source, target = (tuple(rows[part] for part in (0, 2, 3)) for rows in (source, target))
    packed = pack(table, source, chunk, expert_count, step)
    return remote_column(target, chunk, step)[:, None], exchange(packed, expert_count)


def more_rounds(kept, table, source, target, chunk, expert_count, rounds):
    def again(state):
        step, sums = state
        columns, arrived = later_rows(step, table, source, target, chunk, expert_count)
        (sums,) = join(again_kernel, [columns, sums], [arrived], (table.shape[1],))
        return (step + 1, sums)

    return lax.while_loop(lambda state: state[0] < rounds, again, (jnp.int32(1), kept))[1]


def more_first_rounds(kept, table, source, target, chunk, expert_count, rounds, gain, bias, weight):
    width = table.shape[1]

    def again(state):
        step, rows, *_ = state
        columns, arrived = later_rows(step, table, source, target, chunk, expert_count)
        rows, normed, mixed, turned = join(
            first_again_kernel, [columns, rows], [arrived, gain, bias, weight],
            (width, width, 3 * width), (width,),
        )
        return (step + 1, rows, normed, turned, mixed)

    return lax.while_loop(lambda state: state[0] < rounds, again, (jnp.int32(1), *kept))[1:]


def finish_rows(far, kept, arrived, sums):
    steps = 8

    def blocks(array):
        return pl.BlockSpec((array.shape[0] // steps, array.shape[1]), lambda step: (step, 0))

    count, width = kept.shape
    return pl.pallas_call(
        last_kernel,
        grid=(steps,),
        in_specs=[blocks(far), blocks(kept), in_full(arrived)] + [blocks(array) for array in sums],
        out_specs=[blocks(kept)] + [blocks(array) for array in sums],
        out_shape=[jax.ShapeDtypeStruct(kept.shape, bf16)]
        + [jax.ShapeDtypeStruct(array.shape, f32) for array in sums],
        compiler_params=pltpu.CompilerParams(vmem_limit_bytes=BIG_VMEM),
        cost_estimate=pl.CostEstimate(
            flops=2 * count * width * arrived.shape[0],
            bytes_accessed=4 * count * width + 6 * sum(array.size for array in sums),
            transcendentals=0,
        ),
    )(far, kept, arrived, *sums)


def block_rows(width):
    return pl.BlockSpec((256, width), lambda step: (step, 0))


def in_full(array):
    return pl.BlockSpec(array.shape, lambda step: (0,) * array.ndim, pipeline_mode=pl.Buffered(1))


def join(kernel, blocked, whole, widths, turned=()):
    count = blocked[0].shape[0]
    table = next(array for array in whole if array.dtype == bf16)
    inside, width = table.shape
    return pl.pallas_call(
        kernel,
        grid=(count // 256,),
        in_specs=[block_rows(array.shape[1]) for array in blocked]
        + [in_full(array) for array in whole],
        out_specs=[block_rows(size) for size in widths]
        + [pl.BlockSpec((size, 256), lambda step: (0, step)) for size in turned],
        out_shape=[jax.ShapeDtypeStruct((count, size), bf16) for size in widths]
        + [jax.ShapeDtypeStruct((size, count), bf16) for size in turned],
        compiler_params=pltpu.CompilerParams(vmem_limit_bytes=BIG_VMEM),
        cost_estimate=pl.CostEstimate(
            flops=2 * count * width * (inside + sum(widths) - width),
            bytes_accessed=2 * (inside * width + count * sum(widths)),
            transcendentals=0,
        ),
    )(*blocked, *whole)


def expert_kernel(
    columns, kept, grad_y, grad_act, arrived, gain, bias, bias_in, bias_out, weight_in_hbm, weight_out_hbm,
    out_ref, normed_ref, act_ref, grad_pre_ref, grad_ref, sum_ref, weight_in, weight_out, load_sem,
):
    hidden, width = weight_in.shape
    block = width
    loads = []
    for index, low in enumerate(range(0, hidden, block)):
        part = pl.ds(low, block)
        loads.append(
            [
                pltpu.make_async_copy(source.at[part], target.at[part], load_sem.at[index, side])
                for side, (source, target) in enumerate(
                    ((weight_in_hbm, weight_in), (weight_out_hbm, weight_out))
                )
            ]
        )

    def work(first):
        if first:
            for pair in loads:
                for copy in pair:
                    copy.start()
            sum_ref[...] = jnp.zeros_like(sum_ref)
        rows = joined_rows(columns, kept, arrived)
        scaled, inverse = norm_parts(rows)
        normed = (scaled * gain[...] + bias[...]).astype(bf16)
        normed_ref[...] = normed
        result = jnp.zeros(rows.shape, f32)
        grad = jnp.zeros(rows.shape, f32)
        for number, low in enumerate(range(0, hidden, block)):
            if first:
                for copy in loads[number]:
                    copy.wait()
            part = slice(low, low + block)
            pre = dot_last(normed, weight_in[part, :]) + bias_in[:, part]
            square = pre * pre
            tangent = jnp.tanh(gelu_c * (pre + 0.044715 * pre * square))
            half = 0.5 * pre
            act = (half + half * tangent).astype(bf16)
            slope = (0.5 + 0.5 * tangent) + half * (1.0 - tangent * tangent) * (
                gelu_c + (3.0 * 0.044715 * gelu_c) * square
            )
            grad_pre = (grad_act[:, part].astype(f32) * slope).astype(bf16)
            act_ref[:, part] = act
            grad_pre_ref[:, part] = grad_pre
            index = 8 + number
            sum_ref[index : index + 1, :] += jnp.sum(grad_pre.astype(f32), axis=0, keepdims=True)
            result += dot(act, weight_out[part, :])
            grad += dot(grad_pre, weight_in[part, :])
        out = rows + result + bias_out[...]
        out_ref[...] = jnp.where(columns[:, 4:5] > 0, out, 0.0).astype(bf16)
        grad_in = grad_y[...].astype(f32)
        grad_ref[...] = (grad_in + norm_back(grad, scaled, inverse, gain[...])).astype(bf16)
        sum_ref[2:3, :] += jnp.sum(grad * scaled, axis=0, keepdims=True)
        sum_ref[3:4, :] += jnp.sum(grad, axis=0, keepdims=True)
        sum_ref[12:13, :] += jnp.sum(grad_in, axis=0, keepdims=True)

    @pl.when(pl.program_id(0) == 0)
    def _():
        work(True)

    @pl.when(pl.program_id(0) > 0)
    def _():
        work(False)


def run_expert(blocked, whole, weights):
    count, width = blocked[1].shape
    hidden = weights[0].shape[0]
    widths = (width, width, hidden, hidden, width)
    return pl.pallas_call(
        expert_kernel,
        grid=(count // 256,),
        in_specs=[block_rows(array.shape[1]) for array in blocked]
        + [in_full(array) for array in whole]
        + [pl.BlockSpec(memory_space=pl.ANY)] * 2,
        out_specs=[block_rows(size) for size in widths]
        + [pl.BlockSpec((16, width), lambda step: (0, 0))],
        out_shape=[jax.ShapeDtypeStruct((count, size), bf16) for size in widths]
        + [jax.ShapeDtypeStruct((16, width), f32)],
        scratch_shapes=[pltpu.VMEM((hidden, width), bf16)] * 2
        + [pltpu.SemaphoreType.DMA((hidden // width, 2))],
        compiler_params=pltpu.CompilerParams(vmem_limit_bytes=58 << 20),
        cost_estimate=pl.CostEstimate(
            flops=6 * count * width * hidden,
            bytes_accessed=2 * count * (5 * width + 3 * hidden) + 4 * width * hidden,
            transcendentals=count * hidden,
        ),
    )(*blocked, *whole, *weights)


def backward_kernel(
    first, orders, along, count, pairs,
    q_ref, k_ref, v_ref, context_ref, grad_ref, logs_ref, wq_ref, wk_ref, wv_ref, dense_ref,
    normed_t, tokens_ref, hidden_ref, gain_ref, norm_ref, token_rows, slot_columns,
    mixed_sum, dense_sum, norm_out, bias_out, arrived_ref, near_ref, tokens_grad,
    work, done, core_slots, *scratch
):
    steps = len(orders[0])
    part_slots = scratch[:steps]
    (
        along_slots, pair_grad, grad_k, grad_v, total, packed, norm_work, norm_slots,
        core_send, core_recv, part_send, part_recv, along_send, along_recv,
        norm_send, norm_recv, swap_send, swap_recv, local_sem,
    ) = scratch[steps:]
    tick = pl.program_id(0)
    rows, width = work.shape[1], pairs * PAIR
    half, quarter = rows // 2, rows // 4
    own = lax.axis_index("expert")
    others = ring_peers(count)
    links = [first] + list(orders[0]) + [("expert", bit) for bit in along]
    link_peers = [(axis, peer_index(axis, bit)[1]) for axis, bit in links]
    events = 2 * steps + 4
    last = pairs + events // 2 - 1

    @pl.when(tick == 0)
    def _():
        greet([("expert", index) for index in others] + [peer for peer in link_peers if peer[0] == "dp"])

    side0, peer0 = peer_index(*first)
    offsets, sides, peers = [], [], []
    for part in range(2):
        offset = side0 * half + part * quarter
        at, side_list, peer_list = [offset], [], []
        for step, (axis, bit) in enumerate(orders[part]):
            side, peer = peer_index(axis, bit)
            offset = offset + side * (quarter >> (step + 1))
            at.append(offset)
            side_list.append(side)
            peer_list.append((axis, peer))
        offsets.append(at)
        sides.append(side_list)
        peers.append(peer_list)
    spread = 1 << len(along)
    place = (own // along[0]) % spread
    piece = quarter >> steps >> len(along)

    def core_give(chunk):
        given = rows_of((1 - side0) * half, half)
        return remote(work.at[chunk, given], core_slots.at[chunk], core_send.at[chunk, 0], core_recv.at[chunk, 0], first[0], peer0)

    def core_return(chunk):
        kept = rows_of(side0 * half, half)
        return remote(done.at[chunk, kept], done.at[chunk, kept], core_send.at[chunk, 1], core_recv.at[chunk, 1], first[0], peer0)

    def part_give(chunk, part, step):
        size = quarter >> (step + 1)
        given = rows_of(offsets[part][step] + (1 - sides[part][step]) * size, size)
        return remote(
            work.at[chunk, given], part_slots[step].at[chunk, part],
            part_send.at[chunk, part, step], part_recv.at[chunk, part, step], *peers[part][step]
        )

    def part_return(chunk, part, step):
        kept = rows_of(offsets[part][step + 1], quarter >> (step + 1))
        return remote(
            done.at[chunk, kept], done.at[chunk, kept],
            part_send.at[chunk, part, steps + step], part_recv.at[chunk, part, steps + step], *peers[part][step]
        )

    def along_copies(chunk, part, back):
        copies = []
        for turn in range(1, spread):
            there = lax.rem(place + turn, spread)
            index = turn - 1 + back * (spread - 1)
            if back:
                source = target = done.at[chunk, rows_of(offsets[part][steps] + place * piece, piece)]
            else:
                source = work.at[chunk, rows_of(offsets[part][steps] + there * piece, piece)]
                target = along_slots.at[chunk, part, turn - 1]
            copies.append(
                remote(
                    source, target, along_send.at[chunk, part, index], along_recv.at[chunk, part, index],
                    "expert", own + (there - place) * along[0]
                )
            )
        return copies

    def store(chunk):
        for part in range(4):
            source = done.at[chunk, :, part * PAIR : (part + 1) * PAIR]
            column = pl.ds(pl.multiple_of(chunk * PAIR + (part % 3) * width, PAIR), PAIR)
            target = mixed_sum if part < 3 else dense_sum
            yield pltpu.make_async_copy(source, target.at[:, column], local_sem.at[chunk, part])

    def add_rows(chunk, offset, size, slots, target):
        block = min(size, 64)

        @pl.loop(0, size // block)
        def _(index):
            here = rows_of(offset + index * block, block)
            there = rows_of(index * block, block)
            sums = work[chunk, here, :].astype(f32)
            for slot in slots:
                sums = sums + slot[there, :].astype(f32)
            target[chunk, here, :] = sums.astype(bf16)

    def event(chunk, number):
        if number == 1:
            core_give(chunk).wait_recv()
            add_rows(chunk, side0 * half, half, [core_slots.at[chunk]], work)
        for part in range(2):
            if 2 <= number <= steps + 1:
                step = number - 2
                part_give(chunk, part, step).wait_recv()
                add_rows(
                    chunk, offsets[part][step + 1], quarter >> (step + 1), [part_slots[step].at[chunk, part]], work
                )
            if number <= steps:
                part_give(chunk, part, number - 1).start()
            elif number == steps + 1:
                for copy in along_copies(chunk, part, 0):
                    copy.start()
            elif number == steps + 2:
                for copy in along_copies(chunk, part, 0):
                    copy.wait_recv()
                slots = [along_slots.at[chunk, part, turn] for turn in range(spread - 1)]
                add_rows(chunk, offsets[part][steps] + place * piece, piece, slots, done)
                for copy in along_copies(chunk, part, 1):
                    copy.start()
            elif number <= 2 * steps + 3:
                back = 2 * steps + 2 - number
                if back == steps - 1:
                    for copy in along_copies(chunk, part, 1):
                        copy.wait_recv()
                else:
                    part_return(chunk, part, back + 1).wait_recv()
                if back >= 0:
                    part_return(chunk, part, back).start()
        if number == 2 * steps + 3:
            core_return(chunk).start()
        if number == 2 * steps + 4:
            core_return(chunk).wait_recv()
            for copy in store(chunk):
                copy.start()

    def norm_step(step):
        return remote(norm_work.at[step], norm_slots.at[step], norm_send.at[step], norm_recv.at[step], *link_peers[step])

    def norm_event(step):
        norm_step(step).wait_recv()
        summed = norm_work[step] + norm_slots[step]
        if step + 1 < len(links):
            norm_work[step + 1] = summed
            norm_step(step + 1).start()
        else:
            norm_out[...] = summed
        if step + 1 == sum(axis == "dp" for axis, _ in links):
            bias_out[...] = summed[8:16]

    def run_events(side):
        for number in range(events, 0, -1):
            if (number + 1) % 2 == side:
                chunk = tick - (1 + number) // 2

                @pl.when((chunk >= 0) & (chunk < pairs))
                def _(number=number, chunk=chunk):
                    event(chunk, number)

        for step in range(len(links)):
            if step % 2 == side:

                @pl.when(tick == pairs + 1 + step // 2)
                def _(step=step):
                    norm_event(step)

    run_events(0)

    @pl.when(tick < pairs)
    def _():
        attend_back_pair(
            min(256, rows), q_ref, k_ref, v_ref, context_ref, grad_ref, logs_ref,
            pair_grad, grad_k, grad_v,
        )
        run_events(1)
        work[tick, :, : 3 * PAIR] = dot(normed_t[...], pair_grad[...]).astype(bf16)
        work[tick, :, 3 * PAIR :] = dense_ref[...]
        core_give(tick).start()
        weights = jnp.concatenate([wq_ref[...], wk_ref[...], wv_ref[...]], axis=1)

        @pl.when(tick == 0)
        def _():
            total[...] = dot_last(pair_grad[...], weights)

        @pl.when(tick > 0)
        def _():
            total[...] += dot_last(pair_grad[...], weights)

    pieces = swap_send.shape[1]
    piece_rows = packed.shape[1] // pieces

    def swap_rows(step, piece):
        index = others[step]
        here = pl.ds(piece * piece_rows, piece_rows)
        return remote(
            packed.at[index, here], arrived_ref.at[own, here],
            swap_send.at[step, piece], swap_recv.at[step, piece], "expert", index
        )

    def start_swaps(pieces):
        for piece in pieces:
            for step in range(count - 1):
                swap_rows(step, piece).start()

    def home_rows():
        return pltpu.make_async_copy(packed.at[own], arrived_ref.at[own], local_sem.at[pairs, 0])

    @pl.when(tick == pairs)
    def _():
        sums = [jnp.zeros((1, width), f32)] * 2
        for low in range(0, rows, 256):
            part = slice(low, low + 256)
            grad = total[part, :]
            scaled, inverse = norm_parts(tokens_ref[part, :].astype(f32))
            result = hidden_ref[part, :].astype(f32) + norm_back(grad, scaled, inverse, gain_ref[...])
            tokens_grad[part, :] = result.astype(bf16)
            sums[0] = sums[0] + jnp.sum(grad * scaled, axis=0, keepdims=True)
            sums[1] = sums[1] + jnp.sum(grad, axis=0, keepdims=True)
        norm_work[0] = norm_ref[...]
        norm_work[0, 0:1, :] = sums[0]
        norm_work[0, 1:2, :] = sums[1]
        norm_step(0).start()
        chunk = packed.shape[1]
        for index in range(count):
            numbers = index * chunk + lax.broadcasted_iota(jnp.int32, (chunk, 1), 0)
            packed[index] = dot((token_rows[1:2, :] == numbers).astype(bf16), tokens_grad[...]).astype(bf16)
        start_swaps([0])
        home_rows().start()

    @pl.when(tick == pairs + 2)
    def _():
        start_swaps([2])

    @pl.when(tick >= pairs)
    def _():
        run_events(1)

    @pl.when(tick == pairs + 1)
    def _():
        start_swaps([1])

    @pl.when(tick == pairs + 2)
    def _():
        start_swaps([3])

    @pl.when(tick == pairs + 2)
    def _():
        for low in range(0, near_ref.shape[0], 256):
            part = slice(low, low + 256)
            near_ref[part, :] = pick(slot_columns[part, 0:1], near_numbers_of(token_rows[0:1, :]), tokens_grad[...]).astype(bf16)

    @pl.when(tick == last)
    def _():
        @pl.loop(0, pairs)
        def _(chunk):
            core_give(chunk).wait_send()
            core_return(chunk).wait_send()
            for part in range(2):
                for step in range(steps):
                    part_give(chunk, part, step).wait_send()
                    part_return(chunk, part, step).wait_send()
                for back in range(2):
                    for copy in along_copies(chunk, part, back):
                        copy.wait_send()
            for copy in store(chunk):
                copy.wait()

        for step in range(len(links)):
            norm_step(step).wait_send()
        for piece in range(pieces):
            for step in range(count - 1):
                swap_rows(step, piece).wait()
        home_rows().wait()


def backward(mixed, context, grad_context, logs, weight, dense, normed_t, tokens, grad_hidden, gain, norms,
             token_rows, slot_columns, first, orders, along, count, chunk):
    length, width = context.shape
    pairs = width // PAIR
    steps = len(orders[0])
    links = 1 + steps + len(along)
    part = length // 4
    slots = slot_columns.shape[0]
    spread = 1 << len(along)

    def columns(offset):
        return pl.BlockSpec((length, PAIR), lambda tick: (0, offset + jnp.minimum(tick, pairs - 1)))

    def whole(array):
        return pl.BlockSpec(array.shape, lambda tick: (0,) * array.ndim, pipeline_mode=pl.Buffered(1))

    def result(shape):
        return pl.BlockSpec(shape, lambda tick: (0,) * len(shape))

    anywhere = pl.BlockSpec(memory_space=pl.ANY)
    fixed = (normed_t, tokens, grad_hidden, gain, norms, token_rows, slot_columns)
    dma = pltpu.SemaphoreType.DMA
    return pl.pallas_call(
        functools.partial(backward_kernel, first, orders, along, count, pairs),
        grid=(pairs + steps + 2,),
        in_specs=[columns(0), columns(pairs), columns(2 * pairs), columns(0), columns(0)]
        + [pl.BlockSpec((1, 8, length), lambda tick: (jnp.minimum(tick, pairs - 1), 0, 0))]
        + [columns(0), columns(pairs), columns(2 * pairs), columns(0)]
        + [whole(array) for array in fixed],
        out_specs=[
            anywhere, anywhere, result(norms.shape), result((8, width)), anywhere,
            result((slots, width)), result((length, width)),
        ],
        out_shape=[
            jax.ShapeDtypeStruct((length, 3 * width), bf16),
            jax.ShapeDtypeStruct((length, width), bf16),
            jax.ShapeDtypeStruct(norms.shape, f32),
            jax.ShapeDtypeStruct((8, width), f32),
            jax.ShapeDtypeStruct((count, chunk, width), bf16),
            jax.ShapeDtypeStruct((slots, width), bf16),
            jax.ShapeDtypeStruct((length, width), bf16),
        ],
        scratch_shapes=[pltpu.VMEM((pairs, length, 4 * PAIR), bf16)] * 2
        + [pltpu.VMEM((pairs, length // 2, 4 * PAIR), bf16)]
        + [pltpu.VMEM((pairs, 2, part >> (step + 1), 4 * PAIR), bf16) for step in range(steps)]
        + [
            pltpu.VMEM((pairs, 2, spread - 1, part >> steps >> len(along), 4 * PAIR), bf16),
            pltpu.VMEM((length, 3 * PAIR), bf16),
            pltpu.VMEM((length, PAIR), f32),
            pltpu.VMEM((length, PAIR), f32),
            pltpu.VMEM((length, width), f32),
            pltpu.VMEM((count, chunk, width), bf16),
            pltpu.VMEM((links,) + norms.shape, f32),
            pltpu.VMEM((links,) + norms.shape, f32),
            dma((pairs, 2)),
            dma((pairs, 2)),
            dma((pairs, 2, 2 * steps)),
            dma((pairs, 2, 2 * steps)),
            dma((pairs, 2, 2 * (spread - 1))),
            dma((pairs, 2, 2 * (spread - 1))),
            dma((links,)),
            dma((links,)),
            dma((count - 1, 4)),
            dma((count - 1, 4)),
            dma((pairs + 1, 4)),
        ],
        compiler_params=pltpu.CompilerParams(
            collective_id=7, has_side_effects=True, vmem_limit_bytes=61 << 20
        ),
        cost_estimate=pl.CostEstimate(
            flops=10 * length * length * width, bytes_accessed=32 * length * width,
            transcendentals=length * length * width // HEAD_DIM,
        ),
    )(mixed, mixed, mixed, context, grad_context, logs, weight, weight, weight, dense, *fixed)


def begin_kernel(
    count, chunk, dp_count, ids_ref, table_hbm, gain_ref, bias_ref, weight_hbm,
    token_columns, slot_columns, token_rows, slot_rows, info_ref, rows_out, normed_out, turned_out, mixed_out,
    ids_all, table, weight, packed, arrived, near, rows_work, normed_work, turned_work, mixed_work, most_work, most_slots,
    ids_send, ids_recv, swap_send, swap_recv, most_send, most_recv, local_sem, out_sem,
):
    own = lax.axis_index("expert")
    others = ring_peers(count)
    load = pltpu.make_async_copy(table_hbm, table, local_sem.at[0])
    load.start()
    load_weight = pltpu.make_async_copy(weight_hbm, weight, local_sem.at[1])
    load_weight.start()
    dp_own = lax.axis_index("dp")
    dp_others = [lax.rem(dp_own + step, dp_count) for step in range(1, dp_count)]
    greet([("expert", index) for index in others] + [("dp", index) for index in dp_others])
    sends = [
        remote(ids_ref, ids_all.at[own], ids_send.at[step], ids_recv.at[step], "expert", index)
        for step, index in enumerate(others)
    ]
    for copy in sends:
        copy.start()
    ids_all[own] = ids_ref[...]
    length, slots = ids_ref.shape[1], table.shape[0]
    earlier = lax.broadcasted_iota(jnp.int32, (length, length), 0) < lax.broadcasted_iota(
        jnp.int32, (length, length), 1
    )
    earlier = earlier.astype(bf16)
    for copy in sends:
        copy.wait()

    own_f = own.astype(f32)
    rows = [ids_all[index] for index in range(count)]
    ids = jnp.concatenate(rows, axis=0).astype(f32)
    lane = lax.broadcasted_iota(jnp.int32, (count, 128), 1).astype(f32)
    sequence = lax.broadcasted_iota(jnp.int32, (count, 1), 0).astype(f32)
    counts = jnp.zeros((count, 128), f32)
    for expert in range(count):
        taken = jnp.sum((ids == float(expert)).astype(f32), axis=1, keepdims=True)
        counts = jnp.where(lane == float(expert), taken, counts)
    fullest = (counts == jnp.max(counts, axis=0, keepdims=True)) & (lane < float(count))
    fullest = fullest.astype(f32)
    peaks = jnp.sum(fullest, axis=1, keepdims=True)
    single = (jnp.max(peaks, axis=0, keepdims=True) == 1.0) & (jnp.min(peaks, axis=0, keepdims=True) == 1.0)
    owner = jnp.where(single, jnp.sum(fullest * lane, axis=1, keepdims=True), sequence)
    from_each = jnp.sum(jnp.where(lane == own_f, counts, 0.0), axis=1, keepdims=True)
    as_row = jnp.sum(jnp.where(lane == sequence, from_each, 0.0), axis=0, keepdims=True)
    starts = jnp.sum(jnp.where(lane < sequence, as_row, 0.0), axis=1, keepdims=True)
    away = jnp.max(jnp.where(lane == owner, 0.0, counts), axis=1, keepdims=True)
    most = jnp.max(away, axis=0, keepdims=True)
    at_device = lane == owner
    device_starts = jnp.sum(jnp.where(at_device, starts, 0.0), axis=0, keepdims=True)
    limits = jnp.where(owner == own_f, 0.0, from_each)
    device_limits = jnp.sum(jnp.where(at_device, limits, 0.0), axis=0, keepdims=True)
    most_work[...] = jnp.broadcast_to(most, (8, 128))
    mosts = [
        remote(most_work, most_slots.at[step], most_send.at[step], most_recv.at[step], "dp", index)
        for step, index in enumerate(dp_others)
    ]
    for copy in mosts:
        copy.start()

    def places(inside, home, device, rank):
        near = jnp.where(inside & home, rank, -1.0)
        there = inside & ~home
        far = jnp.where(there & (rank < float(chunk)), device * float(chunk) + rank, -1.0)
        rank = jnp.where(there, rank, -float(chunk))
        empty = jnp.zeros((3, rank.shape[1]), f32)
        return jnp.concatenate([near, far, device, rank, inside.astype(f32), empty], axis=0)

    slot = lax.broadcasted_iota(jnp.int32, (1, slots), 1).astype(f32)
    used = jnp.zeros((1, slots), f32)
    slot_rank = jnp.zeros((1, slots), f32)
    slot_device = jnp.zeros((1, slots), f32)
    for index in range(count):
        start = starts[index : index + 1]
        inside = (slot >= start) & (slot < start + from_each[index : index + 1])
        used = jnp.where(inside, 1.0, used)
        slot_rank = jnp.where(inside, slot - start, slot_rank)
        slot_device = jnp.where(inside, owner[index : index + 1], slot_device)
    slot_places = places(used > 0.0, slot_device == own_f, slot_device, slot_rank)
    far_slots = slot_places[1:2]

    load.wait()
    swaps = []
    for step, index in enumerate(others):
        numbers = index * chunk + lax.broadcasted_iota(jnp.int32, (chunk, 1), 0)
        chosen = (far_slots == numbers.astype(f32)).astype(bf16)
        packed[step] = dot(chosen, table[...]).astype(bf16)
        copy = remote(packed.at[step], arrived.at[own], swap_send.at[step], swap_recv.at[step], "expert", index)
        copy.start()
        swaps.append(copy)
    arrived[own] = jnp.zeros(packed.shape[1:], bf16)

    held = jnp.zeros((1, length), f32)
    for index in range(count):
        held = jnp.where(owner[index : index + 1] == own_f, rows[index].astype(f32), held)
    expert = lax.broadcasted_iota(jnp.int32, (16, 1), 0).astype(f32)
    choose = (held == expert).astype(f32)
    before = dot(choose.astype(bf16), earlier)
    token_rank = jnp.sum(choose * before, axis=0, keepdims=True)
    token_places = places(held >= 0.0, held == own_f, held, token_rank)
    slot_rows[...] = slot_places.astype(jnp.int32)
    token_rows[...] = token_places.astype(jnp.int32)
    slot_turned = slot_places.T
    token_turned = token_places.T
    slot_columns[...] = slot_turned.astype(jnp.int32)
    token_columns[...] = token_turned.astype(jnp.int32)
    near_slots = jnp.where(slot_places[0:1] < 0.0, -2.0, slot_places[0:1])
    for low in range(0, length, 256):
        part = slice(low, low + 256)
        near[part, :] = pick(token_turned[part, 0:1], near_slots, table[...]).astype(bf16)
    for copy in mosts:
        copy.wait()
    overall = most_work[0:1, :]
    for step in range(dp_count - 1):
        overall = jnp.maximum(overall, most_slots[step, 0:1, :])
    blank = jnp.zeros((5, 128), f32)
    info = jnp.concatenate([overall, device_starts, device_limits, blank], axis=0)
    info_ref[...] = info.astype(jnp.int32)
    load_weight.wait()
    for copy in swaps:
        copy.wait()
    far_places = lax.broadcasted_iota(jnp.int32, (1, count * chunk), 1).astype(f32)
    stores = []
    for index, low in enumerate(range(0, length, 256)):
        part = slice(low, low + 256)
        there = (token_turned[part, 1:2] == far_places).astype(bf16)
        got = near[part, :].astype(f32)
        for source in range(count):
            got = got + dot(there[:, source * chunk : (source + 1) * chunk], arrived[source])
        normed = (norm_parts(got)[0] * gain_ref[...] + bias_ref[...]).astype(bf16)
        rows_work[part, :] = got.astype(bf16)
        normed_work[part, :] = normed
        turned_work[:, part] = normed.T
        mixed_work[part, :] = dot(normed, weight[...]).astype(bf16)
        here = pl.ds(low, 256)
        for number, (source, target) in enumerate(
            ((rows_work, rows_out), (normed_work, normed_out), (mixed_work, mixed_out))
        ):
            stores.append(pltpu.make_async_copy(source.at[here], target.at[here], out_sem.at[index, number]))
            stores[-1].start()
        stores.append(pltpu.make_async_copy(turned_work.at[:, here], turned_out.at[:, here], out_sem.at[index, 3]))
        stores[-1].start()
    for copy in stores:
        copy.wait()


def begin(ids, table, gain, bias, weight, count, chunk, dp_count):
    length = ids.shape[0]
    slots, width = table.shape
    vmem = pl.BlockSpec(memory_space=pltpu.VMEM)
    anywhere = pl.BlockSpec(memory_space=pl.ANY)
    whole = jax.ShapeDtypeStruct
    dma = pltpu.SemaphoreType.DMA
    return pl.pallas_call(
        functools.partial(begin_kernel, count, chunk, dp_count),
        in_specs=[vmem, anywhere, vmem, vmem, anywhere],
        out_specs=[vmem] * 5 + [anywhere] * 4,
        out_shape=[
            whole((length, 8), jnp.int32),
            whole((slots, 8), jnp.int32),
            whole((8, length), jnp.int32),
            whole((8, slots), jnp.int32),
            whole((8, 128), jnp.int32),
            whole((length, width), bf16),
            whole((length, width), bf16),
            whole((width, length), bf16),
            whole((length, 3 * width), bf16),
        ],
        scratch_shapes=[
            pltpu.VMEM((count, 1, length), jnp.int32),
            pltpu.VMEM((slots, width), bf16),
            pltpu.VMEM(weight.shape, bf16),
            pltpu.VMEM((count - 1, chunk, width), bf16),
            pltpu.VMEM((count, chunk, width), bf16),
            pltpu.VMEM((length, width), bf16),
            pltpu.VMEM((length, width), bf16),
            pltpu.VMEM((length, width), bf16),
            pltpu.VMEM((width, length), bf16),
            pltpu.VMEM((length, 3 * width), bf16),
            pltpu.VMEM((8, 128), f32),
            pltpu.VMEM((dp_count - 1, 8, 128), f32),
            dma((count - 1,)),
            dma((count - 1,)),
            dma((count - 1,)),
            dma((count - 1,)),
            dma((dp_count - 1,)),
            dma((dp_count - 1,)),
            dma((2,)),
            dma((length // 256, 4)),
        ],
        compiler_params=pltpu.CompilerParams(
            collective_id=5, has_side_effects=True, vmem_limit_bytes=BIG_VMEM
        ),
        cost_estimate=pl.CostEstimate(
            flops=12 * length * slots * width, bytes_accessed=8 * slots * width, transcendentals=0
        ),
    )(ids[None, :], table, gain, bias, weight)


def back_kernel(grad_ref, weight_ref, tokens_ref, hidden_ref, gain_ref, out_ref, sum_ref):
    width = gain_ref.shape[1]
    grad = sum(
        dot_last(grad_ref[part], weight_ref[:, part * width : (part + 1) * width])
        for part in range(3)
    )
    scaled, inverse = norm_parts(tokens_ref[...].astype(f32))
    result = hidden_ref[...].astype(f32) + norm_back(grad, scaled, inverse, gain_ref[...])
    out_ref[...] = result.astype(bf16)

    @pl.when(pl.program_id(0) == 0)
    def _():
        sum_ref[...] = jnp.zeros_like(sum_ref)

    sum_ref[0:1, :] += jnp.sum(grad * scaled, axis=0, keepdims=True)
    sum_ref[1:2, :] += jnp.sum(grad, axis=0, keepdims=True)


def back(grad_mixed, weight, tokens, grad_hidden, gain):
    count, width = tokens.shape
    block = 256

    def by_rows():
        return pl.BlockSpec((block, width), lambda step: (step, 0))

    return pl.pallas_call(
        back_kernel,
        grid=(count // block,),
        in_specs=[
            pl.BlockSpec((3, block, width), lambda step: (0, step, 0)),
            pl.BlockSpec(weight.shape, lambda step: (0, 0)),
            by_rows(),
            by_rows(),
            pl.BlockSpec((1, width), lambda step: (0, 0)),
        ],
        out_specs=[by_rows(), pl.BlockSpec((8, width), lambda step: (0, 0))],
        out_shape=[
            jax.ShapeDtypeStruct((count, width), bf16),
            jax.ShapeDtypeStruct((8, width), f32),
        ],
        compiler_params=pltpu.CompilerParams(vmem_limit_bytes=BIG_VMEM),
        cost_estimate=pl.CostEstimate(
            flops=6 * count * width * width, bytes_accessed=20 * count * width, transcendentals=0
        ),
    )(grad_mixed, weight, tokens, grad_hidden, gain)


def body(
    block_input,
    expert_ids,
    ln1_gain,
    ln1_bias,
    w_qkv,
    w_o,
    ln2_gain,
    ln2_bias,
    w_in,
    b_in,
    w_out,
    b_out,
    cotangent,
):
    expert_count = lax.axis_size("expert")
    model_width = block_input.shape[2]
    seq_ids = expert_ids[0]
    seq_length = seq_ids.shape[0]
    chunk = seq_length // expert_count
    dp_index = lax.axis_index("dp")
    dp_count = lax.axis_size("dp")

    def row(values):
        return values.astype(f32).reshape(1, -1)

    token_columns, slot_columns, token_rows, slot_rows, info, *first_rows = begin(
        seq_ids, block_input[0], row(ln1_gain), row(ln1_bias), w_qkv, expert_count, chunk, dp_count
    )
    rounds = (info[0, 0] + chunk - 1) // chunk
    token_places = tuple(token_rows[part] for part in (0, 2, 3))
    token_side = (token_rows, token_columns)
    slot_side = (slot_rows, slot_columns)
    device_starts, device_limits = info[1, :expert_count], info[2, :expert_count]

    def start(table):
        return exchange(pack(table, token_places, chunk, expert_count), expert_count)

    def start_slots(table):
        packed = pack_slots(table, device_starts, device_limits, chunk)
        return exchange(packed, expert_count)

    def near_rows(table, source, target):
        (rows,) = join(near_kernel, [target[1]], [source[0], table], (model_width,))
        return rows

    def sides(kept, table, source, target):
        kept = more_rounds(kept, table, source[0], target[0], chunk, expert_count, rounds)
        return [target[1], kept]

    full_in = lax.all_gather(w_in[0], "dp", axis=0, tiled=True)
    full_out = lax.all_gather(w_out[0], "dp", axis=0, tiled=True)

    tokens_in, normed_low, normed_t, mixed_qkv = more_first_rounds(
        first_rows, block_input[0], slot_rows, token_rows, chunk, expert_count, rounds,
        row(ln1_gain), row(ln1_bias), w_qkv,
    )
    context_low, log_totals = attend(mixed_qkv)
    hidden = (tokens_in.astype(f32) + dot(context_low, w_o)).astype(bf16)
    late, b_in, b_out, hidden = lax.optimization_barrier((cotangent[0], b_in, b_out, hidden))
    arrived = start(hidden)
    grad_low = jnp.where(slot_columns[:, 4:5] > 0, late, jnp.zeros((), jnp.bfloat16))
    grad_act = dot_last(grad_low, full_out).astype(bf16)
    biases = jnp.concatenate([b_in, b_out], axis=1)
    for axis, bit in bits_of("dp"):
        got = swap(biases, axis, bit)
        upper = (dp_index // bit) % 2 == 1
        biases = jnp.where(
            upper, jnp.concatenate([got, biases]), jnp.concatenate([biases, got])
        )
    hidden_part = b_in.shape[1]
    full_bias_in = row(biases[:, :hidden_part])
    full_bias_out = row(biases[:, hidden_part:])
    near = near_rows(hidden, token_side, slot_side)
    arrived, grad_act, near = lax.optimization_barrier((arrived, grad_act, near))
    result, normed_two, act_low, grad_pre, grad_placed, norms = run_expert(
        sides(near, hidden, token_side, slot_side) + [grad_low, grad_act],
        [arrived, row(ln2_gain), row(ln2_bias), full_bias_in, full_bias_out],
        [full_in, full_out],
    )
    arrived = start_slots(grad_placed)
    local_w_in = dot_first(grad_pre, normed_two).astype(bf16)
    local_w_out = dot_first(act_low, grad_low).astype(bf16)
    near = near_rows(grad_placed, slot_side, token_side)
    arrived, near, local_w_in, local_w_out = lax.optimization_barrier(
        (arrived, near, local_w_in, local_w_out)
    )
    sum_in = lax.psum_scatter(local_w_in, "dp", scatter_dimension=0, tiled=True)
    sum_out = lax.psum_scatter(local_w_out, "dp", scatter_dimension=0, tiled=True)
    grad_hidden, grad_context = join(
        third_kernel,
        sides(near, grad_placed, slot_side, token_side),
        [arrived, w_o],
        (model_width, model_width),
    )
    local_w_o = dot_first(context_low, grad_hidden).astype(bf16)
    first, orders, _, short, along = plan_orders(
        dp_count, expert_count, 4 * model_width, model_width
    )
    if (seq_length // 4) >> len(orders[0]) >= 16:
        mixed_sum, dense_sum, norms, bias_sums, arrived, near, grad_tokens = backward(
            mixed_qkv, context_low, grad_context, log_totals, w_qkv, local_w_o, normed_t,
            tokens_in, grad_hidden, row(ln1_gain), norms,
            token_rows, slot_columns,
            first, short, along, expert_count, chunk,
        )
    else:
        grad_mixed = attend_back(mixed_qkv, context_low, grad_context, log_totals)
        grad_tokens, sums_one = back(grad_mixed, w_qkv, tokens_in, grad_hidden, row(ln1_gain))
        packed = pack(grad_tokens, token_places, chunk, expert_count)
        dense = jnp.concatenate(
            [dot_first(normed_low, grad_mixed[part]).astype(bf16) for part in range(3)]
            + [local_w_o]
        )
        norms = norms.at[:2].set(sums_one[:2])
        summed, norms, bias_sums, arrived = finish(
            dense, norms, packed.reshape(expert_count, chunk, model_width), dp_count
        )
        near = near_rows(grad_tokens, token_side, slot_side)
        mixed_sum = jnp.concatenate(
            [summed[part * model_width : (part + 1) * model_width] for part in range(3)], axis=1
        )
        dense_sum = summed[3 * model_width :]
    arrived = arrived.reshape(-1, model_width)
    grad_input, grad_w_qkv, grad_w_o, grad_w_in, grad_w_out = finish_rows(
        slot_columns, near, arrived, [mixed_sum, dense_sum, sum_in, sum_out]
    )
    grad_input = more_rounds(
        grad_input, grad_tokens, token_rows, slot_rows, chunk, expert_count, rounds
    )
    grad_ln1_gain, grad_ln1_bias, grad_ln2_gain, grad_ln2_bias = norms[:4]
    full_parts = bias_sums[:4].reshape(dp_count, -1)
    grad_b_in = lax.dynamic_index_in_dim(full_parts, dp_index, 0, keepdims=False)
    grad_b_out = lax.dynamic_index_in_dim(
        bias_sums[4].reshape(dp_count, -1), dp_index, 0, keepdims=False
    )
    return (
        result[None],
        grad_input[None],
        grad_ln1_gain,
        grad_ln1_bias,
        grad_w_qkv,
        grad_w_o,
        grad_ln2_gain,
        grad_ln2_bias,
        grad_w_in[None],
        grad_b_in[None],
        grad_w_out[None],
        grad_b_out[None],
    )


def solution(mesh):
    placed = (
        P("dp", "expert", None),
        P("dp", "expert"),
        P(),
        P(),
        P(),
        P(),
        P(),
        P(),
        P("expert", "dp", None),
        P("expert", "dp"),
        P("expert", "dp", None),
        P("expert", "dp"),
        P("dp", "expert", None),
    )
    return jax.shard_map(
        body,
        mesh=mesh,
        in_specs=placed,
        out_specs=(
            P("dp", "expert", None),
            P("dp", "expert", None),
            P(),
            P(),
            P(),
            P(),
            P(),
            P(),
            P("expert", "dp", None),
            P("expert", "dp"),
            P("expert", "dp", None),
            P("expert", "dp"),
        ),
        check_vma=False,
    )
```

```python
import functools

import jax
import jax.numpy as jnp
from jax import lax
from jax.experimental import pallas as pl
from jax.experimental.pallas import tpu as pltpu
from jax.sharding import PartitionSpec as P

HEADS = 16
HEAD_DIM = 64


epsilon = 1e-05
gelu_c = 0.7978845608028654
contract_last = (((1,), (1,)), ((), ()))
contract_first = (((0,), (0,)), ((), ()))


bf16 = jnp.bfloat16
PAIR = 2 * HEAD_DIM
BIG_VMEM = 48 << 20
FULL_VMEM = 60 << 20
f32 = jnp.float32


def dot(left, right):
    return jnp.dot(left, right, preferred_element_type=f32)


def dot_last(left, right):
    return lax.dot_general(left, right, contract_last, preferred_element_type=f32)


def dot_first(left, right):
    return lax.dot_general(left, right, contract_first, preferred_element_type=f32)


def head_parts(pair):
    first = lax.broadcasted_iota(jnp.int32, (1, PAIR), 1) < HEAD_DIM
    zero = jnp.zeros_like(pair)
    return [jnp.where(first, pair, zero), jnp.where(first, zero, pair)]


def attend_kernel(block, q_ref, k_ref, v_ref, context_ref, logs_ref):
    length = q_ref.shape[0]
    keys = head_parts(k_ref[...])
    values_t = v_ref[...].T
    rows = lax.broadcasted_iota(jnp.int32, (block, block), 0)
    cols = lax.broadcasted_iota(jnp.int32, (block, block), 1)
    allowed = rows <= cols
    for low in range(0, length, block):
        high = low + block
        queries = q_ref[low:high, :] * jnp.asarray(0.125, bf16)
        outputs = []
        for head in range(2):
            value_rows = values_t[head * HEAD_DIM : (head + 1) * HEAD_DIM]
            near = jnp.where(allowed, dot_last(keys[head][low:high], queries), -1e30)
            peak = jnp.max(near, axis=0, keepdims=True)
            if low:
                far = dot_last(keys[head][:low], queries)
                peak = jnp.maximum(peak, jnp.max(far, axis=0, keepdims=True))
            near = jnp.exp(near - peak)
            total = jnp.sum(near, axis=0, keepdims=True)
            result = dot(value_rows[:, low:high], near.astype(bf16))
            if low:
                far = jnp.exp(far - peak)
                total = total + jnp.sum(far, axis=0, keepdims=True)
                result = result + dot(value_rows[:, :low], far.astype(bf16))
            outputs.append(result / total)
            logs_ref[0, head : head + 1, low:high] = peak + jnp.log(total)
        context_ref[low:high, :] = jnp.concatenate(outputs, axis=0).T.astype(bf16)


def pair_columns(length, offset):
    return pl.BlockSpec((length, PAIR), lambda pair: (0, offset + pair))


def pair_logs(length):
    return pl.BlockSpec((1, 8, length), lambda pair: (pair, 0, 0))


def attend(mixed):
    length, width = mixed.shape[0], mixed.shape[1] // 3
    pairs = width // PAIR
    return pl.pallas_call(
        functools.partial(attend_kernel, min(1024, length)),
        grid=(pairs,),
        in_specs=[pair_columns(length, part * pairs) for part in range(3)],
        out_specs=[pair_columns(length, 0), pair_logs(length)],
        out_shape=[
            jax.ShapeDtypeStruct((length, width), bf16),
            jax.ShapeDtypeStruct((pairs, 8, length), f32),
        ],
        compiler_params=pltpu.CompilerParams(vmem_limit_bytes=BIG_VMEM),
        cost_estimate=pl.CostEstimate(
            flops=4 * length * length * width,
            bytes_accessed=8 * length * width,
            transcendentals=length * length * width // HEAD_DIM,
        ),
    )(mixed, mixed, mixed)


def attend_back_pair(
    block, q_ref, k_ref, v_ref, context_ref, grad_ref, logs_ref, out_ref, grad_k, grad_v
):
    length = q_ref.shape[0]
    keys, values, grads = k_ref[...], v_ref[...], grad_ref[...]
    queries = head_parts(q_ref[...] * jnp.asarray(0.125, bf16))
    key_parts = head_parts(keys)
    grad_parts = head_parts(grads)
    products = head_parts(grads.astype(f32) * context_ref[...].astype(f32))
    centres = [jnp.sum(part, axis=1, keepdims=True) for part in products]
    logs = logs_ref[0].T
    rows = lax.broadcasted_iota(jnp.int32, (block, block), 0)
    cols = lax.broadcasted_iota(jnp.int32, (block, block), 1)
    allowed = cols <= rows
    for low in reversed(range(0, length, block)):
        high = low + block
        add_q, add_k, add_v = [], [], []
        for head in range(2):
            scores = dot_last(queries[head][low:high], keys[:high])
            probs = jnp.exp(scores - logs[low:high, head : head + 1])
            near = jnp.where(allowed, probs[:, low:], 0.0)
            probs = jnp.concatenate([probs[:, :low], near], axis=1) if low else near
            grad_probs = dot_last(grad_parts[head][low:high], values[:high])
            grad_scores = (probs * (grad_probs - centres[head][low:high])).astype(bf16)
            add_q.append(dot(grad_scores, key_parts[head][:high]))
            add_k.append(dot_first(grad_scores, queries[head][low:high]))
            add_v.append(dot_first(probs.astype(bf16), grad_parts[head][low:high]))
        out_ref[low:high, :PAIR] = ((add_q[0] + add_q[1]) * 0.125).astype(bf16)
        if high == length:
            grad_k[...] = add_k[0] + add_k[1]
            grad_v[...] = add_v[0] + add_v[1]
        else:
            grad_k[:high, :] += add_k[0] + add_k[1]
            grad_v[:high, :] += add_v[0] + add_v[1]
    out_ref[:, PAIR : 2 * PAIR] = grad_k[...].astype(bf16)
    out_ref[:, 2 * PAIR :] = grad_v[...].astype(bf16)


def attend_back_kernel(block, *refs):
    out_ref, pair_grad, grad_k, grad_v = refs[6:]
    attend_back_pair(block, *refs[:6], pair_grad, grad_k, grad_v)
    for part in range(3):
        out_ref[part] = pair_grad[:, part * PAIR : (part + 1) * PAIR]


def attend_back(mixed, context, grad_context, logs):
    length, width = context.shape
    pairs = width // PAIR
    return pl.pallas_call(
        functools.partial(attend_back_kernel, min(256, length)),
        grid=(pairs,),
        in_specs=[pair_columns(length, part * pairs) for part in range(3)]
        + [pair_columns(length, 0)] * 2
        + [pair_logs(length)],
        out_specs=pl.BlockSpec((3, length, PAIR), lambda pair: (0, 0, pair)),
        out_shape=jax.ShapeDtypeStruct((3, length, width), bf16),
        scratch_shapes=[pltpu.VMEM((length, 3 * PAIR), bf16)]
        + [pltpu.VMEM((length, PAIR), f32)] * 2,
        compiler_params=pltpu.CompilerParams(vmem_limit_bytes=BIG_VMEM),
        cost_estimate=pl.CostEstimate(
            flops=10 * length * length * width,
            bytes_accessed=16 * length * width,
            transcendentals=length * length * width // HEAD_DIM,
        ),
    )(mixed, mixed, mixed, context, grad_context, logs)


def place_rows(columns, count, table):
    chosen = (columns[None, :] == jnp.arange(count, dtype=jnp.int32)[:, None]).astype(bf16)
    return dot(chosen, table).astype(bf16)


def exchange(packed, expert_count):
    return lax.all_to_all(
        packed.reshape(expert_count, -1, packed.shape[-1]),
        "expert",
        split_axis=0,
        concat_axis=0,
        tiled=True,
    ).reshape(-1, packed.shape[-1])


def remote_column(places, chunk, step):
    device, rank = places[1:]
    return jnp.where(rank // chunk == step, device * chunk + rank % chunk, -1)


def pack(table, places, chunk, expert_count, step=0):
    return place_rows(remote_column(places, chunk, step), expert_count * chunk, table)


def pack_slots_kernel(starts, limits, table_ref, out_ref):
    index = pl.program_id(0)
    rows, window = out_ref.shape[0], min(256, table_ref.shape[0])
    start = starts[index]
    base = jnp.minimum(start // 16 * 16, table_ref.shape[0] - window)
    rank = lax.broadcasted_iota(jnp.int32, (rows, window), 0)
    place = lax.broadcasted_iota(jnp.int32, (rows, window), 1)
    chosen = (place == rank + (start - base)) & (rank < limits[index])
    near = table_ref[pl.ds(pl.multiple_of(base, 16), window), :]
    out_ref[...] = dot(chosen.astype(bf16), near).astype(bf16)


def pack_slots(table, starts, limits, chunk):
    count, width = starts.shape[0], table.shape[1]
    return pl.pallas_call(
        pack_slots_kernel,
        grid_spec=pltpu.PrefetchScalarGridSpec(
            num_scalar_prefetch=2,
            grid=(count,),
            in_specs=[
                pl.BlockSpec(
                    table.shape, lambda index, *_: (0, 0), pipeline_mode=pl.Buffered(1)
                )
            ],
            out_specs=pl.BlockSpec((chunk, width), lambda index, *_: (index, 0)),
        ),
        out_shape=jax.ShapeDtypeStruct((count * chunk, width), bf16),
        compiler_params=pltpu.CompilerParams(vmem_limit_bytes=BIG_VMEM),
        cost_estimate=pl.CostEstimate(
            flops=512 * count * chunk * width, bytes_accessed=2 * table.size, transcendentals=0
        ),
    )(starts, limits, table)


def swap(values, axis, bit):
    size = lax.axis_size(axis)
    return lax.ppermute(values, axis, [(i, i ^ bit) for i in range(size)])


def bits_of(axis, size=None):
    size = size or lax.axis_size(axis)
    return [(axis, 1 << k) for k in range(size.bit_length() - 1)]


def peer_index(axis, bit):
    own = lax.axis_index(axis)
    side = (own // bit) % 2
    return side, own + bit * (1 - 2 * side)


def greet(peers):
    barrier = pltpu.get_barrier_semaphore()
    for axis, index in peers:
        pl.semaphore_signal(
            barrier, inc=1, device_id={axis: index}, device_id_type=pl.DeviceIdType.MESH
        )
    pl.semaphore_wait(barrier, len(peers))


def ring_peers(count):
    own = lax.axis_index("expert")
    return [lax.rem(own + step, count) for step in range(1, count)]


def remote(source, target, send_sem, recv_sem, axis, index):
    return pltpu.make_async_remote_copy(
        src_ref=source,
        dst_ref=target,
        send_sem=send_sem,
        recv_sem=recv_sem,
        device_id={axis: index},
        device_id_type=pl.DeviceIdType.MESH,
    )


def rows_of(offset, size):
    return pl.ds(pl.multiple_of(offset, 16), size)


def plan_orders(dp_count, expert_count, rows, width):
    dp_bits, expert_bits = bits_of("dp", dp_count), bits_of("expert", expert_count)
    across, along = dp_bits[1:], expert_bits
    y_bits = along[: max(1, len(along) // 2)]
    z_bits = along[len(y_bits) :]
    if expert_count == 8:
        y_bits, z_bits = along[:1], along[1:]
    orders = (across + y_bits + z_bits, y_bits + across + z_bits)
    steps = len(orders[0])
    short = tuple(order[: steps - len(z_bits)] for order in orders)
    chunks = max(1, rows // (4 * 16 << steps))
    return dp_bits[0], orders, chunks, short, [bit for _, bit in z_bits]


def finish_kernel(
    first, orders, chunks, count, dense_ref, norm_ref, packed_ref, sum_ref, norm_out, bias_out, arrived_ref,
    work, done, *scratch
):
    steps = len(orders[0])
    core_slots = scratch[0]
    part_slots = scratch[1 : 1 + steps]
    norm_work, norm_slots = scratch[1 + steps : 3 + steps]
    core_send, core_recv, part_send, part_recv, norm_send, norm_recv = scratch[3 + steps : 9 + steps]
    swap_send, swap_recv, local_sem = scratch[9 + steps :]
    rows = work.shape[0] // chunks
    half, quarter = rows // 2, rows // 4
    own = lax.axis_index("expert")
    others = ring_peers(count)
    links = [first] + list(orders[0])
    dp_peers = [(axis, peer_index(axis, bit)[1]) for axis, bit in links if axis == "dp"]
    greet([("expert", index) for index in others] + dp_peers)

    swaps = []
    import os
    for step, index in enumerate(others):
        copy = remote(packed_ref.at[index], arrived_ref.at[own], swap_send.at[step], swap_recv.at[step], "expert", index)
        copy.start()
        swaps.append(copy)
    home = pltpu.make_async_copy(packed_ref.at[own], arrived_ref.at[own], local_sem.at[chunks])
    home.start()

    side0, peer0 = peer_index(*first)
    started = []
    norm_work[...] = norm_ref[...]

    def add_rows(offset, size, slot, target):
        block = min(size, 64)

        @pl.loop(0, size // block)
        def _(index):
            here = rows_of(offset + index * block, block)
            there = rows_of(index * block, block)
            target[here, :] = (work[here, :].astype(f32) + slot[there, :].astype(f32)).astype(bf16)

    state = {}

    def event(chunk, number):
        base = chunk * rows
        if number == 0:
            kept = base + side0 * half
            given = base + (1 - side0) * half
            load = pltpu.make_async_copy(dense_ref.at[rows_of(kept, half)], work.at[rows_of(kept, half)], local_sem.at[chunk])
            load.start()
            copy = remote(dense_ref.at[rows_of(given, half)], core_slots.at[chunk], core_send.at[chunk, 0], core_recv.at[chunk, 0], first[0], peer0)
            copy.start()
            started.append(copy)
            state[chunk] = dict(kept=kept, load=load, copy=copy)
        elif number <= 2 * steps + 1:
            for part in range(2):
                go_on(chunk, part, number - 1)
        if number == 2 * steps + 1:
            kept = state[chunk]["kept"]
            copy = remote(done.at[rows_of(kept, half)], done.at[rows_of(kept, half)], core_send.at[chunk, 1], core_recv.at[chunk, 1], first[0], peer0)
            copy.start()
            started.append(copy)
            state[chunk]["copy"] = copy
        if number == 2 * steps + 2:
            state[chunk]["copy"].wait_recv()
            store = pltpu.make_async_copy(done.at[pl.ds(base, rows)], sum_ref.at[pl.ds(base, rows)], local_sem.at[chunk])
            store.start()
            state[chunk]["store"] = store

    def go_on(chunk, part, step):
        here = state[chunk]
        if step == 0:
            if part == 0:
                here["load"].wait()
                here["copy"].wait_recv()
                add_rows(here["kept"], half, core_slots.at[chunk], work)
            offset = here["kept"] + part * quarter
        else:
            offset, size, copy, slot = here[part]
            copy.wait_recv()
            if step <= steps:
                add_rows(offset, size, slot, work if step < steps else done)
        if step < steps:
            axis, bit = orders[part][step]
            side, peer = peer_index(axis, bit)
            size = quarter >> (step + 1)
            slot = part_slots[step].at[chunk, part]
            given = offset + (1 - side) * size
            kept = offset + side * size
            copy = remote(work.at[rows_of(given, size)], slot, part_send.at[chunk, part, step], part_recv.at[chunk, part, step], axis, peer)
            copy.start()
            started.append(copy)
            here[part] = (kept, size, copy, slot)
        elif step < 2 * steps:
            back = 2 * steps - 1 - step
            axis, bit = orders[part][back]
            side, peer = peer_index(axis, bit)
            size = quarter >> (back + 1)
            if step > steps:
                offset = offset - here["side", part] * (size // 2)
            here["side", part] = side
            copy = remote(done.at[rows_of(offset, size)], done.at[rows_of(offset, size)], part_send.at[chunk, part, step], part_recv.at[chunk, part, step], axis, peer)
            copy.start()
            started.append(copy)
            here[part] = (offset, size, copy, None)

    norm_copy = None
    for tick in range(2 * steps + 2 + chunks):
        for chunk in range(chunks):
            number = tick - chunk
            if 0 <= number <= 2 * steps + 2:
                event(chunk, number)
        if tick <= len(links):
            if norm_copy is not None:
                norm_copy.wait()
                norm_work[...] += norm_slots[tick - 1]
                if tick == sum(axis == "dp" for axis, _ in links):
                    bias_out[...] = norm_work[8:16, :]
            if tick < len(links):
                axis, bit = links[tick]
                norm_copy = remote(norm_work, norm_slots.at[tick], norm_send.at[tick], norm_recv.at[tick], axis, peer_index(axis, bit)[1])
                norm_copy.start()
            else:
                norm_out[...] = norm_work[...]
    for copy in started:
        copy.wait_send()
    for copy in swaps:
        copy.wait()
    home.wait()
    for chunk in range(chunks):
        state[chunk]["store"].wait()


def finish(dense, norms, packed, dp_count):
    count = packed.shape[0]
    rows, width = dense.shape
    first, orders, chunks, _, _ = plan_orders(dp_count, count, rows, width)
    steps = len(orders[0])
    part = rows // chunks // 4
    return pl.pallas_call(
        functools.partial(finish_kernel, first, orders, chunks, count),
        in_specs=[
            pl.BlockSpec(memory_space=pl.ANY),
            pl.BlockSpec(memory_space=pltpu.VMEM),
            pl.BlockSpec(memory_space=pl.ANY),
        ],
        out_specs=[
            pl.BlockSpec(memory_space=pl.ANY),
            pl.BlockSpec(memory_space=pltpu.VMEM),
            pl.BlockSpec(memory_space=pltpu.VMEM),
            pl.BlockSpec(memory_space=pl.ANY),
        ],
        out_shape=[
            jax.ShapeDtypeStruct(dense.shape, bf16),
            jax.ShapeDtypeStruct(norms.shape, f32),
            jax.ShapeDtypeStruct((8, width), f32),
            jax.ShapeDtypeStruct(packed.shape, bf16),
        ],
        scratch_shapes=[pltpu.VMEM(dense.shape, bf16)] * 2 + [pltpu.VMEM((chunks, 2 * part, width), bf16)]
        + [pltpu.VMEM((chunks, 2, part >> (step + 1), width), bf16) for step in range(steps)]
        + [
            pltpu.VMEM(norms.shape, f32),
            pltpu.VMEM((steps + 1,) + norms.shape, f32),
            pltpu.SemaphoreType.DMA((chunks, 2)),
            pltpu.SemaphoreType.DMA((chunks, 2)),
            pltpu.SemaphoreType.DMA((chunks, 2, 2 * steps)),
            pltpu.SemaphoreType.DMA((chunks, 2, 2 * steps)),
            pltpu.SemaphoreType.DMA((steps + 1,)),
            pltpu.SemaphoreType.DMA((steps + 1,)),
            pltpu.SemaphoreType.DMA((count - 1,)),
            pltpu.SemaphoreType.DMA((count - 1,)),
            pltpu.SemaphoreType.DMA((chunks + 1,)),
        ],
        compiler_params=pltpu.CompilerParams(
            collective_id=7, has_side_effects=True, vmem_limit_bytes=BIG_VMEM
        ),
        cost_estimate=pl.CostEstimate(
            flops=2 * rows * width, bytes_accessed=8 * rows * width, transcendentals=0
        ),
    )(dense, norms, packed)


def pick(columns, numbers, table):
    return dot((columns == numbers).astype(bf16), table)


def joined_rows(columns, kept, arrived):
    places = lax.broadcasted_iota(jnp.int32, (1, arrived.shape[0]), 1)
    return pick(columns[:, 1:2], places, arrived[...]) + kept[...].astype(f32)


def near_numbers_of(rows):
    return jnp.where(rows < 0, -2, rows)


def near_kernel(columns, numbers, table, rows_ref):
    chosen = near_numbers_of(numbers[0:1, :])
    rows_ref[...] = pick(columns[:, 0:1], chosen, table[...]).astype(bf16)


def norm_parts(rows):
    centre = jnp.mean(rows, axis=-1, keepdims=True)
    centred = rows - centre
    inverse = lax.rsqrt(jnp.mean(centred * centred, axis=-1, keepdims=True) + epsilon)
    return centred * inverse, inverse


def norm_back(grad, scaled, inverse, gains):
    grad_scaled = grad * gains
    first = jnp.mean(grad_scaled, axis=-1, keepdims=True)
    second = jnp.mean(grad_scaled * scaled, axis=-1, keepdims=True)
    return inverse * (grad_scaled - first - scaled * second)


def third_kernel(far, kept, arrived, weight, rows_ref, product_ref):
    rows = joined_rows(far, kept, arrived).astype(bf16)
    rows_ref[...] = rows
    product_ref[...] = dot_last(rows, weight[...]).astype(bf16)


def last_kernel(far, kept, arrived, *rest):
    rows_ref = rest[len(rest) // 2]
    rows_ref[...] = joined_rows(far, kept, arrived).astype(bf16)
    for source, target in zip(rest[: len(rest) // 2], rest[len(rest) // 2 + 1 :]):
        target[...] = source[...].astype(f32)


def again_kernel(columns, kept, arrived, rows_ref):
    places = lax.broadcasted_iota(jnp.int32, (1, arrived.shape[0]), 1)
    rows = pick(columns[...], places, arrived[...]) + kept[...].astype(f32)
    rows_ref[...] = rows.astype(bf16)


def first_again_kernel(columns, kept, arrived, gain, bias, weight, rows_ref, normed_ref, mixed_ref, turned_ref):
    again_kernel(columns, kept, arrived, rows_ref)
    normed = (norm_parts(rows_ref[...].astype(f32))[0] * gain[...] + bias[...]).astype(bf16)
    normed_ref[...] = normed
    mixed_ref[...] = dot(normed, weight[...]).astype(bf16)
    turned_ref[...] = normed.T


def later_rows(step, table, source, target, chunk, expert_count):
    step, source, target = lax.optimization_barrier((step, source, target))
    source, target = (tuple(rows[part] for part in (0, 2, 3)) for rows in (source, target))
    packed = pack(table, source, chunk, expert_count, step)
    return remote_column(target, chunk, step)[:, None], exchange(packed, expert_count)


def more_rounds(kept, table, source, target, chunk, expert_count, rounds):
    def again(state):
        step, sums = state
        columns, arrived = later_rows(step, table, source, target, chunk, expert_count)
        (sums,) = join(again_kernel, [columns, sums], [arrived], (table.shape[1],))
        return (step + 1, sums)

    return lax.while_loop(lambda state: state[0] < rounds, again, (jnp.int32(1), kept))[1]


def more_first_rounds(kept, table, source, target, chunk, expert_count, rounds, gain, bias, weight):
    width = table.shape[1]

    def again(state):
        step, rows, *_ = state
        columns, arrived = later_rows(step, table, source, target, chunk, expert_count)
        rows, normed, mixed, turned = join(
            first_again_kernel, [columns, rows], [arrived, gain, bias, weight],
            (width, width, 3 * width), (width,),
        )
        return (step + 1, rows, normed, turned, mixed)

    return lax.while_loop(lambda state: state[0] < rounds, again, (jnp.int32(1), *kept))[1:]


def finish_rows(far, kept, arrived, sums):
    steps = 8

    def blocks(array):
        return pl.BlockSpec((array.shape[0] // steps, array.shape[1]), lambda step: (step, 0))

    count, width = kept.shape
    return pl.pallas_call(
        last_kernel,
        grid=(steps,),
        in_specs=[blocks(far), blocks(kept), in_full(arrived)] + [blocks(array) for array in sums],
        out_specs=[blocks(kept)] + [blocks(array) for array in sums],
        out_shape=[jax.ShapeDtypeStruct(kept.shape, bf16)]
        + [jax.ShapeDtypeStruct(array.shape, f32) for array in sums],
        compiler_params=pltpu.CompilerParams(vmem_limit_bytes=FULL_VMEM),
        cost_estimate=pl.CostEstimate(
            flops=2 * count * width * arrived.shape[0],
            bytes_accessed=4 * count * width + 6 * sum(array.size for array in sums),
            transcendentals=0,
        ),
    )(far, kept, arrived, *sums)


def block_rows(width):
    return pl.BlockSpec((256, width), lambda step: (step, 0))


def in_full(array):
    return pl.BlockSpec(array.shape, lambda step: (0,) * array.ndim, pipeline_mode=pl.Buffered(1))


def join(kernel, blocked, whole, widths, turned=()):
    count = blocked[0].shape[0]
    table = next(array for array in whole if array.dtype == bf16)
    inside, width = table.shape
    return pl.pallas_call(
        kernel,
        grid=(count // 256,),
        in_specs=[block_rows(array.shape[1]) for array in blocked]
        + [in_full(array) for array in whole],
        out_specs=[block_rows(size) for size in widths]
        + [pl.BlockSpec((size, 256), lambda step: (0, step)) for size in turned],
        out_shape=[jax.ShapeDtypeStruct((count, size), bf16) for size in widths]
        + [jax.ShapeDtypeStruct((size, count), bf16) for size in turned],
        compiler_params=pltpu.CompilerParams(vmem_limit_bytes=FULL_VMEM if len(widths) > 1 else BIG_VMEM),
        cost_estimate=pl.CostEstimate(
            flops=2 * count * width * (inside + sum(widths) - width),
            bytes_accessed=2 * (inside * width + count * sum(widths)),
            transcendentals=0,
        ),
    )(*blocked, *whole)


def expert_kernel(
    columns, kept, grad_y, grad_act, arrived, gain, bias, bias_in, bias_out, weight_in_hbm, weight_out_hbm,
    out_ref, normed_ref, act_ref, grad_pre_ref, grad_ref, sum_ref, weight_in, weight_out, load_sem,
):
    hidden, width = weight_in.shape
    block = width
    loads = []
    for index, low in enumerate(range(0, hidden, block)):
        part = pl.ds(low, block)
        loads.append(
            [
                pltpu.make_async_copy(source.at[part], target.at[part], load_sem.at[index, side])
                for side, (source, target) in enumerate(
                    ((weight_in_hbm, weight_in), (weight_out_hbm, weight_out))
                )
            ]
        )

    def work(first):
        if first:
            for pair in loads:
                for copy in pair:
                    copy.start()
            sum_ref[...] = jnp.zeros_like(sum_ref)
        rows = joined_rows(columns, kept, arrived)
        scaled, inverse = norm_parts(rows)
        normed = (scaled * gain[...] + bias[...]).astype(bf16)
        normed_ref[...] = normed
        result = jnp.zeros(rows.shape, f32)
        grad = jnp.zeros(rows.shape, f32)
        for number, low in enumerate(range(0, hidden, block)):
            if first:
                for copy in loads[number]:
                    copy.wait()
            part = slice(low, low + block)
            pre = dot_last(normed, weight_in[part, :]) + bias_in[:, part]
            square = pre * pre
            tangent = jnp.tanh(gelu_c * (pre + 0.044715 * pre * square))
            half = 0.5 * pre
            act = (half + half * tangent).astype(bf16)
            slope = (0.5 + 0.5 * tangent) + half * (1.0 - tangent * tangent) * (
                gelu_c + (3.0 * 0.044715 * gelu_c) * square
            )
            grad_pre = (grad_act[:, part].astype(f32) * slope).astype(bf16)
            act_ref[:, part] = act
            grad_pre_ref[:, part] = grad_pre
            index = 8 + number
            sum_ref[index : index + 1, :] += jnp.sum(grad_pre.astype(f32), axis=0, keepdims=True)
            result += dot(act, weight_out[part, :])
            grad += dot(grad_pre, weight_in[part, :])
        out = rows + result + bias_out[...]
        out_ref[...] = jnp.where(columns[:, 4:5] > 0, out, 0.0).astype(bf16)
        grad_in = grad_y[...].astype(f32)
        grad_ref[...] = (grad_in + norm_back(grad, scaled, inverse, gain[...])).astype(bf16)
        sum_ref[2:3, :] += jnp.sum(grad * scaled, axis=0, keepdims=True)
        sum_ref[3:4, :] += jnp.sum(grad, axis=0, keepdims=True)
        sum_ref[12:13, :] += jnp.sum(grad_in, axis=0, keepdims=True)

    @pl.when(pl.program_id(0) == 0)
    def _():
        work(True)

    @pl.when(pl.program_id(0) > 0)
    def _():
        work(False)


def run_expert(blocked, whole, weights):
    count, width = blocked[1].shape
    hidden = weights[0].shape[0]
    widths = (width, width, hidden, hidden, width)
    return pl.pallas_call(
        expert_kernel,
        grid=(count // 256,),
        in_specs=[block_rows(array.shape[1]) for array in blocked]
        + [in_full(array) for array in whole]
        + [pl.BlockSpec(memory_space=pl.ANY)] * 2,
        out_specs=[block_rows(size) for size in widths]
        + [pl.BlockSpec((16, width), lambda step: (0, 0))],
        out_shape=[jax.ShapeDtypeStruct((count, size), bf16) for size in widths]
        + [jax.ShapeDtypeStruct((16, width), f32)],
        scratch_shapes=[pltpu.VMEM((hidden, width), bf16)] * 2
        + [pltpu.SemaphoreType.DMA((hidden // width, 2))],
        compiler_params=pltpu.CompilerParams(vmem_limit_bytes=FULL_VMEM),
        cost_estimate=pl.CostEstimate(
            flops=6 * count * width * hidden,
            bytes_accessed=2 * count * (5 * width + 3 * hidden) + 4 * width * hidden,
            transcendentals=count * hidden,
        ),
    )(*blocked, *whole, *weights)


def backward_kernel(
    first, orders, along, count, pairs,
    q_ref, k_ref, v_ref, context_ref, grad_ref, logs_ref, wq_ref, wk_ref, wv_ref, dense_ref,
    normed_t, tokens_ref, hidden_ref, gain_ref, norm_ref, token_rows, slot_columns,
    mixed_sum, dense_sum, norm_out, bias_out, arrived_ref, near_ref, tokens_grad,
    work, done, core_slots, *scratch
):
    steps = len(orders[0])
    part_slots = scratch[:steps]
    (
        along_slots, pair_grad, grad_k, grad_v, total, packed, norm_work, norm_slots,
        core_send, core_recv, part_send, part_recv, along_send, along_recv,
        norm_send, norm_recv, swap_send, swap_recv, local_sem,
    ) = scratch[steps:]
    tick = pl.program_id(0)
    rows, width = work.shape[1], pairs * PAIR
    half, quarter = rows // 2, rows // 4
    own = lax.axis_index("expert")
    others = ring_peers(count)
    links = [first] + list(orders[0]) + [("expert", bit) for bit in along]
    link_peers = [(axis, peer_index(axis, bit)[1]) for axis, bit in links]
    events = 2 * steps + 4
    last = pairs + events // 2 - 1

    @pl.when(tick == 0)
    def _():
        greet([("expert", index) for index in others] + [peer for peer in link_peers if peer[0] == "dp"])

    side0, peer0 = peer_index(*first)
    offsets, sides, peers = [], [], []
    for part in range(2):
        offset = side0 * half + part * quarter
        at, side_list, peer_list = [offset], [], []
        for step, (axis, bit) in enumerate(orders[part]):
            side, peer = peer_index(axis, bit)
            offset = offset + side * (quarter >> (step + 1))
            at.append(offset)
            side_list.append(side)
            peer_list.append((axis, peer))
        offsets.append(at)
        sides.append(side_list)
        peers.append(peer_list)
    spread = 1 << len(along)
    place = (own // along[0]) % spread
    piece = quarter >> steps >> len(along)

    def core_give(chunk):
        given = rows_of((1 - side0) * half, half)
        return remote(work.at[chunk, given], core_slots.at[chunk], core_send.at[chunk, 0], core_recv.at[chunk, 0], first[0], peer0)

    def core_return(chunk):
        kept = rows_of(side0 * half, half)
        return remote(done.at[chunk, kept], done.at[chunk, kept], core_send.at[chunk, 1], core_recv.at[chunk, 1], first[0], peer0)

    def part_give(chunk, part, step):
        size = quarter >> (step + 1)
        given = rows_of(offsets[part][step] + (1 - sides[part][step]) * size, size)
        return remote(
            work.at[chunk, given], part_slots[step].at[chunk, part],
            part_send.at[chunk, part, step], part_recv.at[chunk, part, step], *peers[part][step]
        )

    def part_return(chunk, part, step):
        kept = rows_of(offsets[part][step + 1], quarter >> (step + 1))
        return remote(
            done.at[chunk, kept], done.at[chunk, kept],
            part_send.at[chunk, part, steps + step], part_recv.at[chunk, part, steps + step], *peers[part][step]
        )

    def along_copies(chunk, part, back):
        copies = []
        for turn in range(1, spread):
            there = lax.rem(place + turn, spread)
            index = turn - 1 + back * (spread - 1)
            if back:
                source = target = done.at[chunk, rows_of(offsets[part][steps] + place * piece, piece)]
            else:
                source = work.at[chunk, rows_of(offsets[part][steps] + there * piece, piece)]
                target = along_slots.at[chunk, part, turn - 1]
            copies.append(
                remote(
                    source, target, along_send.at[chunk, part, index], along_recv.at[chunk, part, index],
                    "expert", own + (there - place) * along[0]
                )
            )
        return copies

    def store(chunk):
        for part in range(4):
            source = done.at[chunk, :, part * PAIR : (part + 1) * PAIR]
            column = pl.ds(pl.multiple_of(chunk * PAIR + (part % 3) * width, PAIR), PAIR)
            target = mixed_sum if part < 3 else dense_sum
            yield pltpu.make_async_copy(source, target.at[:, column], local_sem.at[chunk, part])

    def add_rows(chunk, offset, size, slots, target):
        block = min(size, 64)

        @pl.loop(0, size // block)
        def _(index):
            here = rows_of(offset + index * block, block)
            there = rows_of(index * block, block)
            sums = work[chunk, here, :].astype(f32)
            for slot in slots:
                sums = sums + slot[there, :].astype(f32)
            target[chunk, here, :] = sums.astype(bf16)

    def event(chunk, number):
        if number == 1:
            core_give(chunk).wait_recv()
            add_rows(chunk, side0 * half, half, [core_slots.at[chunk]], work)
        for part in range(2):
            if 2 <= number <= steps + 1:
                step = number - 2
                part_give(chunk, part, step).wait_recv()
                add_rows(
                    chunk, offsets[part][step + 1], quarter >> (step + 1), [part_slots[step].at[chunk, part]], work
                )
            if number <= steps:
                part_give(chunk, part, number - 1).start()
            elif number == steps + 1:
                for copy in along_copies(chunk, part, 0):
                    copy.start()
            elif number == steps + 2:
                for copy in along_copies(chunk, part, 0):
                    copy.wait_recv()
                slots = [along_slots.at[chunk, part, turn] for turn in range(spread - 1)]
                add_rows(chunk, offsets[part][steps] + place * piece, piece, slots, done)
                for copy in along_copies(chunk, part, 1):
                    copy.start()
            elif number <= 2 * steps + 3:
                back = 2 * steps + 2 - number
                if back == steps - 1:
                    for copy in along_copies(chunk, part, 1):
                        copy.wait_recv()
                else:
                    part_return(chunk, part, back + 1).wait_recv()
                if back >= 0:
                    part_return(chunk, part, back).start()
        if number == 2 * steps + 3:
            core_return(chunk).start()
        if number == 2 * steps + 4:
            core_return(chunk).wait_recv()
            for copy in store(chunk):
                copy.start()

    def norm_step(step):
        return remote(norm_work.at[step], norm_slots.at[step], norm_send.at[step], norm_recv.at[step], *link_peers[step])

    def norm_event(step):
        norm_step(step).wait_recv()
        summed = norm_work[step] + norm_slots[step]
        if step + 1 < len(links):
            norm_work[step + 1] = summed
            norm_step(step + 1).start()
        else:
            norm_out[...] = summed
        if step + 1 == sum(axis == "dp" for axis, _ in links):
            bias_out[...] = summed[8:16]

    def run_events(side):
        for number in range(events, 0, -1):
            if (number + 1) % 2 == side:
                chunk = tick - (1 + number) // 2

                @pl.when((chunk >= 0) & (chunk < pairs))
                def _(number=number, chunk=chunk):
                    event(chunk, number)

        for step in range(len(links)):
            if step % 2 == side:

                @pl.when(tick == pairs + 1 + step // 2)
                def _(step=step):
                    norm_event(step)

    run_events(0)

    @pl.when(tick < pairs)
    def _():
        attend_back_pair(
            min(256, rows), q_ref, k_ref, v_ref, context_ref, grad_ref, logs_ref,
            pair_grad, grad_k, grad_v,
        )
        run_events(1)
        work[tick, :, : 3 * PAIR] = dot(normed_t[...], pair_grad[...]).astype(bf16)
        work[tick, :, 3 * PAIR :] = dense_ref[...]
        core_give(tick).start()
        weights = jnp.concatenate([wq_ref[...], wk_ref[...], wv_ref[...]], axis=1)

        @pl.when(tick == 0)
        def _():
            total[...] = dot_last(pair_grad[...], weights)

        @pl.when(tick > 0)
        def _():
            total[...] += dot_last(pair_grad[...], weights)

    pieces = swap_send.shape[1]
    piece_rows = packed.shape[1] // pieces

    def swap_rows(step, piece):
        index = others[step]
        here = pl.ds(piece * piece_rows, piece_rows)
        return remote(
            packed.at[index, here], arrived_ref.at[own, here],
            swap_send.at[step, piece], swap_recv.at[step, piece], "expert", index
        )

    def start_swaps(pieces):
        for piece in pieces:
            for step in range(count - 1):
                swap_rows(step, piece).start()

    def home_rows():
        return pltpu.make_async_copy(packed.at[own], arrived_ref.at[own], local_sem.at[pairs, 0])

    @pl.when(tick == pairs)
    def _():
        sums = [jnp.zeros((1, width), f32)] * 2
        for low in range(0, rows, 256):
            part = slice(low, low + 256)
            grad = total[part, :]
            scaled, inverse = norm_parts(tokens_ref[part, :].astype(f32))
            result = hidden_ref[part, :].astype(f32) + norm_back(grad, scaled, inverse, gain_ref[...])
            tokens_grad[part, :] = result.astype(bf16)
            sums[0] = sums[0] + jnp.sum(grad * scaled, axis=0, keepdims=True)
            sums[1] = sums[1] + jnp.sum(grad, axis=0, keepdims=True)
        norm_work[0] = norm_ref[...]
        norm_work[0, 0:1, :] = sums[0]
        norm_work[0, 1:2, :] = sums[1]
        norm_step(0).start()
        chunk = packed.shape[1]
        for index in range(count):
            numbers = index * chunk + lax.broadcasted_iota(jnp.int32, (chunk, 1), 0)
            packed[index] = dot((token_rows[1:2, :] == numbers).astype(bf16), tokens_grad[...]).astype(bf16)
        start_swaps([0])
        home_rows().start()

    @pl.when(tick == pairs + 2)
    def _():
        start_swaps([2])

    @pl.when(tick >= pairs)
    def _():
        run_events(1)

    @pl.when(tick == pairs + 1)
    def _():
        start_swaps([1])

    @pl.when(tick == pairs + 2)
    def _():
        start_swaps([3])

    @pl.when(tick == pairs + 2)
    def _():
        for low in range(0, near_ref.shape[0], 256):
            part = slice(low, low + 256)
            near_ref[part, :] = pick(slot_columns[part, 0:1], near_numbers_of(token_rows[0:1, :]), tokens_grad[...]).astype(bf16)

    @pl.when(tick == last)
    def _():
        @pl.loop(0, pairs)
        def _(chunk):
            core_give(chunk).wait_send()
            core_return(chunk).wait_send()
            for part in range(2):
                for step in range(steps):
                    part_give(chunk, part, step).wait_send()
                    part_return(chunk, part, step).wait_send()
                for back in range(2):
                    for copy in along_copies(chunk, part, back):
                        copy.wait_send()
            for copy in store(chunk):
                copy.wait()

        for step in range(len(links)):
            norm_step(step).wait_send()
        for piece in range(pieces):
            for step in range(count - 1):
                swap_rows(step, piece).wait()
        home_rows().wait()


def backward(mixed, context, grad_context, logs, weight, dense, normed_t, tokens, grad_hidden, gain, norms,
             token_rows, slot_columns, first, orders, along, count, chunk):
    length, width = context.shape
    pairs = width // PAIR
    steps = len(orders[0])
    links = 1 + steps + len(along)
    part = length // 4
    slots = slot_columns.shape[0]
    spread = 1 << len(along)

    def columns(offset):
        return pl.BlockSpec((length, PAIR), lambda tick: (0, offset + jnp.minimum(tick, pairs - 1)))

    def whole(array):
        return pl.BlockSpec(array.shape, lambda tick: (0,) * array.ndim, pipeline_mode=pl.Buffered(1))

    def result(shape):
        return pl.BlockSpec(shape, lambda tick: (0,) * len(shape))

    anywhere = pl.BlockSpec(memory_space=pl.ANY)
    fixed = (normed_t, tokens, grad_hidden, gain, norms, token_rows, slot_columns)
    dma = pltpu.SemaphoreType.DMA
    return pl.pallas_call(
        functools.partial(backward_kernel, first, orders, along, count, pairs),
        grid=(pairs + steps + 2,),
        in_specs=[columns(0), columns(pairs), columns(2 * pairs), columns(0), columns(0)]
        + [pl.BlockSpec((1, 8, length), lambda tick: (jnp.minimum(tick, pairs - 1), 0, 0))]
        + [columns(0), columns(pairs), columns(2 * pairs), columns(0)]
        + [whole(array) for array in fixed],
        out_specs=[
            anywhere, anywhere, result(norms.shape), result((8, width)), anywhere,
            result((slots, width)), result((length, width)),
        ],
        out_shape=[
            jax.ShapeDtypeStruct((length, 3 * width), bf16),
            jax.ShapeDtypeStruct((length, width), bf16),
            jax.ShapeDtypeStruct(norms.shape, f32),
            jax.ShapeDtypeStruct((8, width), f32),
            jax.ShapeDtypeStruct((count, chunk, width), bf16),
            jax.ShapeDtypeStruct((slots, width), bf16),
            jax.ShapeDtypeStruct((length, width), bf16),
        ],
        scratch_shapes=[pltpu.VMEM((pairs, length, 4 * PAIR), bf16)] * 2
        + [pltpu.VMEM((pairs, length // 2, 4 * PAIR), bf16)]
        + [pltpu.VMEM((pairs, 2, part >> (step + 1), 4 * PAIR), bf16) for step in range(steps)]
        + [
            pltpu.VMEM((pairs, 2, spread - 1, part >> steps >> len(along), 4 * PAIR), bf16),
            pltpu.VMEM((length, 3 * PAIR), bf16),
            pltpu.VMEM((length, PAIR), f32),
            pltpu.VMEM((length, PAIR), f32),
            pltpu.VMEM((length, width), f32),
            pltpu.VMEM((count, chunk, width), bf16),
            pltpu.VMEM((links,) + norms.shape, f32),
            pltpu.VMEM((links,) + norms.shape, f32),
            dma((pairs, 2)),
            dma((pairs, 2)),
            dma((pairs, 2, 2 * steps)),
            dma((pairs, 2, 2 * steps)),
            dma((pairs, 2, 2 * (spread - 1))),
            dma((pairs, 2, 2 * (spread - 1))),
            dma((links,)),
            dma((links,)),
            dma((count - 1, 4)),
            dma((count - 1, 4)),
            dma((pairs + 1, 4)),
        ],
        compiler_params=pltpu.CompilerParams(
            collective_id=7, has_side_effects=True, vmem_limit_bytes=61 << 20
        ),
        cost_estimate=pl.CostEstimate(
            flops=10 * length * length * width, bytes_accessed=32 * length * width,
            transcendentals=length * length * width // HEAD_DIM,
        ),
    )(mixed, mixed, mixed, context, grad_context, logs, weight, weight, weight, dense, *fixed)


def begin_kernel(
    count, chunk, dp_count, ids_ref, table_hbm, gain_ref, bias_ref, weight_hbm,
    token_columns, slot_columns, token_rows, slot_rows, info_ref, rows_out, normed_out, turned_out, mixed_out,
    ids_all, table, weight, packed, arrived, near, rows_work, normed_work, turned_work, mixed_work, most_work, most_slots,
    ids_send, ids_recv, swap_send, swap_recv, most_send, most_recv, local_sem, out_sem,
):
    own = lax.axis_index("expert")
    others = ring_peers(count)
    load = pltpu.make_async_copy(table_hbm, table, local_sem.at[0])
    load.start()
    load_weight = pltpu.make_async_copy(weight_hbm, weight, local_sem.at[1])
    load_weight.start()
    dp_own = lax.axis_index("dp")
    dp_others = [lax.rem(dp_own + step, dp_count) for step in range(1, dp_count)]
    greet([("expert", index) for index in others] + [("dp", index) for index in dp_others])
    sends = [
        remote(ids_ref, ids_all.at[own], ids_send.at[step], ids_recv.at[step], "expert", index)
        for step, index in enumerate(others)
    ]
    for copy in sends:
        copy.start()
    ids_all[own] = ids_ref[...]
    length, slots = ids_ref.shape[1], table.shape[0]
    earlier = lax.broadcasted_iota(jnp.int32, (length, length), 0) < lax.broadcasted_iota(
        jnp.int32, (length, length), 1
    )
    earlier = earlier.astype(bf16)
    for copy in sends:
        copy.wait()

    own_f = own.astype(f32)
    rows = [ids_all[index] for index in range(count)]
    ids = jnp.concatenate(rows, axis=0).astype(f32)
    lane = lax.broadcasted_iota(jnp.int32, (count, 128), 1).astype(f32)
    sequence = lax.broadcasted_iota(jnp.int32, (count, 1), 0).astype(f32)
    counts = jnp.zeros((count, 128), f32)
    for expert in range(count):
        taken = jnp.sum((ids == float(expert)).astype(f32), axis=1, keepdims=True)
        counts = jnp.where(lane == float(expert), taken, counts)
    fullest = (counts == jnp.max(counts, axis=0, keepdims=True)) & (lane < float(count))
    fullest = fullest.astype(f32)
    peaks = jnp.sum(fullest, axis=1, keepdims=True)
    single = (jnp.max(peaks, axis=0, keepdims=True) == 1.0) & (jnp.min(peaks, axis=0, keepdims=True) == 1.0)
    owner = jnp.where(single, jnp.sum(fullest * lane, axis=1, keepdims=True), sequence)
    from_each = jnp.sum(jnp.where(lane == own_f, counts, 0.0), axis=1, keepdims=True)
    as_row = jnp.sum(jnp.where(lane == sequence, from_each, 0.0), axis=0, keepdims=True)
    starts = jnp.sum(jnp.where(lane < sequence, as_row, 0.0), axis=1, keepdims=True)
    away = jnp.max(jnp.where(lane == owner, 0.0, counts), axis=1, keepdims=True)
    most = jnp.max(away, axis=0, keepdims=True)
    at_device = lane == owner
    device_starts = jnp.sum(jnp.where(at_device, starts, 0.0), axis=0, keepdims=True)
    limits = jnp.where(owner == own_f, 0.0, from_each)
    device_limits = jnp.sum(jnp.where(at_device, limits, 0.0), axis=0, keepdims=True)
    most_work[...] = jnp.broadcast_to(most, (8, 128))
    mosts = [
        remote(most_work, most_slots.at[step], most_send.at[step], most_recv.at[step], "dp", index)
        for step, index in enumerate(dp_others)
    ]
    for copy in mosts:
        copy.start()

    def places(inside, home, device, rank):
        near = jnp.where(inside & home, rank, -1.0)
        there = inside & ~home
        far = jnp.where(there & (rank < float(chunk)), device * float(chunk) + rank, -1.0)
        rank = jnp.where(there, rank, -float(chunk))
        empty = jnp.zeros((3, rank.shape[1]), f32)
        return jnp.concatenate([near, far, device, rank, inside.astype(f32), empty], axis=0)

    slot = lax.broadcasted_iota(jnp.int32, (1, slots), 1).astype(f32)
    used = jnp.zeros((1, slots), f32)
    slot_rank = jnp.zeros((1, slots), f32)
    slot_device = jnp.zeros((1, slots), f32)
    for index in range(count):
        start = starts[index : index + 1]
        inside = (slot >= start) & (slot < start + from_each[index : index + 1])
        used = jnp.where(inside, 1.0, used)
        slot_rank = jnp.where(inside, slot - start, slot_rank)
        slot_device = jnp.where(inside, owner[index : index + 1], slot_device)
    slot_places = places(used > 0.0, slot_device == own_f, slot_device, slot_rank)
    far_slots = slot_places[1:2]

    load.wait()
    swaps = []
    for step, index in enumerate(others):
        numbers = index * chunk + lax.broadcasted_iota(jnp.int32, (chunk, 1), 0)
        chosen = (far_slots == numbers.astype(f32)).astype(bf16)
        packed[step] = dot(chosen, table[...]).astype(bf16)
        copy = remote(packed.at[step], arrived.at[own], swap_send.at[step], swap_recv.at[step], "expert", index)
        copy.start()
        swaps.append(copy)
    arrived[own] = jnp.zeros(packed.shape[1:], bf16)

    held = jnp.zeros((1, length), f32)
    for index in range(count):
        held = jnp.where(owner[index : index + 1] == own_f, rows[index].astype(f32), held)
    expert = lax.broadcasted_iota(jnp.int32, (16, 1), 0).astype(f32)
    choose = (held == expert).astype(f32)
    before = dot(choose.astype(bf16), earlier)
    token_rank = jnp.sum(choose * before, axis=0, keepdims=True)
    token_places = places(held >= 0.0, held == own_f, held, token_rank)
    slot_rows[...] = slot_places.astype(jnp.int32)
    token_rows[...] = token_places.astype(jnp.int32)
    slot_turned = slot_places.T
    token_turned = token_places.T
    slot_columns[...] = slot_turned.astype(jnp.int32)
    token_columns[...] = token_turned.astype(jnp.int32)
    near_slots = jnp.where(slot_places[0:1] < 0.0, -2.0, slot_places[0:1])
    for low in range(0, length, 256):
        part = slice(low, low + 256)
        near[part, :] = pick(token_turned[part, 0:1], near_slots, table[...]).astype(bf16)
    for copy in mosts:
        copy.wait()
    overall = most_work[0:1, :]
    for step in range(dp_count - 1):
        overall = jnp.maximum(overall, most_slots[step, 0:1, :])
    blank = jnp.zeros((5, 128), f32)
    info = jnp.concatenate([overall, device_starts, device_limits, blank], axis=0)
    info_ref[...] = info.astype(jnp.int32)
    load_weight.wait()
    for copy in swaps:
        copy.wait()
    far_places = lax.broadcasted_iota(jnp.int32, (1, count * chunk), 1).astype(f32)
    stores = []
    for index, low in enumerate(range(0, length, 256)):
        part = slice(low, low + 256)
        there = (token_turned[part, 1:2] == far_places).astype(bf16)
        got = near[part, :].astype(f32)
        for source in range(count):
            got = got + dot(there[:, source * chunk : (source + 1) * chunk], arrived[source])
        normed = (norm_parts(got)[0] * gain_ref[...] + bias_ref[...]).astype(bf16)
        rows_work[part, :] = got.astype(bf16)
        normed_work[part, :] = normed
        turned_work[:, part] = normed.T
        mixed_work[part, :] = dot(normed, weight[...]).astype(bf16)
        here = pl.ds(low, 256)
        for number, (source, target) in enumerate(
            ((rows_work, rows_out), (normed_work, normed_out), (mixed_work, mixed_out))
        ):
            stores.append(pltpu.make_async_copy(source.at[here], target.at[here], out_sem.at[index, number]))
            stores[-1].start()
        stores.append(pltpu.make_async_copy(turned_work.at[:, here], turned_out.at[:, here], out_sem.at[index, 3]))
        stores[-1].start()
    for copy in stores:
        copy.wait()


def begin(ids, table, gain, bias, weight, count, chunk, dp_count):
    length = ids.shape[0]
    slots, width = table.shape
    vmem = pl.BlockSpec(memory_space=pltpu.VMEM)
    anywhere = pl.BlockSpec(memory_space=pl.ANY)
    whole = jax.ShapeDtypeStruct
    dma = pltpu.SemaphoreType.DMA
    return pl.pallas_call(
        functools.partial(begin_kernel, count, chunk, dp_count),
        in_specs=[vmem, anywhere, vmem, vmem, anywhere],
        out_specs=[vmem] * 5 + [anywhere] * 4,
        out_shape=[
            whole((length, 8), jnp.int32),
            whole((slots, 8), jnp.int32),
            whole((8, length), jnp.int32),
            whole((8, slots), jnp.int32),
            whole((8, 128), jnp.int32),
            whole((length, width), bf16),
            whole((length, width), bf16),
            whole((width, length), bf16),
            whole((length, 3 * width), bf16),
        ],
        scratch_shapes=[
            pltpu.VMEM((count, 1, length), jnp.int32),
            pltpu.VMEM((slots, width), bf16),
            pltpu.VMEM(weight.shape, bf16),
            pltpu.VMEM((count - 1, chunk, width), bf16),
            pltpu.VMEM((count, chunk, width), bf16),
            pltpu.VMEM((length, width), bf16),
            pltpu.VMEM((length, width), bf16),
            pltpu.VMEM((length, width), bf16),
            pltpu.VMEM((width, length), bf16),
            pltpu.VMEM((length, 3 * width), bf16),
            pltpu.VMEM((8, 128), f32),
            pltpu.VMEM((dp_count - 1, 8, 128), f32),
            dma((count - 1,)),
            dma((count - 1,)),
            dma((count - 1,)),
            dma((count - 1,)),
            dma((dp_count - 1,)),
            dma((dp_count - 1,)),
            dma((2,)),
            dma((length // 256, 4)),
        ],
        compiler_params=pltpu.CompilerParams(
            collective_id=5, has_side_effects=True, vmem_limit_bytes=BIG_VMEM
        ),
        cost_estimate=pl.CostEstimate(
            flops=12 * length * slots * width, bytes_accessed=8 * slots * width, transcendentals=0
        ),
    )(ids[None, :], table, gain, bias, weight)


def back_kernel(grad_ref, weight_ref, tokens_ref, hidden_ref, gain_ref, out_ref, sum_ref):
    width = gain_ref.shape[1]
    grad = sum(
        dot_last(grad_ref[part], weight_ref[:, part * width : (part + 1) * width])
        for part in range(3)
    )
    scaled, inverse = norm_parts(tokens_ref[...].astype(f32))
    result = hidden_ref[...].astype(f32) + norm_back(grad, scaled, inverse, gain_ref[...])
    out_ref[...] = result.astype(bf16)

    @pl.when(pl.program_id(0) == 0)
    def _():
        sum_ref[...] = jnp.zeros_like(sum_ref)

    sum_ref[0:1, :] += jnp.sum(grad * scaled, axis=0, keepdims=True)
    sum_ref[1:2, :] += jnp.sum(grad, axis=0, keepdims=True)


def back(grad_mixed, weight, tokens, grad_hidden, gain):
    count, width = tokens.shape
    block = 256

    def by_rows():
        return pl.BlockSpec((block, width), lambda step: (step, 0))

    return pl.pallas_call(
        back_kernel,
        grid=(count // block,),
        in_specs=[
            pl.BlockSpec((3, block, width), lambda step: (0, step, 0)),
            pl.BlockSpec(weight.shape, lambda step: (0, 0)),
            by_rows(),
            by_rows(),
            pl.BlockSpec((1, width), lambda step: (0, 0)),
        ],
        out_specs=[by_rows(), pl.BlockSpec((8, width), lambda step: (0, 0))],
        out_shape=[
            jax.ShapeDtypeStruct((count, width), bf16),
            jax.ShapeDtypeStruct((8, width), f32),
        ],
        compiler_params=pltpu.CompilerParams(vmem_limit_bytes=BIG_VMEM),
        cost_estimate=pl.CostEstimate(
            flops=6 * count * width * width, bytes_accessed=20 * count * width, transcendentals=0
        ),
    )(grad_mixed, weight, tokens, grad_hidden, gain)


def body(
    block_input,
    expert_ids,
    ln1_gain,
    ln1_bias,
    w_qkv,
    w_o,
    ln2_gain,
    ln2_bias,
    w_in,
    b_in,
    w_out,
    b_out,
    cotangent,
):
    expert_count = lax.axis_size("expert")
    model_width = block_input.shape[2]
    seq_ids = expert_ids[0]
    seq_length = seq_ids.shape[0]
    chunk = seq_length // expert_count
    dp_index = lax.axis_index("dp")
    dp_count = lax.axis_size("dp")

    def row(values):
        return values.astype(f32).reshape(1, -1)

    token_columns, slot_columns, token_rows, slot_rows, info, *first_rows = begin(
        seq_ids, block_input[0], row(ln1_gain), row(ln1_bias), w_qkv, expert_count, chunk, dp_count
    )
    rounds = (info[0, 0] + chunk - 1) // chunk
    token_places = tuple(token_rows[part] for part in (0, 2, 3))
    token_side = (token_rows, token_columns)
    slot_side = (slot_rows, slot_columns)
    device_starts, device_limits = info[1, :expert_count], info[2, :expert_count]

    def start(table):
        return exchange(pack(table, token_places, chunk, expert_count), expert_count)

    def start_slots(table):
        packed = pack_slots(table, device_starts, device_limits, chunk)
        return exchange(packed, expert_count)

    def near_rows(table, source, target):
        (rows,) = join(near_kernel, [target[1]], [source[0], table], (model_width,))
        return rows

    def sides(kept, table, source, target):
        kept = more_rounds(kept, table, source[0], target[0], chunk, expert_count, rounds)
        return [target[1], kept]

    full_in = lax.all_gather(w_in[0], "dp", axis=0, tiled=True)
    full_out = lax.all_gather(w_out[0], "dp", axis=0, tiled=True)

    tokens_in, normed_low, normed_t, mixed_qkv = more_first_rounds(
        first_rows, block_input[0], slot_rows, token_rows, chunk, expert_count, rounds,
        row(ln1_gain), row(ln1_bias), w_qkv,
    )
    context_low, log_totals = attend(mixed_qkv)
    hidden = (tokens_in.astype(f32) + dot(context_low, w_o)).astype(bf16)
    late, b_in, b_out, hidden = lax.optimization_barrier((cotangent[0], b_in, b_out, hidden))
    arrived = start(hidden)
    grad_low = jnp.where(slot_columns[:, 4:5] > 0, late, jnp.zeros((), jnp.bfloat16))
    grad_act = dot_last(grad_low, full_out).astype(bf16)
    biases = jnp.concatenate([b_in, b_out], axis=1)
    for axis, bit in bits_of("dp"):
        got = swap(biases, axis, bit)
        upper = (dp_index // bit) % 2 == 1
        biases = jnp.where(
            upper, jnp.concatenate([got, biases]), jnp.concatenate([biases, got])
        )
    hidden_part = b_in.shape[1]
    full_bias_in = row(biases[:, :hidden_part])
    full_bias_out = row(biases[:, hidden_part:])
    near = near_rows(hidden, token_side, slot_side)
    arrived, grad_act, near = lax.optimization_barrier((arrived, grad_act, near))
    result, normed_two, act_low, grad_pre, grad_placed, norms = run_expert(
        sides(near, hidden, token_side, slot_side) + [grad_low, grad_act],
        [arrived, row(ln2_gain), row(ln2_bias), full_bias_in, full_bias_out],
        [full_in, full_out],
    )
    arrived = start_slots(grad_placed)
    local_w_in = dot_first(grad_pre, normed_two).astype(bf16)
    local_w_out = dot_first(act_low, grad_low).astype(bf16)
    near = near_rows(grad_placed, slot_side, token_side)
    arrived, near, local_w_in, local_w_out = lax.optimization_barrier(
        (arrived, near, local_w_in, local_w_out)
    )
    sum_in = lax.psum_scatter(local_w_in, "dp", scatter_dimension=0, tiled=True)
    sum_out = lax.psum_scatter(local_w_out, "dp", scatter_dimension=0, tiled=True)
    grad_hidden, grad_context = join(
        third_kernel,
        sides(near, grad_placed, slot_side, token_side),
        [arrived, w_o],
        (model_width, model_width),
    )
    local_w_o = dot_first(context_low, grad_hidden).astype(bf16)
    first, orders, _, short, along = plan_orders(
        dp_count, expert_count, 4 * model_width, model_width
    )
    if (seq_length // 4) >> len(orders[0]) >= 16:
        mixed_sum, dense_sum, norms, bias_sums, arrived, near, grad_tokens = backward(
            mixed_qkv, context_low, grad_context, log_totals, w_qkv, local_w_o, normed_t,
            tokens_in, grad_hidden, row(ln1_gain), norms,
            token_rows, slot_columns,
            first, short, along, expert_count, chunk,
        )
    else:
        grad_mixed = attend_back(mixed_qkv, context_low, grad_context, log_totals)
        grad_tokens, sums_one = back(grad_mixed, w_qkv, tokens_in, grad_hidden, row(ln1_gain))
        packed = pack(grad_tokens, token_places, chunk, expert_count)
        dense = jnp.concatenate(
            [dot_first(normed_low, grad_mixed[part]).astype(bf16) for part in range(3)]
            + [local_w_o]
        )
        norms = norms.at[:2].set(sums_one[:2])
        summed, norms, bias_sums, arrived = finish(
            dense, norms, packed.reshape(expert_count, chunk, model_width), dp_count
        )
        near = near_rows(grad_tokens, token_side, slot_side)
        mixed_sum = jnp.concatenate(
            [summed[part * model_width : (part + 1) * model_width] for part in range(3)], axis=1
        )
        dense_sum = summed[3 * model_width :]
    arrived = arrived.reshape(-1, model_width)
    grad_input, grad_w_qkv, grad_w_o, grad_w_in, grad_w_out = finish_rows(
        slot_columns, near, arrived, [mixed_sum, dense_sum, sum_in, sum_out]
    )
    grad_input = more_rounds(
        grad_input, grad_tokens, token_rows, slot_rows, chunk, expert_count, rounds
    )
    grad_ln1_gain, grad_ln1_bias, grad_ln2_gain, grad_ln2_bias = norms[:4]
    full_parts = bias_sums[:4].reshape(dp_count, -1)
    grad_b_in = lax.dynamic_index_in_dim(full_parts, dp_index, 0, keepdims=False)
    grad_b_out = lax.dynamic_index_in_dim(
        bias_sums[4].reshape(dp_count, -1), dp_index, 0, keepdims=False
    )
    return (
        result[None],
        grad_input[None],
        grad_ln1_gain,
        grad_ln1_bias,
        grad_w_qkv,
        grad_w_o,
        grad_ln2_gain,
        grad_ln2_bias,
        grad_w_in[None],
        grad_b_in[None],
        grad_w_out[None],
        grad_b_out[None],
    )


def solution(mesh):
    placed = (
        P("dp", "expert", None),
        P("dp", "expert"),
        P(),
        P(),
        P(),
        P(),
        P(),
        P(),
        P("expert", "dp", None),
        P("expert", "dp"),
        P("expert", "dp", None),
        P("expert", "dp"),
        P("dp", "expert", None),
    )
    return jax.shard_map(
        body,
        mesh=mesh,
        in_specs=placed,
        out_specs=(
            P("dp", "expert", None),
            P("dp", "expert", None),
            P(),
            P(),
            P(),
            P(),
            P(),
            P(),
            P("expert", "dp", None),
            P("expert", "dp"),
            P("expert", "dp", None),
            P("expert", "dp"),
        ),
        check_vma=False,
    )
```
